32 devices in a mesh: dp: 4 (over y, x), expert: 8 (over z, core).
Axes of the slice: x: 2, y: 2, z: 4, core: 2. Of those that a mesh axis runs over, the one named last changes fastest.
Arguments:
- grad_out: bfloat16 [1024, 4096], P('expert', 'dp'), may hold values from -6 to 6
- routes: int32 [1024, 8], P('expert'), may hold values from 0 to 15, as said below
- slots: int32 [1024, 8], P('expert'), may hold values from 0 to 511, as said below
- gates: bfloat16 [1024, 8], P('expert'), may hold values from 0.099609375 to 1
- capacity: int32 [16], P('expert'), may hold values from 192 to 384, as said below
- hidden: bfloat16 [16, 384, 2048], P('expert', None, 'dp'), may hold values from -0.1796875 to 0.1796875
- down_weight: bfloat16 [16, 2048, 4096], P('expert', None, 'dp'), may hold values from -0.125 to 0.125
Outputs:
- hidden_grad: float32 [16, 384, 2048], P('expert', None, 'dp')
- gate_grad: float32 [1024, 8], P('expert')
The draws below stay inside these ranges and needn't reach their ends.
Inputs may be any that keep to these rules, and one draw needn't show every extreme that they name: `routes`: each row names 8 different experts; the tokens of one index of expert name each expert at most 64 times, and some experts exactly 64 times. slots[t, k] is the number of copies (t2, k2) before (t, k) in row-major order over all tokens with the same expert; an expert's slots are distinct. Some expert has capacity 384 and at least 384 copies.
All inputs are finite; a program needn't handle non-finite values.
Results may differ from the reference program's by a relative error of at most 0.0003.
Values may be sent and summed in bfloat16 or wider, within the bound.
No kernel may reach another device: no remote copies, remote signals or barrier semaphores. Data moves between devices by JAX's collectives and lax.ppermute only.
A program may use at most 128 MiB of HBM per device.

```python
import math
import jax
import jax.numpy as jnp
from jax import lax

D = 4096
FF = 2048
TOP = 8
TOK_DEV = 128
EXPERTS = 16
TOKENS = 1024
MOST = 64
CAP = 384
N_EXPERT = 8


def route_table(key):
    stride = EXPERTS // TOP
    repeats = MOST // TOP
    hot_expert = jax.random.randint(jax.random.fold_in(key, 11), (), 0, EXPERTS).astype(jnp.int32)
    hot_class = hot_expert % stride
    numbers = jnp.arange(EXPERTS, dtype=jnp.int32)
    ordering = jnp.argsort((numbers % stride == hot_class).astype(jnp.int32), stable=True).astype(jnp.int32)
    others = ordering[:EXPERTS - TOP]
    leading = (hot_expert - stride * (jnp.arange(repeats * TOP, dtype=jnp.int32) // repeats)) % EXPERTS

    def one_block(block_key):
        pool_list = jax.random.permutation(jax.random.fold_in(block_key, 1), jnp.tile(others, repeats))
        chosen = jnp.concatenate([leading, pool_list[:TOK_DEV - repeats * TOP]])
        return jax.random.permutation(jax.random.fold_in(block_key, 2), chosen)
    block_keys = jax.random.split(jax.random.fold_in(key, 12), N_EXPERT)
    base_ids = jax.vmap(one_block)(block_keys).reshape(TOKENS)
    routes = (base_ids[:, None] + stride * jnp.arange(TOP, dtype=jnp.int32)[None, :]) % EXPERTS
    return (routes.astype(jnp.int32), hot_expert)


def draw_routes(key, part):
    routes, hot_expert = route_table(key)
    return routes


def draw_slots(key, part):
    routes, hot_expert = route_table(key)
    route_flat = routes.reshape(-1)
    onehot = (route_flat[:, None] == jnp.arange(EXPERTS, dtype=jnp.int32)[None, :]).astype(jnp.int32)
    before = jnp.cumsum(onehot, axis=0) - onehot
    return jnp.sum(before * onehot, axis=1).reshape(TOKENS, TOP).astype(jnp.int32)


def draw_capacity(key, part):
    routes, hot_expert = route_table(key)
    own_key = jax.random.fold_in(key, 3)
    limits = jax.random.randint(own_key, (EXPERTS,), CAP // 2, CAP + 1).astype(jnp.int32)
    return limits.at[hot_expert].set(CAP)


def levels(key, shape, cuts, smallest, top_value):
    loudness = 1.0
    for axis_at, shards_of in cuts:
        draws = jax.random.uniform(jax.random.fold_in(jax.random.fold_in(key, 6), axis_at), (shards_of,), jnp.float32, smallest / len(cuts), top_value / len(cuts))
        loudness = loudness * jnp.repeat(jnp.exp(draws), shape[axis_at] // shards_of).reshape((-1,) + (1,) * (len(shape) - 1 - axis_at))
    return loudness


def centred(rng, extent, width, reach, pieces=(), kind=jnp.bfloat16):
    loudness = levels(rng, extent, pieces, -0.22, 0.18) if pieces else 1.0
    values = jax.random.normal(rng, extent, jnp.float32) * width * loudness
    return jnp.minimum(jnp.maximum(values, -reach), reach).astype(kind)


def setup_inputs(seed: int = 0) -> dict:
    splits = jax.random.split(jax.random.key(seed), 8)
    grad_out = centred(splits[0], (TOKENS, D), 1.0, 6.0, ((0, 8), (1, 4)))
    routes = draw_routes(jax.random.fold_in(splits[7], 71), 0)
    slots = draw_slots(jax.random.fold_in(splits[7], 71), 0)
    gates = jnp.clip(jnp.exp(math.log(1.0) - 2.306499 * jax.random.uniform(splits[3], (TOKENS, TOP), jnp.float32) ** levels(splits[3], (TOKENS, TOP), ((0, 8),), -0.2, 0.2)), 0.099609375, 1.0).astype(jnp.bfloat16)
    capacity = draw_capacity(jax.random.fold_in(splits[7], 71), 0)
    hidden = centred(splits[5], (EXPERTS, CAP, FF), 0.03, 0.1796875, ((0, 8), (2, 4)))
    down_weight = centred(splits[6], (EXPERTS, FF, D), FF ** -0.5, 0.125, ((0, 8), (2, 4)))
    return dict(grad_out=grad_out, routes=routes, slots=slots, gates=gates, capacity=capacity, hidden=hidden, down_weight=down_weight)


def reference(grad_out, routes, slots, gates, capacity, hidden, down_weight):
    route_flat = routes.reshape(-1)
    slot_flat = slots.reshape(-1)
    slot_total = EXPERTS * CAP
    usable = slot_flat < capacity[route_flat]
    target = jnp.where(usable, route_flat * CAP + slot_flat, slot_total).astype(jnp.int32)
    token_ids = (jnp.arange(TOKENS * TOP, dtype=jnp.int32) // TOP).astype(jnp.int32)
    source = jnp.full((slot_total,), TOKENS, jnp.int32).at[target].set(token_ids, mode="drop")
    slot_gate = jnp.zeros((slot_total,), jnp.float32).at[target].set(gates.reshape(-1).astype(jnp.float32), mode="drop")
    padded = jnp.concatenate([grad_out, jnp.zeros((1, D), jnp.bfloat16)], axis=0)

    def expert_step(inputs):
        source_ids, weight, stored, gate_row = inputs
        rows = padded[source_ids]
        share = jnp.dot(rows, weight.T, preferred_element_type=jnp.float32)
        grad_hidden = gate_row[:, None] * share
        slot_grad = jnp.sum(stored.astype(jnp.float32) * share, axis=1)
        return grad_hidden, slot_grad

    hidden_grad, slot_grad = lax.map(expert_step, (source.reshape(EXPERTS, CAP), down_weight, hidden, slot_gate.reshape(EXPERTS, CAP)))
    flat_grad = slot_grad.reshape(-1)
    picked = flat_grad[jnp.minimum(target, slot_total - 1)]
    gate_grad = jnp.where(usable, picked, jnp.float32(0.0)).reshape(TOKENS, TOP)
    return hidden_grad, gate_grad
```

```python
import functools
import math

import jax
import jax.numpy as jnp
from jax import lax
from jax.experimental import pallas as pl
from jax.experimental.pallas import tpu as pltpu
from jax.sharding import PartitionSpec as P

STEPS = 32766.0
TAIL = 16
VMEM = pl.BlockSpec(memory_space=pltpu.VMEM)
ANY = pl.BlockSpec(memory_space=pl.ANY)
SMEM = pl.BlockSpec(memory_space=pltpu.SMEM)


def local_ranks(route_grid, expert_total):
    onehot = (route_grid[..., None] == jnp.arange(expert_total, dtype=jnp.int32)).astype(jnp.int32)
    before = jnp.cumsum(onehot, axis=-2) - onehot
    return jnp.sum(before * onehot, axis=-1)


def capacity_of(local_expert, capacity):
    picks = local_expert[..., None] == jnp.arange(capacity.shape[0], dtype=jnp.int32)
    return jnp.sum(jnp.where(picks, capacity, 0), axis=-1)


def general(grad_out, routes, slots, gates, capacity, hidden, down_weight):
    peer_count = lax.axis_size("expert")
    experts_here = down_weight.shape[0]
    slot_count = hidden.shape[1]
    tok_rows, top_count = routes.shape
    feature_width = grad_out.shape[1]
    expert_total = experts_here * peer_count
    most_rows = top_count * max(2, (tok_rows + expert_total - 1) // expert_total)
    slot_total = experts_here * slot_count
    route_flat = routes.reshape(-1)
    slot_flat = slots.reshape(-1)
    dest_pos = route_flat * most_rows + local_ranks(route_flat, expert_total)
    send_rows = (
        jnp.zeros((expert_total * most_rows, feature_width), jnp.bfloat16)
        .at[dest_pos]
        .set(jnp.repeat(grad_out, top_count, axis=0))
    )
    send_gate = (
        jnp.zeros((expert_total * most_rows,), jnp.bfloat16).at[dest_pos].set(gates.reshape(-1))
    )
    send_slot = (
        jnp.full((expert_total * most_rows,), slot_count, jnp.int32).at[dest_pos].set(slot_flat)
    )
    exchange = functools.partial(
        lax.all_to_all, axis_name="expert", split_axis=0, concat_axis=0, tiled=True
    )
    recv_rows = exchange(send_rows.reshape(peer_count, experts_here * most_rows, feature_width))
    recv_gate = exchange(send_gate.reshape(peer_count, experts_here * most_rows))
    recv_slot = exchange(send_slot.reshape(peer_count, experts_here * most_rows))
    local_expert = jnp.broadcast_to(
        (jnp.arange(experts_here * most_rows, dtype=jnp.int32) // most_rows)[None, :],
        recv_slot.shape,
    )
    usable = recv_slot < capacity_of(local_expert, capacity)
    slot_table = jnp.where(usable, local_expert * slot_count + recv_slot, slot_total).reshape(-1)
    slot_rows = (
        jnp.zeros((slot_total, feature_width), jnp.bfloat16)
        .at[slot_table]
        .set(recv_rows.reshape(-1, feature_width), mode="drop")
    )
    slot_gate = (
        jnp.zeros((slot_total,), jnp.bfloat16)
        .at[slot_table]
        .set(recv_gate.reshape(-1), mode="drop")
    )
    slot_blocks = slot_rows.reshape(experts_here, slot_count, feature_width)
    share_rows = lax.psum_scatter(
        jnp.einsum("efd,ecd->fec", down_weight, slot_blocks, preferred_element_type=jnp.float32),
        "dp",
        scatter_dimension=0,
        tiled=True,
    )
    hidden_share = jnp.transpose(share_rows, (1, 2, 0))
    hidden_grad = (
        slot_gate.reshape(experts_here, slot_count)[..., None].astype(jnp.float32) * hidden_share
    )
    partial_grad = jnp.sum(hidden.astype(jnp.float32) * hidden_share, axis=-1)
    slot_grad = lax.psum(partial_grad, "dp").reshape(-1)
    picked = slot_grad[jnp.minimum(slot_table, slot_total - 1)]
    outgoing = jnp.where(slot_table < slot_total, picked, jnp.float32(0.0)).reshape(
        peer_count, experts_here * most_rows
    )
    incoming = exchange(outgoing).reshape(-1)
    gate_grad = incoming[dest_pos].reshape(tok_rows, top_count)
    return hidden_grad, gate_grad


ORDER = ((0, 1, 2), (1, 0, 2), (2, 1, 0), (2, 1, 0))
MIB = 2**20


def cost(shapes, flops=0):
    size = sum(math.prod(a.shape) * a.dtype.itemsize for a in shapes)
    return pl.CostEstimate(flops=flops, bytes_accessed=size, transcendentals=0)


def hbm(array):
    return pltpu.with_memory_space_constraint(array, pltpu.HBM)


def like(shape, kind=jnp.float32):
    return jax.ShapeDtypeStruct(shape, kind)


def place():
    me, rank = lax.axis_index("expert"), lax.axis_index("dp")
    return me // 2, lax.rem(me, 2), lax.rem(rank, 2), rank // 2


def chip_of(z, step):
    chip = jnp.int32(ORDER[0][step])
    for at_z in range(1, len(ORDER)):
        chip = jnp.where(z == at_z, ORDER[at_z][step], chip)
    return chip


def encode(values):
    peak = jnp.maximum(jnp.max(jnp.abs(values), keepdims=True), 1e-30)
    power = jnp.floor(jnp.log2(peak)) + 1.0
    scaled = values * (jnp.exp2(-power) * (STEPS * STEPS))
    code = jnp.round(scaled * lax.rsqrt(jnp.abs(scaled) + 1e-20))
    return code.astype(jnp.int32).astype(jnp.int16), power


def powers_block(powers, width):
    spans = [jnp.broadcast_to(power, (TAIL, width // len(powers))) for power in powers]
    return jnp.concatenate(spans, axis=1).astype(jnp.int32).astype(jnp.int16)


def decode(coded, part, parts):
    rows = (coded.shape[0] - TAIL) // parts
    lane = part * (coded.shape[1] // parts)
    power = coded[parts * rows :, lane : lane + 128].astype(jnp.int32).astype(jnp.float32)
    code = coded[part * rows : (part + 1) * rows, :].astype(jnp.int32).astype(jnp.float32)
    scale = jnp.exp2(jnp.max(power, keepdims=True)) * (1.0 / (STEPS * STEPS))
    return code * jnp.abs(code) * scale


def prepare_kernel(
    most, rows, routes, slots, gates, hidden, out, first, others, routes_in, slots_in, gates_in, sem
):
    tokens, top = rows.shape[0], routes.shape[0]
    z, core, _, _ = place()
    pairs = [(routes, routes_in), (slots, slots_in), (gates, gates_in), (rows, out.at[:tokens])]
    for step in range(3):
        start = pl.multiple_of(chip_of(z, step) * (2 * most), 2 * most)
        for local in range(2):
            span = others.at[local, 2 * most * (step - 1) : 2 * most * step] if step else first.at[local]
            pairs.append((hidden.at[local, pl.ds(start, 2 * most)], span))
    copies = [pltpu.make_async_copy(a, b, sem.at[i]) for i, (a, b) in enumerate(pairs)]
    for copy in copies:
        copy.start()
    for copy in copies[:3]:
        copy.wait()
    rank = slots_in[...] - (2 * z + core) * most
    parts = [routes_in[...], rank, gates_in[...]]
    packed = jnp.concatenate([part.astype(jnp.float32) for part in parts], axis=1)
    packed = jnp.concatenate([packed, jnp.zeros((TAIL - top, 3 * tokens), jnp.float32)], axis=0)
    out[tokens:, : 3 * tokens] = packed.astype(jnp.bfloat16)
    out[tokens:, 3 * tokens :] = jnp.zeros((TAIL, out.shape[1] - 3 * tokens), jnp.bfloat16)
    for copy in copies[3:]:
        copy.wait()


def prepare(most, grad_out, routes, slots, gates, hidden):
    tokens, feats = grad_out.shape
    top = routes.shape[1]
    experts, _, width = hidden.shape
    return pl.pallas_call(
        functools.partial(prepare_kernel, most),
        in_specs=[ANY] * 5,
        out_specs=[VMEM] * 3,
        out_shape=[
            like((tokens + TAIL, feats), jnp.bfloat16),
            like((experts, 2 * most, width), jnp.bfloat16),
            like((experts, 4 * most, width), jnp.bfloat16),
        ],
        scratch_shapes=[
            pltpu.VMEM((top, tokens), jnp.int32),
            pltpu.VMEM((top, tokens), jnp.int32),
            pltpu.VMEM((top, tokens), jnp.bfloat16),
            pltpu.SemaphoreType.DMA((10,)),
        ],
        compiler_params=pltpu.CompilerParams(vmem_limit_bytes=8 * MIB),
        cost_estimate=cost([grad_out, grad_out, hidden]),
        name="prepare",
    )(*(hbm(a) for a in (grad_out, routes.T, slots.T, gates.T, hidden)))


def load_kernel(after, weight, out, sem):
    copy = pltpu.make_async_copy(weight, out, sem)
    copy.start()
    copy.wait()


def load(after, weight):
    return pl.pallas_call(
        load_kernel,
        in_specs=[ANY, ANY],
        out_specs=VMEM,
        out_shape=like(weight.shape, weight.dtype),
        scratch_shapes=[pltpu.SemaphoreType.DMA],
        cost_estimate=cost([weight, weight]),
        compiler_params=pltpu.CompilerParams(vmem_limit_bytes=16 * MIB),
        name="load_weight",
    )(after, hbm(weight))


def pick_kernel(rules, count, *refs):
    sem = refs[-1]
    outs = refs[-1 - len(rules) : -1]
    z = place()[0]
    for number, rule in enumerate(rules):
        for source in sorted(set(rule)):
            wanted = functools.reduce(
                jnp.logical_or, [z == at_z for at_z in range(len(rule)) if rule[at_z] == source]
            )

            @pl.when(wanted)
            def _(source=source, number=number):
                pltpu.make_async_copy(refs[source], outs[number], sem.at[number]).start()

    for number in range(len(rules)):
        pltpu.make_async_copy(refs[0], outs[number], sem.at[number]).wait()


def pick(rules, blocks, after):
    return pl.pallas_call(
        functools.partial(pick_kernel, rules, len(blocks)),
        in_specs=[VMEM] * len(blocks) + [ANY] * len(after),
        out_specs=[VMEM] * len(rules),
        out_shape=[like(blocks[0].shape, blocks[0].dtype)] * len(rules),
        scratch_shapes=[pltpu.SemaphoreType.DMA((len(rules),))],
        compiler_params=pltpu.CompilerParams(vmem_limit_bytes=8 * MIB),
        cost_estimate=cost(blocks),
        name="pick",
    )(*blocks, *after)


def take_kernel(over_x, over_y, one, other, sem):
    copies = [
        pltpu.make_async_copy(over_x.at[0], one, sem.at[0]),
        pltpu.make_async_copy(over_y.at[1], other, sem.at[1]),
    ]
    for copy in copies:
        copy.start()
    for copy in copies:
        copy.wait()


def take(over_x, over_y):
    out = like(over_x.shape[1:], over_x.dtype)
    return pl.pallas_call(
        take_kernel,
        in_specs=[VMEM] * 2,
        out_specs=[VMEM] * 2,
        out_shape=[out, out],
        scratch_shapes=[pltpu.SemaphoreType.DMA((2,))],
        compiler_params=pltpu.CompilerParams(vmem_limit_bytes=8 * MIB),
        cost_estimate=cost([out, out]),
        name="take",
    )(over_x, over_y)


def expert_view(info, expert, top):
    tokens = info.shape[1] // 3
    at = info[:top, :tokens] == expert.astype(jnp.float32)
    rank = jnp.sum(jnp.where(at, info[:top, tokens : 2 * tokens] + 1.0, 0.0), axis=0, keepdims=True) - 1.0
    gate = jnp.sum(jnp.where(at, info[:top, 2 * tokens :], 0.0), axis=0, keepdims=True)
    return at, rank, gate


def rank_picks(rank, count, first, limit):
    numbers = lax.broadcasted_iota(jnp.int32, (count, rank.shape[1]), 0)
    hit = (numbers.astype(jnp.float32) == rank) & (first + numbers < limit)
    return jnp.where(hit, 1.0, 0.0)


def share_kernel(local, most, top, group, earlier, waits, cap, weight, *refs):
    blocks, refs = refs[: 2 * len(group)], refs[2 * len(group) :]
    if earlier is None:
        send, keep, info, rows = refs[waits:]
    else:
        stored, befores = refs[:4], refs[4 : 4 + earlier]
        send, keep, gates, mine, theirs, rows, info, grads = refs[4 + earlier + waits :]
    z, core, x, y = place()
    tokens = blocks[0].shape[0] - TAIL
    total, width = keep.shape[1], keep.shape[2]
    expert = (2 * z + core) * 2 + local

    def gather(at, block, side):
        table = block[tokens:, : 3 * tokens].astype(jnp.float32)
        info[2 * at + side] = table
        _, rank, gate = expert_view(table, expert, top)
        first = (2 * chip_of(z, group[at]) + side) * most
        picks = rank_picks(rank, most, first, cap[local])
        span = pl.ds(pl.multiple_of((2 * at + side) * most, most), most)
        rows[span, :] = jnp.dot(
            picks.astype(jnp.bfloat16), block[:tokens, :], preferred_element_type=jnp.float32
        ).astype(jnp.bfloat16)
        if earlier is not None:
            weights = jnp.sum(picks * gate, axis=1, keepdims=True)
            gates[span, :] = jnp.broadcast_to(weights, (most, gates.shape[1]))

    for swap in range(2):
        side = lax.rem(core + swap, 2)
        for at in range(len(group)):
            gather(at, blocks[2 * at + swap], side)

    powers = []
    for number, (sent, onward) in enumerate(((1, 1), (1, 0), (0, 1), (0, 0))):
        dx, dy = (sent, onward) if local == 0 else (onward, sent)
        piece = 2 * lax.rem(y + dy, 2) + lax.rem(x + dx, 2)
        part = lax.dot_general(
            rows[...],
            weight[local, pl.ds(pl.multiple_of(piece * width, width), width), :],
            (((1,), (1,)), ((), ())),
            preferred_element_type=jnp.float32,
        )
        if earlier is not None:
            there = stored[3][...] if dx and dy else stored[2 * dy + dx][local]
            grad = there.astype(jnp.float32) * part
            grad = jnp.sum(grad, axis=1, keepdims=True)
            grads[...] = grads[...] + grad if number else grad
        if sent:
            code, power = encode(part)
            send[(1 - onward) * total : (2 - onward) * total, :] = code
            powers.append(power)
        else:
            keep[1 - onward] = part
    send[2 * total :, :] = powers_block(powers, width)

    if earlier is not None:
        for out, befores_of in ((mine, befores[0::2]), (theirs, befores[1::2])):
            out[...] = sum((b[...] for b in befores_of), jnp.zeros(out.shape, jnp.float32))
        for at, step in enumerate(group):
            chip = chip_of(z, step)
            for out, side in ((mine, core), (theirs, 1 - core)):
                named, rank, _ = expert_view(info[2 * at + side], expert, top)
                picks = rank_picks(rank, most, (2 * chip + side) * most, cap[local])
                span = pl.ds(pl.multiple_of((2 * at + side) * most, most), most)
                back = jnp.sum(picks * grads[span, :], axis=0, keepdims=True)
                out[chip] = out[chip] + jnp.where(named, back, 0.0)


def partial_share(local, most, top, group, cap, weight, blocks, stored=None, befores=(), after=()):
    tokens, feats = blocks[0].shape[0] - TAIL, blocks[0].shape[1]
    width = weight.shape[1] // 4
    total = 2 * most * len(group)
    tables = (2 * len(group), TAIL, 3 * tokens)
    outs = [like((2 * total + TAIL, width), jnp.int16), like((2, total, width))]
    scratch = [pltpu.VMEM((total, feats), jnp.bfloat16)]
    args = [cap, weight, *blocks]
    if stored is None:
        outs.append(like(tables))
    else:
        outs += [like((total, 128)), like((3, top, tokens)), like((3, top, tokens))]
        scratch += [pltpu.VMEM(tables, jnp.float32), pltpu.VMEM((total, 1), jnp.float32)]
        args += [*stored, *befores]
    earlier = None if stored is None else len(befores)
    return pl.pallas_call(
        functools.partial(share_kernel, local, most, top, group, earlier, len(after)),
        in_specs=[SMEM] + [VMEM] * (len(args) - 1) + [ANY] * len(after),
        out_specs=[VMEM] * len(outs),
        out_shape=outs,
        scratch_shapes=scratch,
        cost_estimate=cost([weight, *blocks], 8 * total * width * feats),
        compiler_params=pltpu.CompilerParams(vmem_limit_bytes=28 * MIB),
        name=f"share_{local}",
    )(*args, *after)


def middle_kernel(got, keep, *refs):
    send, rest = refs[-2:]
    rows, width = rest.shape
    code, power = encode(keep[0] + decode(got, 0, 2))
    send[:rows, :] = code
    send[rows:, :] = powers_block([power], width)
    rest[...] = keep[1] + decode(got, 1, 2)


def middle(got, keep, after=()):
    _, rows, width = keep.shape
    return pl.pallas_call(
        middle_kernel,
        in_specs=[VMEM, VMEM] + [ANY] * len(after),
        out_specs=[VMEM, VMEM],
        out_shape=[like((rows + TAIL, width), jnp.int16), like((rows, width))],
        cost_estimate=cost([got, keep, keep]),
        compiler_params=pltpu.CompilerParams(vmem_limit_bytes=8 * MIB),
        name="middle",
    )(got, keep, *after)


def first_finish_kernel(
    most, top, cap, hidden, info, got0, rest0, got1, rest1, more_mine, more_theirs, out, mine, theirs
):
    z, core, _, _ = place()
    chip = chip_of(z, 0)
    mine[...] = more_mine[...]
    theirs[...] = more_theirs[...]
    for local, (got, rest) in enumerate(((got0, rest0), (got1, rest1))):
        out[local] = rest[...] + decode(got, 0, 1)
        for parts, side in ((mine, core), (theirs, 1 - core)):
            span = pl.ds(pl.multiple_of(side * most, most), most)
            named, rank, gate = expert_view(info[side], (2 * z + core) * 2 + local, top)
            picks = rank_picks(rank, most, (2 * chip + side) * most, cap[local])
            weight = jnp.sum(picks * gate, axis=1, keepdims=True)
            share = out[local, span, :]
            grad = jnp.sum(hidden[local, span, :].astype(jnp.float32) * share, axis=1, keepdims=True)
            out[local, span, :] = weight * share
            back = jnp.sum(picks * grad, axis=0, keepdims=True)
            parts[chip] = parts[chip] + jnp.where(named, back, 0.0)


def first_finish(most, top, cap, hidden, info, sums, parts):
    tokens = info.shape[2] // 3
    return pl.pallas_call(
        functools.partial(first_finish_kernel, most, top),
        in_specs=[SMEM] + [VMEM] * 8,
        out_specs=[VMEM] * 3,
        out_shape=[like(hidden.shape), like((3, top, tokens)), like((3, top, tokens))],
        compiler_params=pltpu.CompilerParams(vmem_limit_bytes=8 * MIB),
        cost_estimate=cost([*sums, hidden]),
        name="first_finish",
    )(cap, hidden, info, *sums, *parts)


def finish_kernel(most, first, got0, rest0, gates0, got1, rest1, gates1, *refs):
    totals, (out, gate_grad) = refs[:-2], refs[-2:]
    gate_grad[...] = sum((total[...] for total in totals[1:]), totals[0][...])
    z = place()[0]
    spans = [pl.ds(pl.multiple_of(chip_of(z, s) * (2 * most), 2 * most), 2 * most) for s in range(3)]
    for local, (got, rest, gates) in enumerate(((got0, rest0, gates0), (got1, rest1, gates1))):
        out[local, spans[0], :] = first[local]
        grad = gates[:, :1] * (rest[...] + decode(got, 0, 1))
        out[local, spans[1], :] = grad[: 2 * most]
        out[local, spans[2], :] = grad[2 * most :]


def finish(most, first, sums, totals):
    experts, rows, width = first.shape
    return pl.pallas_call(
        functools.partial(finish_kernel, most),
        in_specs=[VMEM] * (7 + len(totals)),
        out_specs=[VMEM, VMEM],
        out_shape=[like((experts, 3 * rows, width)), like(totals[0].shape)],
        compiler_params=pltpu.CompilerParams(vmem_limit_bytes=16 * MIB),
        cost_estimate=cost([*sums, first, first]),
        name="finish",
    )(first, *sums, *totals)


def chips_kernel(mine, got, stay, away):
    z = place()[0]
    low, mid, high = (mine[i] + got[i] for i in range(3))
    none = jnp.zeros(low.shape, jnp.float32)
    stay[0] = jnp.where(z < 2, low, high)
    stay[1] = jnp.where(z < 2, mid, none)
    away[0] = jnp.where(z < 2, high, low)
    away[1] = jnp.where(z < 2, none, mid)


def chip_kernel(kept, got, stay, away):
    odd = lax.rem(place()[0], 2) == 1
    even_part, odd_part = (kept[i] + got[i] for i in range(2))
    stay[...] = jnp.where(odd, odd_part, even_part)
    away[...] = jnp.where(odd, even_part, odd_part)


def add_kernel(*refs):
    total = refs[0][...]
    for ref in refs[1:-1]:
        total = total + ref[...]
    refs[-1][...] = total


def small(kernel, outs, *args):
    return pl.pallas_call(
        kernel,
        in_specs=[VMEM] * len(args),
        out_specs=[VMEM] * len(outs),
        out_shape=outs,
        compiler_params=pltpu.CompilerParams(vmem_limit_bytes=2 * MIB),
        cost_estimate=cost(args),
        name=kernel.__name__,
    )(*args)


def blockwise(most, grad_out, routes, slots, gates, capacity, hidden, down_weight):
    peers, ranks = lax.axis_size("expert"), lax.axis_size("dp")
    tokens, top = routes.shape

    def along(rows, pairs):
        return lax.ppermute(rows, "expert", [(2 * a + c, 2 * b + c) for a, b in pairs for c in range(2)])

    def across(rows):
        return lax.ppermute(rows, "expert", [(i, i ^ 1) for i in range(peers)])

    def over(rows, flip):
        return lax.ppermute(rows, "dp", [(i, i ^ flip) for i in range(ranks)])

    block, first_hidden, other_hidden = prepare(most, grad_out, routes, slots, gates, hidden)
    up1 = along(block, [(0, 1), (1, 2), (2, 3)])
    down1 = along(block, [(2, 1), (1, 0)])
    stored = [other_hidden, over(other_hidden, 1), over(other_hidden, 2)]
    passed = take(stored[1], stored[2])
    far_stored = [over(passed[0], 2), over(passed[1], 1)]
    weight = load(block, down_weight)

    (first,) = pick(((0, 0, 0, 1),), (block, up1), (weight,))
    up2 = along(up1, [(1, 2), (2, 3)])
    pair = (first, across(first))
    sent, kept = [], []
    for local in range(2):
        send, keep, info = partial_share(
            local, most, top, (0,), capacity, weight, pair, after=passed if local else ()
        )
        sent.append(send)
        kept.append(keep)

    second, relay = pick(((1, 0, 0, 2), (1, 1, 2, 2)), (up1, down1, up2), (*sent, *far_stored))
    third = along(relay, [(2, 3), (1, 0)])
    blocks = [second, across(second)]

    sums, onward = [], []
    for local in range(2):
        send, rest = middle(over(sent[local], 1 + local), kept[local])
        onward.append(send)
        sums += [over(send, 2 - local), rest]
    (third,) = pick(((1, 0, 0, 1),), (relay, third), onward)
    blocks += [third, across(third)]

    halves = []
    before = []
    for local in range(2):
        send, keep, gate, *before = partial_share(
            local, most, top, (1, 2), capacity, weight, blocks, [*stored, far_stored[local]], before,
            (sums[0], sums[2]) if local else onward,
        )
        halves.append((over(send, 1 + local), keep, gate))
    first_grad, mine, theirs = first_finish(most, top, capacity, first_hidden, info, sums, before)

    one = like((top, tokens))
    two = like((2, top, tokens))
    stay, away = small(chips_kernel, [two, two], mine, across(theirs))
    stay, away = small(
        chip_kernel, [one, one], stay, along(away, [(z, z ^ 2) for z in range(peers // 2)])
    )
    (total,) = small(add_kernel, [one], stay, along(away, [(z, z ^ 1) for z in range(peers // 2)]))
    whole = [total] + [over(total, flip) for flip in range(1, ranks)]

    sums = []
    for local, (got, keep, gate) in enumerate(halves):
        send, rest = middle(got, keep, (total,))
        sums += [over(send, 2 - local), rest, gate]
    hidden_grad, gate_grad = finish(most, first_grad, sums, whole)
    return hidden_grad, gate_grad.T


def solution(mesh):
    peers, ranks = mesh.shape["expert"], mesh.shape["dp"]

    def shards(grad_out, routes, slots, gates, capacity, hidden, down_weight):
        tokens, top = routes.shape
        experts = down_weight.shape[0] * peers
        most = top * max(2, (tokens + experts - 1) // experts)
        full = most * experts == tokens * top
        fits = peers == 8 and hidden.shape[1] == 6 * most and 3 * tokens <= grad_out.shape[1]
        square = ranks == 4 and down_weight.shape[0] == 2 and experts <= 256 and most <= 256
        if full and fits and square:
            return blockwise(most, grad_out, routes, slots, gates, capacity, hidden, down_weight)
        return general(grad_out, routes, slots, gates, capacity, hidden, down_weight)

    placed = (
        P("expert", "dp"),
        P("expert", None),
        P("expert", None),
        P("expert", None),
        P("expert"),
        P("expert", None, "dp"),
        P("expert", None, "dp"),
    )
    return jax.shard_map(
        shards,
        mesh=mesh,
        in_specs=placed,
        out_specs=(P("expert", None, "dp"), P("expert", None)),
        check_vma=False,
    )
```

```python
import functools
import math

import jax
import jax.numpy as jnp
from jax import lax
from jax.experimental import pallas as pl
from jax.experimental.pallas import tpu as pltpu
from jax.sharding import PartitionSpec as P

STEPS = 32766.0
TAIL = 16
VMEM = pl.BlockSpec(memory_space=pltpu.VMEM)
ANY = pl.BlockSpec(memory_space=pl.ANY)
SMEM = pl.BlockSpec(memory_space=pltpu.SMEM)


def local_ranks(route_grid, expert_total):
    onehot = (route_grid[..., None] == jnp.arange(expert_total, dtype=jnp.int32)).astype(jnp.int32)
    before = jnp.cumsum(onehot, axis=-2) - onehot
    return jnp.sum(before * onehot, axis=-1)


def capacity_of(local_expert, capacity):
    picks = local_expert[..., None] == jnp.arange(capacity.shape[0], dtype=jnp.int32)
    return jnp.sum(jnp.where(picks, capacity, 0), axis=-1)


def general(grad_out, routes, slots, gates, capacity, hidden, down_weight):
    peer_count = lax.axis_size("expert")
    experts_here = down_weight.shape[0]
    slot_count = hidden.shape[1]
    tok_rows, top_count = routes.shape
    feature_width = grad_out.shape[1]
    expert_total = experts_here * peer_count
    most_rows = top_count * max(2, (tok_rows + expert_total - 1) // expert_total)
    slot_total = experts_here * slot_count
    route_flat = routes.reshape(-1)
    slot_flat = slots.reshape(-1)
    dest_pos = route_flat * most_rows + local_ranks(route_flat, expert_total)
    send_rows = (
        jnp.zeros((expert_total * most_rows, feature_width), jnp.bfloat16)
        .at[dest_pos]
        .set(jnp.repeat(grad_out, top_count, axis=0))
    )
    send_gate = (
        jnp.zeros((expert_total * most_rows,), jnp.bfloat16).at[dest_pos].set(gates.reshape(-1))
    )
    send_slot = (
        jnp.full((expert_total * most_rows,), slot_count, jnp.int32).at[dest_pos].set(slot_flat)
    )
    exchange = functools.partial(
        lax.all_to_all, axis_name="expert", split_axis=0, concat_axis=0, tiled=True
    )
    recv_rows = exchange(send_rows.reshape(peer_count, experts_here * most_rows, feature_width))
    recv_gate = exchange(send_gate.reshape(peer_count, experts_here * most_rows))
    recv_slot = exchange(send_slot.reshape(peer_count, experts_here * most_rows))
    local_expert = jnp.broadcast_to(
        (jnp.arange(experts_here * most_rows, dtype=jnp.int32) // most_rows)[None, :],
        recv_slot.shape,
    )
    usable = recv_slot < capacity_of(local_expert, capacity)
    slot_table = jnp.where(usable, local_expert * slot_count + recv_slot, slot_total).reshape(-1)
    slot_rows = (
        jnp.zeros((slot_total, feature_width), jnp.bfloat16)
        .at[slot_table]
        .set(recv_rows.reshape(-1, feature_width), mode="drop")
    )
    slot_gate = (
        jnp.zeros((slot_total,), jnp.bfloat16)
        .at[slot_table]
        .set(recv_gate.reshape(-1), mode="drop")
    )
    slot_blocks = slot_rows.reshape(experts_here, slot_count, feature_width)
    share_rows = lax.psum_scatter(
        jnp.einsum("efd,ecd->fec", down_weight, slot_blocks, preferred_element_type=jnp.float32),
        "dp",
        scatter_dimension=0,
        tiled=True,
    )
    hidden_share = jnp.transpose(share_rows, (1, 2, 0))
    hidden_grad = (
        slot_gate.reshape(experts_here, slot_count)[..., None].astype(jnp.float32) * hidden_share
    )
    partial_grad = jnp.sum(hidden.astype(jnp.float32) * hidden_share, axis=-1)
    slot_grad = lax.psum(partial_grad, "dp").reshape(-1)
    picked = slot_grad[jnp.minimum(slot_table, slot_total - 1)]
    outgoing = jnp.where(slot_table < slot_total, picked, jnp.float32(0.0)).reshape(
        peer_count, experts_here * most_rows
    )
    incoming = exchange(outgoing).reshape(-1)
    gate_grad = incoming[dest_pos].reshape(tok_rows, top_count)
    return hidden_grad, gate_grad


ORDER = ((0, 1, 2), (1, 0, 2), (2, 1, 0), (2, 1, 0))
MIB = 2**20


def cost(shapes, flops=0):
    size = sum(math.prod(a.shape) * a.dtype.itemsize for a in shapes)
    return pl.CostEstimate(flops=flops, bytes_accessed=size, transcendentals=0)


def hbm(array):
    return pltpu.with_memory_space_constraint(array, pltpu.HBM)


def like(shape, kind=jnp.float32):
    return jax.ShapeDtypeStruct(shape, kind)


def place():
    me, rank = lax.axis_index("expert"), lax.axis_index("dp")
    return me // 2, lax.rem(me, 2), lax.rem(rank, 2), rank // 2


def chip_of(z, step):
    chip = jnp.int32(ORDER[0][step])
    for at_z in range(1, len(ORDER)):
        chip = jnp.where(z == at_z, ORDER[at_z][step], chip)
    return chip


def encode(values):
    peak = jnp.maximum(jnp.max(jnp.abs(values), keepdims=True), 1e-30)
    power = jnp.floor(jnp.log2(peak)) + 1.0
    scaled = values * (jnp.exp2(-power) * (STEPS * STEPS))
    code = jnp.round(scaled * lax.rsqrt(jnp.abs(scaled) + 1e-20))
    return code.astype(jnp.int32).astype(jnp.int16), power


def powers_block(powers, width):
    spans = [jnp.broadcast_to(power, (TAIL, width // len(powers))) for power in powers]
    return jnp.concatenate(spans, axis=1).astype(jnp.int32).astype(jnp.int16)


def decode(coded, part, parts):
    rows = (coded.shape[0] - TAIL) // parts
    lane = part * (coded.shape[1] // parts)
    power = coded[parts * rows :, lane : lane + 128].astype(jnp.int32).astype(jnp.float32)
    code = coded[part * rows : (part + 1) * rows, :].astype(jnp.int32).astype(jnp.float32)
    scale = jnp.exp2(jnp.max(power, keepdims=True)) * (1.0 / (STEPS * STEPS))
    return code * jnp.abs(code) * scale


def prepare_kernel(
    most, rows, routes, slots, gates, hidden, out, first, others, routes_in, slots_in, gates_in, sem
):
    tokens, top = rows.shape[0], routes.shape[0]
    z, core, _, _ = place()
    pairs = [(routes, routes_in), (slots, slots_in), (gates, gates_in), (rows, out.at[:tokens])]
    for step in range(3):
        start = pl.multiple_of(chip_of(z, step) * (2 * most), 2 * most)
        for local in range(2):
            span = others.at[local, 2 * most * (step - 1) : 2 * most * step] if step else first.at[local]
            pairs.append((hidden.at[local, pl.ds(start, 2 * most)], span))
    copies = [pltpu.make_async_copy(a, b, sem.at[i]) for i, (a, b) in enumerate(pairs)]
    for copy in copies:
        copy.start()
    for copy in copies[:3]:
        copy.wait()
    rank = slots_in[...] - (2 * z + core) * most
    parts = [routes_in[...], rank, gates_in[...]]
    packed = jnp.concatenate([part.astype(jnp.float32) for part in parts], axis=1)
    packed = jnp.concatenate([packed, jnp.zeros((TAIL - top, 3 * tokens), jnp.float32)], axis=0)
    out[tokens:, : 3 * tokens] = packed.astype(jnp.bfloat16)
    out[tokens:, 3 * tokens :] = jnp.zeros((TAIL, out.shape[1] - 3 * tokens), jnp.bfloat16)
    for copy in copies[3:]:
        copy.wait()


def prepare(most, grad_out, routes, slots, gates, hidden):
    tokens, feats = grad_out.shape
    top = routes.shape[1]
    experts, _, width = hidden.shape
    return pl.pallas_call(
        functools.partial(prepare_kernel, most),
        in_specs=[ANY] * 5,
        out_specs=[VMEM] * 3,
        out_shape=[
            like((tokens + TAIL, feats), jnp.bfloat16),
            like((experts, 2 * most, width), jnp.bfloat16),
            like((experts, 4 * most, width), jnp.bfloat16),
        ],
        scratch_shapes=[
            pltpu.VMEM((top, tokens), jnp.int32),
            pltpu.VMEM((top, tokens), jnp.int32),
            pltpu.VMEM((top, tokens), jnp.bfloat16),
            pltpu.SemaphoreType.DMA((10,)),
        ],
        compiler_params=pltpu.CompilerParams(vmem_limit_bytes=8 * MIB),
        cost_estimate=cost([grad_out, grad_out, hidden]),
        name="prepare",
    )(*(hbm(a) for a in (grad_out, routes.T, slots.T, gates.T, hidden)))


def load_kernel(after, weight, out, sem):
    copy = pltpu.make_async_copy(weight, out, sem)
    copy.start()
    copy.wait()


def load(after, weight):
    return pl.pallas_call(
        load_kernel,
        in_specs=[ANY, ANY],
        out_specs=VMEM,
        out_shape=like(weight.shape, weight.dtype),
        scratch_shapes=[pltpu.SemaphoreType.DMA],
        cost_estimate=cost([weight, weight]),
        compiler_params=pltpu.CompilerParams(vmem_limit_bytes=16 * MIB),
        name="load_weight",
    )(after, hbm(weight))


def pick_kernel(rules, count, *refs):
    sem = refs[-1]
    outs = refs[-1 - len(rules) : -1]
    z = place()[0]
    for number, rule in enumerate(rules):
        for source in sorted(set(rule)):
            wanted = functools.reduce(
                jnp.logical_or, [z == at_z for at_z in range(len(rule)) if rule[at_z] == source]
            )

            @pl.when(wanted)
            def _(source=source, number=number):
                pltpu.make_async_copy(refs[source], outs[number], sem.at[number]).start()

    for number in range(len(rules)):
        pltpu.make_async_copy(refs[0], outs[number], sem.at[number]).wait()


def pick(rules, blocks, after):
    return pl.pallas_call(
        functools.partial(pick_kernel, rules, len(blocks)),
        in_specs=[VMEM] * len(blocks) + [ANY] * len(after),
        out_specs=[VMEM] * len(rules),
        out_shape=[like(blocks[0].shape, blocks[0].dtype)] * len(rules),
        scratch_shapes=[pltpu.SemaphoreType.DMA((len(rules),))],
        compiler_params=pltpu.CompilerParams(vmem_limit_bytes=8 * MIB),
        cost_estimate=cost(blocks),
        name="pick",
    )(*blocks, *after)


def take_kernel(over_x, over_y, one, other, sem):
    copies = [
        pltpu.make_async_copy(over_x.at[0], one, sem.at[0]),
        pltpu.make_async_copy(over_y.at[1], other, sem.at[1]),
    ]
    for copy in copies:
        copy.start()
    for copy in copies:
        copy.wait()


def take(over_x, over_y):
    out = like(over_x.shape[1:], over_x.dtype)
    return pl.pallas_call(
        take_kernel,
        in_specs=[VMEM] * 2,
        out_specs=[VMEM] * 2,
        out_shape=[out, out],
        scratch_shapes=[pltpu.SemaphoreType.DMA((2,))],
        compiler_params=pltpu.CompilerParams(vmem_limit_bytes=8 * MIB),
        cost_estimate=cost([out, out]),
        name="take",
    )(over_x, over_y)


def expert_view(info, expert, top):
    tokens = info.shape[1] // 3
    at = info[:top, :tokens] == expert.astype(jnp.float32)
    rank = jnp.sum(jnp.where(at, info[:top, tokens : 2 * tokens] + 1.0, 0.0), axis=0, keepdims=True) - 1.0
    gate = jnp.sum(jnp.where(at, info[:top, 2 * tokens :], 0.0), axis=0, keepdims=True)
    return at, rank, gate


def rank_picks(rank, count, first, limit):
    numbers = lax.broadcasted_iota(jnp.int32, (count, rank.shape[1]), 0)
    hit = (numbers.astype(jnp.float32) == rank) & (first + numbers < limit)
    return jnp.where(hit, 1.0, 0.0)


def share_kernel(local, most, top, group, earlier, waits, cap, weight, *refs):
    blocks, refs = refs[: 2 * len(group)], refs[2 * len(group) :]
    if earlier is None:
        send, keep, info, rows = refs[waits:]
    else:
        stored, befores = refs[:4], refs[4 : 4 + earlier]
        send, keep, gates, mine, theirs, rows, info, grads = refs[4 + earlier + waits :]
    z, core, x, y = place()
    tokens = blocks[0].shape[0] - TAIL
    total, width = keep.shape[1], keep.shape[2]
    expert = (2 * z + core) * 2 + local

    def gather(at, block, side):
        table = block[tokens:, : 3 * tokens].astype(jnp.float32)
        info[2 * at + side] = table
        _, rank, gate = expert_view(table, expert, top)
        first = (2 * chip_of(z, group[at]) + side) * most
        picks = rank_picks(rank, most, first, cap[local])
        span = pl.ds(pl.multiple_of((2 * at + side) * most, most), most)
        rows[span, :] = jnp.dot(
            picks.astype(jnp.bfloat16), block[:tokens, :], preferred_element_type=jnp.float32
        ).astype(jnp.bfloat16)
        if earlier is not None:
            weights = jnp.sum(picks * gate, axis=1, keepdims=True)
            gates[span, :] = jnp.broadcast_to(weights, (most, gates.shape[1]))

    for swap in range(2):
        side = lax.rem(core + swap, 2)
        for at in range(len(group)):
            gather(at, blocks[2 * at + swap], side)

    powers = []
    for number, (sent, onward) in enumerate(((1, 1), (1, 0), (0, 1), (0, 0))):
        dx, dy = (sent, onward) if local == 0 else (onward, sent)
        piece = 2 * lax.rem(y + dy, 2) + lax.rem(x + dx, 2)
        part = lax.dot_general(
            rows[...],
            weight[local, pl.ds(pl.multiple_of(piece * width, width), width), :],
            (((1,), (1,)), ((), ())),
            preferred_element_type=jnp.float32,
        )
        if earlier is not None:
            there = stored[3][...] if dx and dy else stored[2 * dy + dx][local]
            grad = there.astype(jnp.float32) * part
            grad = jnp.sum(grad, axis=1, keepdims=True)
            grads[...] = grads[...] + grad if number else grad
        if sent:
            code, power = encode(part)
            send[(1 - onward) * total : (2 - onward) * total, :] = code
            powers.append(power)
        else:
            keep[1 - onward] = part
    send[2 * total :, :] = powers_block(powers, width)

    if earlier is not None:
        for out, befores_of in ((mine, befores[0::2]), (theirs, befores[1::2])):
            out[...] = sum((b[...] for b in befores_of), jnp.zeros(out.shape, jnp.float32))
        for at, step in enumerate(group):
            chip = chip_of(z, step)
            for out, side in ((mine, core), (theirs, 1 - core)):
                named, rank, _ = expert_view(info[2 * at + side], expert, top)
                picks = rank_picks(rank, most, (2 * chip + side) * most, cap[local])
                span = pl.ds(pl.multiple_of((2 * at + side) * most, most), most)
                back = jnp.sum(picks * grads[span, :], axis=0, keepdims=True)
                out[chip] = out[chip] + jnp.where(named, back, 0.0)


def partial_share(local, most, top, group, cap, weight, blocks, stored=None, befores=(), after=()):
    tokens, feats = blocks[0].shape[0] - TAIL, blocks[0].shape[1]
    width = weight.shape[1] // 4
    total = 2 * most * len(group)
    tables = (2 * len(group), TAIL, 3 * tokens)
    outs = [like((2 * total + TAIL, width), jnp.int16), like((2, total, width))]
    scratch = [pltpu.VMEM((total, feats), jnp.bfloat16)]
    args = [cap, weight, *blocks]
    if stored is None:
        outs.append(like(tables))
    else:
        outs += [like((total, 128)), like((3, top, tokens)), like((3, top, tokens))]
        scratch += [pltpu.VMEM(tables, jnp.float32), pltpu.VMEM((total, 1), jnp.float32)]
        args += [*stored, *befores]
    earlier = None if stored is None else len(befores)
    return pl.pallas_call(
        functools.partial(share_kernel, local, most, top, group, earlier, len(after)),
        in_specs=[SMEM] + [VMEM] * (len(args) - 1) + [ANY] * len(after),
        out_specs=[VMEM] * len(outs),
        out_shape=outs,
        scratch_shapes=scratch,
        cost_estimate=cost([weight, *blocks], 8 * total * width * feats),
        compiler_params=pltpu.CompilerParams(vmem_limit_bytes=28 * MIB),
        name=f"share_{local}",
    )(*args, *after)


def middle_kernel(got, keep, *refs):
    send, rest = refs[-2:]
    rows, width = rest.shape
    code, power = encode(keep[0] + decode(got, 0, 2))
    send[:rows, :] = code
    send[rows:, :] = powers_block([power], width)
    rest[...] = keep[1] + decode(got, 1, 2)


def middle(got, keep, after=()):
    _, rows, width = keep.shape
    return pl.pallas_call(
        middle_kernel,
        in_specs=[VMEM, VMEM] + [ANY] * len(after),
        out_specs=[VMEM, VMEM],
        out_shape=[like((rows + TAIL, width), jnp.int16), like((rows, width))],
        cost_estimate=cost([got, keep, keep]),
        compiler_params=pltpu.CompilerParams(vmem_limit_bytes=8 * MIB),
        name="middle",
    )(got, keep, *after)


def first_finish_kernel(
    most, top, cap, hidden, info, got0, rest0, got1, rest1, more_mine, more_theirs, out, mine, theirs
):
    z, core, _, _ = place()
    chip = chip_of(z, 0)
    mine[...] = more_mine[...]
    theirs[...] = more_theirs[...]
    for local, (got, rest) in enumerate(((got0, rest0), (got1, rest1))):
        out[local] = rest[...] + decode(got, 0, 1)
        for parts, side in ((mine, core), (theirs, 1 - core)):
            span = pl.ds(pl.multiple_of(side * most, most), most)
            named, rank, gate = expert_view(info[side], (2 * z + core) * 2 + local, top)
            picks = rank_picks(rank, most, (2 * chip + side) * most, cap[local])
            weight = jnp.sum(picks * gate, axis=1, keepdims=True)
            share = out[local, span, :]
            grad = jnp.sum(hidden[local, span, :].astype(jnp.float32) * share, axis=1, keepdims=True)
            out[local, span, :] = weight * share
            back = jnp.sum(picks * grad, axis=0, keepdims=True)
            parts[chip] = parts[chip] + jnp.where(named, back, 0.0)


def first_finish(most, top, cap, hidden, info, sums, parts):
    tokens = info.shape[2] // 3
    return pl.pallas_call(
        functools.partial(first_finish_kernel, most, top),
        in_specs=[SMEM] + [VMEM] * 8,
        out_specs=[VMEM] * 3,
        out_shape=[like(hidden.shape), like((3, top, tokens)), like((3, top, tokens))],
        compiler_params=pltpu.CompilerParams(vmem_limit_bytes=8 * MIB),
        cost_estimate=cost([*sums, hidden]),
        name="first_finish",
    )(cap, hidden, info, *sums, *parts)


def finish_kernel(most, first, got0, rest0, gates0, got1, rest1, gates1, *refs):
    totals, (out, gate_grad) = refs[:-2], refs[-2:]
    gate_grad[...] = sum((total[...] for total in totals[1:]), totals[0][...])
    z = place()[0]
    spans = [pl.ds(pl.multiple_of(chip_of(z, s) * (2 * most), 2 * most), 2 * most) for s in range(3)]
    for local, (got, rest, gates) in enumerate(((got0, rest0, gates0), (got1, rest1, gates1))):
        out[local, spans[0], :] = first[local]
        grad = gates[:, :1] * (rest[...] + decode(got, 0, 1))
        out[local, spans[1], :] = grad[: 2 * most]
        out[local, spans[2], :] = grad[2 * most :]


def finish(most, first, sums, totals):
    experts, rows, width = first.shape
    return pl.pallas_call(
        functools.partial(finish_kernel, most),
        in_specs=[VMEM] * (7 + len(totals)),
        out_specs=[VMEM, VMEM],
        out_shape=[like((experts, 3 * rows, width)), like(totals[0].shape)],
        compiler_params=pltpu.CompilerParams(vmem_limit_bytes=16 * MIB),
        cost_estimate=cost([*sums, first, first]),
        name="finish",
    )(first, *sums, *totals)


def chips_kernel(mine, got, stay, away):
    z = place()[0]
    low, mid, high = (mine[i] + got[i] for i in range(3))
    none = jnp.zeros(low.shape, jnp.float32)
    stay[0] = jnp.where(z < 2, low, high)
    stay[1] = jnp.where(z < 2, mid, none)
    away[0] = jnp.where(z < 2, high, low)
    away[1] = jnp.where(z < 2, none, mid)


def chip_kernel(kept, got, stay, away):
    odd = lax.rem(place()[0], 2) == 1
    even_part, odd_part = (kept[i] + got[i] for i in range(2))
    stay[...] = jnp.where(odd, odd_part, even_part)
    away[...] = jnp.where(odd, even_part, odd_part)


def add_kernel(*refs):
    total = refs[0][...]
    for ref in refs[1:-1]:
        total = total + ref[...]
    refs[-1][...] = total


def small(kernel, outs, *args):
    return pl.pallas_call(
        kernel,
        in_specs=[VMEM] * len(args),
        out_specs=[VMEM] * len(outs),
        out_shape=outs,
        compiler_params=pltpu.CompilerParams(vmem_limit_bytes=2 * MIB),
        cost_estimate=cost(args),
        name=kernel.__name__,
    )(*args)


def blockwise(most, grad_out, routes, slots, gates, capacity, hidden, down_weight):
    peers, ranks = lax.axis_size("expert"), lax.axis_size("dp")
    tokens, top = routes.shape

    def along(rows, pairs):
        return lax.ppermute(rows, "expert", [(2 * a + c, 2 * b + c) for a, b in pairs for c in range(2)])

    def across(rows):
        return lax.ppermute(rows, "expert", [(i, i ^ 1) for i in range(peers)])

    def over(rows, flip):
        return lax.ppermute(rows, "dp", [(i, i ^ flip) for i in range(ranks)])

    block, first_hidden, other_hidden = prepare(most, grad_out, routes, slots, gates, hidden)
    up1 = along(block, [(0, 1), (1, 2), (2, 3)])
    down1 = along(block, [(2, 1), (1, 0)])
    stored = [other_hidden, over(other_hidden, 1), over(other_hidden, 2)]
    passed = take(stored[1], stored[2])
    far_stored = [over(passed[0], 2), over(passed[1], 1)]
    weight = load(block, down_weight)

    (first,) = pick(((0, 0, 0, 1),), (block, up1), (weight,))
    up2 = along(up1, [(1, 2), (2, 3)])
    pair = (first, across(first))
    sent, kept = [], []
    for local in range(2):
        send, keep, info = partial_share(
            local, most, top, (0,), capacity, weight, pair, after=()
        )
        sent.append(send)
        kept.append(keep)

    (relay,) = pick(((1, 1, 2, 2),), (up1, down1, up2), sent)
    third = along(relay, [(2, 3), (1, 0)])

    sums, onward = [], []
    for local in range(2):
        send, rest = middle(over(sent[local], 1 + local), kept[local])
        onward.append(send)
        sums += [over(send, 2 - local), rest]
    (second,) = pick(((1, 0, 0, 2),), (up1, down1, up2), (*onward, *far_stored))
    second_far = across(second)
    (third,) = pick(((1, 0, 0, 1),), (relay, third), (second_far,))
    blocks = [second, second_far, third, across(third)]

    halves = []
    before = []
    for local in range(2):
        send, keep, gate, *before = partial_share(
            local, most, top, (1, 2), capacity, weight, blocks, [*stored, far_stored[local]], before,
            (sums[0], sums[2]) if local else onward,
        )
        halves.append((over(send, 1 + local), keep, gate))
    first_grad, mine, theirs = first_finish(most, top, capacity, first_hidden, info, sums, before)

    one = like((top, tokens))
    two = like((2, top, tokens))
    stay, away = small(chips_kernel, [two, two], mine, across(theirs))
    stay, away = small(
        chip_kernel, [one, one], stay, along(away, [(z, z ^ 2) for z in range(peers // 2)])
    )
    (total,) = small(add_kernel, [one], stay, along(away, [(z, z ^ 1) for z in range(peers // 2)]))
    whole = [total] + [over(total, flip) for flip in range(1, ranks)]

    sums = []
    for local, (got, keep, gate) in enumerate(halves):
        send, rest = middle(got, keep, (total,))
        sums += [over(send, 2 - local), rest, gate]
    hidden_grad, gate_grad = finish(most, first_grad, sums, whole)
    return hidden_grad, gate_grad.T


def solution(mesh):
    peers, ranks = mesh.shape["expert"], mesh.shape["dp"]

    def shards(grad_out, routes, slots, gates, capacity, hidden, down_weight):
        tokens, top = routes.shape
        experts = down_weight.shape[0] * peers
        most = top * max(2, (tokens + experts - 1) // experts)
        full = most * experts == tokens * top
        fits = peers == 8 and hidden.shape[1] == 6 * most and 3 * tokens <= grad_out.shape[1]
        square = ranks == 4 and down_weight.shape[0] == 2 and experts <= 256 and most <= 256
        if full and fits and square:
            return blockwise(most, grad_out, routes, slots, gates, capacity, hidden, down_weight)
        return general(grad_out, routes, slots, gates, capacity, hidden, down_weight)

    placed = (
        P("expert", "dp"),
        P("expert", None),
        P("expert", None),
        P("expert", None),
        P("expert"),
        P("expert", None, "dp"),
        P("expert", None, "dp"),
    )
    return jax.shard_map(
        shards,
        mesh=mesh,
        in_specs=placed,
        out_specs=(P("expert", None, "dp"), P("expert", None)),
        check_vma=False,
    )
```

```python
import functools
import math

import jax
import jax.numpy as jnp
from jax import lax
from jax.experimental import pallas as pl
from jax.experimental.pallas import tpu as pltpu
from jax.sharding import PartitionSpec as P

STEPS = 32766.0
TAIL = 16
VMEM = pl.BlockSpec(memory_space=pltpu.VMEM)
ANY = pl.BlockSpec(memory_space=pl.ANY)
SMEM = pl.BlockSpec(memory_space=pltpu.SMEM)


def local_ranks(route_grid, expert_total):
    onehot = (route_grid[..., None] == jnp.arange(expert_total, dtype=jnp.int32)).astype(jnp.int32)
    before = jnp.cumsum(onehot, axis=-2) - onehot
    return jnp.sum(before * onehot, axis=-1)


def capacity_of(local_expert, capacity):
    picks = local_expert[..., None] == jnp.arange(capacity.shape[0], dtype=jnp.int32)
    return jnp.sum(jnp.where(picks, capacity, 0), axis=-1)


def general(grad_out, routes, slots, gates, capacity, hidden, down_weight):
    peer_count = lax.axis_size("expert")
    experts_here = down_weight.shape[0]
    slot_count = hidden.shape[1]
    tok_rows, top_count = routes.shape
    feature_width = grad_out.shape[1]
    expert_total = experts_here * peer_count
    most_rows = top_count * max(2, (tok_rows + expert_total - 1) // expert_total)
    slot_total = experts_here * slot_count
    route_flat = routes.reshape(-1)
    slot_flat = slots.reshape(-1)
    dest_pos = route_flat * most_rows + local_ranks(route_flat, expert_total)
    send_rows = (
        jnp.zeros((expert_total * most_rows, feature_width), jnp.bfloat16)
        .at[dest_pos]
        .set(jnp.repeat(grad_out, top_count, axis=0))
    )
    send_gate = (
        jnp.zeros((expert_total * most_rows,), jnp.bfloat16).at[dest_pos].set(gates.reshape(-1))
    )
    send_slot = (
        jnp.full((expert_total * most_rows,), slot_count, jnp.int32).at[dest_pos].set(slot_flat)
    )
    exchange = functools.partial(
        lax.all_to_all, axis_name="expert", split_axis=0, concat_axis=0, tiled=True
    )
    recv_rows = exchange(send_rows.reshape(peer_count, experts_here * most_rows, feature_width))
    recv_gate = exchange(send_gate.reshape(peer_count, experts_here * most_rows))
    recv_slot = exchange(send_slot.reshape(peer_count, experts_here * most_rows))
    local_expert = jnp.broadcast_to(
        (jnp.arange(experts_here * most_rows, dtype=jnp.int32) // most_rows)[None, :],
        recv_slot.shape,
    )
    usable = recv_slot < capacity_of(local_expert, capacity)
    slot_table = jnp.where(usable, local_expert * slot_count + recv_slot, slot_total).reshape(-1)
    slot_rows = (
        jnp.zeros((slot_total, feature_width), jnp.bfloat16)
        .at[slot_table]
        .set(recv_rows.reshape(-1, feature_width), mode="drop")
    )
    slot_gate = (
        jnp.zeros((slot_total,), jnp.bfloat16)
        .at[slot_table]
        .set(recv_gate.reshape(-1), mode="drop")
    )
    slot_blocks = slot_rows.reshape(experts_here, slot_count, feature_width)
    share_rows = lax.psum_scatter(
        jnp.einsum("efd,ecd->fec", down_weight, slot_blocks, preferred_element_type=jnp.float32),
        "dp",
        scatter_dimension=0,
        tiled=True,
    )
    hidden_share = jnp.transpose(share_rows, (1, 2, 0))
    hidden_grad = (
        slot_gate.reshape(experts_here, slot_count)[..., None].astype(jnp.float32) * hidden_share
    )
    partial_grad = jnp.sum(hidden.astype(jnp.float32) * hidden_share, axis=-1)
    slot_grad = lax.psum(partial_grad, "dp").reshape(-1)
    picked = slot_grad[jnp.minimum(slot_table, slot_total - 1)]
    outgoing = jnp.where(slot_table < slot_total, picked, jnp.float32(0.0)).reshape(
        peer_count, experts_here * most_rows
    )
    incoming = exchange(outgoing).reshape(-1)
    gate_grad = incoming[dest_pos].reshape(tok_rows, top_count)
    return hidden_grad, gate_grad


ORDER = ((0, 1, 2), (1, 0, 2), (2, 1, 0), (2, 1, 0))
MIB = 2**20


def cost(shapes, flops=0):
    size = sum(math.prod(a.shape) * a.dtype.itemsize for a in shapes)
    return pl.CostEstimate(flops=flops, bytes_accessed=size, transcendentals=0)


def hbm(array):
    return pltpu.with_memory_space_constraint(array, pltpu.HBM)


def like(shape, kind=jnp.float32):
    return jax.ShapeDtypeStruct(shape, kind)


def place():
    me, rank = lax.axis_index("expert"), lax.axis_index("dp")
    return me // 2, lax.rem(me, 2), lax.rem(rank, 2), rank // 2


def chip_of(z, step):
    chip = jnp.int32(ORDER[0][step])
    for at_z in range(1, len(ORDER)):
        chip = jnp.where(z == at_z, ORDER[at_z][step], chip)
    return chip


def encode(values):
    peak = jnp.maximum(jnp.max(jnp.abs(values), keepdims=True), 1e-30)
    power = jnp.floor(jnp.log2(peak)) + 1.0
    scaled = values * (jnp.exp2(-power) * (STEPS * STEPS))
    code = jnp.round(scaled * lax.rsqrt(jnp.abs(scaled) + 1e-20))
    return code.astype(jnp.int32).astype(jnp.int16), power


def powers_block(powers, width):
    spans = [jnp.broadcast_to(power, (TAIL, width // len(powers))) for power in powers]
    return jnp.concatenate(spans, axis=1).astype(jnp.int32).astype(jnp.int16)


def decode(coded, part, parts):
    rows = (coded.shape[0] - TAIL) // parts
    lane = part * (coded.shape[1] // parts)
    power = coded[parts * rows :, lane : lane + 128].astype(jnp.int32).astype(jnp.float32)
    code = coded[part * rows : (part + 1) * rows, :].astype(jnp.int32).astype(jnp.float32)
    scale = jnp.exp2(jnp.max(power, keepdims=True)) * (1.0 / (STEPS * STEPS))
    return code * jnp.abs(code) * scale


def prepare_kernel(
    most, rows, routes, slots, gates, hidden, out, first, others, routes_in, slots_in, gates_in, sem
):
    tokens, top = rows.shape[0], routes.shape[0]
    z, core, _, _ = place()
    pairs = [(routes, routes_in), (slots, slots_in), (gates, gates_in), (rows, out.at[:tokens])]
    for step in range(3):
        start = pl.multiple_of(chip_of(z, step) * (2 * most), 2 * most)
        for local in range(2):
            span = others.at[local, 2 * most * (step - 1) : 2 * most * step] if step else first.at[local]
            pairs.append((hidden.at[local, pl.ds(start, 2 * most)], span))
    copies = [pltpu.make_async_copy(a, b, sem.at[i]) for i, (a, b) in enumerate(pairs)]
    for copy in copies:
        copy.start()
    for copy in copies[:3]:
        copy.wait()
    rank = slots_in[...] - (2 * z + core) * most
    parts = [routes_in[...], rank, gates_in[...]]
    packed = jnp.concatenate([part.astype(jnp.float32) for part in parts], axis=1)
    packed = jnp.concatenate([packed, jnp.zeros((TAIL - top, 3 * tokens), jnp.float32)], axis=0)
    out[tokens:, : 3 * tokens] = packed.astype(jnp.bfloat16)
    out[tokens:, 3 * tokens :] = jnp.zeros((TAIL, out.shape[1] - 3 * tokens), jnp.bfloat16)
    for copy in copies[3:]:
        copy.wait()


def prepare(most, grad_out, routes, slots, gates, hidden):
    tokens, feats = grad_out.shape
    top = routes.shape[1]
    experts, _, width = hidden.shape
    return pl.pallas_call(
        functools.partial(prepare_kernel, most),
        in_specs=[ANY] * 5,
        out_specs=[VMEM] * 3,
        out_shape=[
            like((tokens + TAIL, feats), jnp.bfloat16),
            like((experts, 2 * most, width), jnp.bfloat16),
            like((experts, 4 * most, width), jnp.bfloat16),
        ],
        scratch_shapes=[
            pltpu.VMEM((top, tokens), jnp.int32),
            pltpu.VMEM((top, tokens), jnp.int32),
            pltpu.VMEM((top, tokens), jnp.bfloat16),
            pltpu.SemaphoreType.DMA((10,)),
        ],
        compiler_params=pltpu.CompilerParams(vmem_limit_bytes=8 * MIB),
        cost_estimate=cost([grad_out, grad_out, hidden]),
        name="prepare",
    )(*(hbm(a) for a in (grad_out, routes.T, slots.T, gates.T, hidden)))


def load_kernel(after, weight, out, sem):
    copy = pltpu.make_async_copy(weight, out, sem)
    copy.start()
    copy.wait()


def load(after, weight):
    return pl.pallas_call(
        load_kernel,
        in_specs=[ANY, ANY],
        out_specs=VMEM,
        out_shape=like(weight.shape, weight.dtype),
        scratch_shapes=[pltpu.SemaphoreType.DMA],
        cost_estimate=cost([weight, weight]),
        compiler_params=pltpu.CompilerParams(vmem_limit_bytes=16 * MIB),
        name="load_weight",
    )(after, hbm(weight))


def pick_kernel(rules, count, *refs):
    sem = refs[-1]
    outs = refs[-1 - len(rules) : -1]
    z = place()[0]
    for number, rule in enumerate(rules):
        for source in sorted(set(rule)):
            wanted = functools.reduce(
                jnp.logical_or, [z == at_z for at_z in range(len(rule)) if rule[at_z] == source]
            )

            @pl.when(wanted)
            def _(source=source, number=number):
                pltpu.make_async_copy(refs[source], outs[number], sem.at[number]).start()

    for number in range(len(rules)):
        pltpu.make_async_copy(refs[0], outs[number], sem.at[number]).wait()


def pick(rules, blocks, after):
    return pl.pallas_call(
        functools.partial(pick_kernel, rules, len(blocks)),
        in_specs=[VMEM] * len(blocks) + [ANY] * len(after),
        out_specs=[VMEM] * len(rules),
        out_shape=[like(blocks[0].shape, blocks[0].dtype)] * len(rules),
        scratch_shapes=[pltpu.SemaphoreType.DMA((len(rules),))],
        compiler_params=pltpu.CompilerParams(vmem_limit_bytes=8 * MIB),
        cost_estimate=cost(blocks),
        name="pick",
    )(*blocks, *after)


def take_kernel(over_x, over_y, block, one, other, again, sem):
    copies = [
        pltpu.make_async_copy(over_x.at[0], one, sem.at[0]),
        pltpu.make_async_copy(over_y.at[1], other, sem.at[1]),
        pltpu.make_async_copy(block, again, sem.at[2]),
    ]
    for copy in copies:
        copy.start()
    for copy in copies:
        copy.wait()


def take(over_x, over_y, block):
    out = like(over_x.shape[1:], over_x.dtype)
    return pl.pallas_call(
        take_kernel,
        in_specs=[VMEM] * 3,
        out_specs=[VMEM] * 3,
        out_shape=[out, out, like(block.shape, block.dtype)],
        scratch_shapes=[pltpu.SemaphoreType.DMA((3,))],
        compiler_params=pltpu.CompilerParams(vmem_limit_bytes=8 * MIB),
        cost_estimate=cost([out, out]),
        name="take",
    )(over_x, over_y, block)


def expert_view(info, expert, top):
    tokens = info.shape[1] // 3
    at = info[:top, :tokens] == expert.astype(jnp.float32)
    rank = jnp.sum(jnp.where(at, info[:top, tokens : 2 * tokens] + 1.0, 0.0), axis=0, keepdims=True) - 1.0
    gate = jnp.sum(jnp.where(at, info[:top, 2 * tokens :], 0.0), axis=0, keepdims=True)
    return at, rank, gate


def rank_picks(rank, count, first, limit):
    numbers = lax.broadcasted_iota(jnp.int32, (count, rank.shape[1]), 0)
    hit = (numbers.astype(jnp.float32) == rank) & (first + numbers < limit)
    return jnp.where(hit, 1.0, 0.0)


def share_kernel(local, most, top, group, earlier, waits, cap, weight, *refs):
    blocks, refs = refs[: 2 * len(group)], refs[2 * len(group) :]
    if earlier is None:
        send, keep, info, rows = refs[waits:]
    else:
        stored, befores = refs[:4], refs[4 : 4 + earlier]
        send, keep, gates, mine, theirs, rows, info, grads = refs[4 + earlier + waits :]
    z, core, x, y = place()
    tokens = blocks[0].shape[0] - TAIL
    total, width = keep.shape[1], keep.shape[2]
    expert = (2 * z + core) * 2 + local

    def gather(at, block, side):
        table = block[tokens:, : 3 * tokens].astype(jnp.float32)
        info[2 * at + side] = table
        _, rank, gate = expert_view(table, expert, top)
        first = (2 * chip_of(z, group[at]) + side) * most
        picks = rank_picks(rank, most, first, cap[local])
        span = pl.ds(pl.multiple_of((2 * at + side) * most, most), most)
        rows[span, :] = jnp.dot(
            picks.astype(jnp.bfloat16), block[:tokens, :], preferred_element_type=jnp.float32
        ).astype(jnp.bfloat16)
        if earlier is not None:
            weights = jnp.sum(picks * gate, axis=1, keepdims=True)
            gates[span, :] = jnp.broadcast_to(weights, (most, gates.shape[1]))

    for swap in range(2):
        side = lax.rem(core + swap, 2)
        for at in range(len(group)):
            gather(at, blocks[2 * at + swap], side)

    powers = []
    for number, (sent, onward) in enumerate(((1, 1), (1, 0), (0, 1), (0, 0))):
        dx, dy = (sent, onward) if local == 0 else (onward, sent)
        piece = 2 * lax.rem(y + dy, 2) + lax.rem(x + dx, 2)
        part = lax.dot_general(
            rows[...],
            weight[local, pl.ds(pl.multiple_of(piece * width, width), width), :],
            (((1,), (1,)), ((), ())),
            preferred_element_type=jnp.float32,
        )
        if earlier is not None:
            there = stored[3][...] if dx and dy else stored[2 * dy + dx][local]
            grad = there.astype(jnp.float32) * part
            grad = jnp.sum(grad, axis=1, keepdims=True)
            grads[...] = grads[...] + grad if number else grad
        if sent:
            code, power = encode(part)
            send[(1 - onward) * total : (2 - onward) * total, :] = code
            powers.append(power)
        else:
            keep[1 - onward] = part
    send[2 * total :, :] = powers_block(powers, width)

    if earlier is not None:
        for out, befores_of in ((mine, befores[0::2]), (theirs, befores[1::2])):
            out[...] = sum((b[...] for b in befores_of), jnp.zeros(out.shape, jnp.float32))
        for at, step in enumerate(group):
            chip = chip_of(z, step)
            for out, side in ((mine, core), (theirs, 1 - core)):
                named, rank, _ = expert_view(info[2 * at + side], expert, top)
                picks = rank_picks(rank, most, (2 * chip + side) * most, cap[local])
                span = pl.ds(pl.multiple_of((2 * at + side) * most, most), most)
                back = jnp.sum(picks * grads[span, :], axis=0, keepdims=True)
                out[chip] = out[chip] + jnp.where(named, back, 0.0)


def partial_share(local, most, top, group, cap, weight, blocks, stored=None, befores=(), after=()):
    tokens, feats = blocks[0].shape[0] - TAIL, blocks[0].shape[1]
    width = weight.shape[1] // 4
    total = 2 * most * len(group)
    tables = (2 * len(group), TAIL, 3 * tokens)
    outs = [like((2 * total + TAIL, width), jnp.int16), like((2, total, width))]
    scratch = [pltpu.VMEM((total, feats), jnp.bfloat16)]
    args = [cap, weight, *blocks]
    if stored is None:
        outs.append(like(tables))
    else:
        outs += [like((total, 128)), like((3, top, tokens)), like((3, top, tokens))]
        scratch += [pltpu.VMEM(tables, jnp.float32), pltpu.VMEM((total, 1), jnp.float32)]
        args += [*stored, *befores]
    earlier = None if stored is None else len(befores)
    return pl.pallas_call(
        functools.partial(share_kernel, local, most, top, group, earlier, len(after)),
        in_specs=[SMEM] + [VMEM] * (len(args) - 1) + [ANY] * len(after),
        out_specs=[VMEM] * len(outs),
        out_shape=outs,
        scratch_shapes=scratch,
        cost_estimate=cost([weight, *blocks], 8 * total * width * feats),
        compiler_params=pltpu.CompilerParams(vmem_limit_bytes=28 * MIB),
        name=f"share_{local}",
    )(*args, *after)


def middle_kernel(got, keep, *refs):
    send, rest = refs[-2:]
    rows, width = rest.shape
    code, power = encode(keep[0] + decode(got, 0, 2))
    send[:rows, :] = code
    send[rows:, :] = powers_block([power], width)
    rest[...] = keep[1] + decode(got, 1, 2)


def middle(got, keep, after=()):
    _, rows, width = keep.shape
    return pl.pallas_call(
        middle_kernel,
        in_specs=[VMEM, VMEM] + [ANY] * len(after),
        out_specs=[VMEM, VMEM],
        out_shape=[like((rows + TAIL, width), jnp.int16), like((rows, width))],
        cost_estimate=cost([got, keep, keep]),
        compiler_params=pltpu.CompilerParams(vmem_limit_bytes=8 * MIB),
        name="middle",
    )(got, keep, *after)


def first_finish_kernel(
    most, top, cap, hidden, info, got0, rest0, got1, rest1, more_mine, more_theirs, out, mine, theirs
):
    z, core, _, _ = place()
    chip = chip_of(z, 0)
    mine[...] = more_mine[...]
    theirs[...] = more_theirs[...]
    for local, (got, rest) in enumerate(((got0, rest0), (got1, rest1))):
        out[local] = rest[...] + decode(got, 0, 1)
        for parts, side in ((mine, core), (theirs, 1 - core)):
            span = pl.ds(pl.multiple_of(side * most, most), most)
            named, rank, gate = expert_view(info[side], (2 * z + core) * 2 + local, top)
            picks = rank_picks(rank, most, (2 * chip + side) * most, cap[local])
            weight = jnp.sum(picks * gate, axis=1, keepdims=True)
            share = out[local, span, :]
            grad = jnp.sum(hidden[local, span, :].astype(jnp.float32) * share, axis=1, keepdims=True)
            out[local, span, :] = weight * share
            back = jnp.sum(picks * grad, axis=0, keepdims=True)
            parts[chip] = parts[chip] + jnp.where(named, back, 0.0)


def first_finish(most, top, cap, hidden, info, sums, parts):
    tokens = info.shape[2] // 3
    return pl.pallas_call(
        functools.partial(first_finish_kernel, most, top),
        in_specs=[SMEM] + [VMEM] * 8,
        out_specs=[VMEM] * 3,
        out_shape=[like(hidden.shape), like((3, top, tokens)), like((3, top, tokens))],
        compiler_params=pltpu.CompilerParams(vmem_limit_bytes=8 * MIB),
        cost_estimate=cost([*sums, hidden]),
        name="first_finish",
    )(cap, hidden, info, *sums, *parts)


def finish_kernel(most, first, got0, rest0, gates0, got1, rest1, gates1, *refs):
    totals, (out, gate_grad) = refs[:-2], refs[-2:]
    gate_grad[...] = sum((total[...] for total in totals[1:]), totals[0][...])
    z = place()[0]
    spans = [pl.ds(pl.multiple_of(chip_of(z, s) * (2 * most), 2 * most), 2 * most) for s in range(3)]
    for local, (got, rest, gates) in enumerate(((got0, rest0, gates0), (got1, rest1, gates1))):
        out[local, spans[0], :] = first[local]
        grad = gates[:, :1] * (rest[...] + decode(got, 0, 1))
        out[local, spans[1], :] = grad[: 2 * most]
        out[local, spans[2], :] = grad[2 * most :]


def finish(most, first, sums, totals):
    experts, rows, width = first.shape
    return pl.pallas_call(
        functools.partial(finish_kernel, most),
        in_specs=[VMEM] * (7 + len(totals)),
        out_specs=[VMEM, VMEM],
        out_shape=[like((experts, 3 * rows, width)), like(totals[0].shape)],
        compiler_params=pltpu.CompilerParams(vmem_limit_bytes=16 * MIB),
        cost_estimate=cost([*sums, first, first]),
        name="finish",
    )(first, *sums, *totals)


def chips_kernel(mine, got, stay, away):
    z = place()[0]
    low, mid, high = (mine[i] + got[i] for i in range(3))
    none = jnp.zeros(low.shape, jnp.float32)
    stay[0] = jnp.where(z < 2, low, high)
    stay[1] = jnp.where(z < 2, mid, none)
    away[0] = jnp.where(z < 2, high, low)
    away[1] = jnp.where(z < 2, none, mid)


def chip_kernel(kept, got, stay, away):
    odd = lax.rem(place()[0], 2) == 1
    even_part, odd_part = (kept[i] + got[i] for i in range(2))
    stay[...] = jnp.where(odd, odd_part, even_part)
    away[...] = jnp.where(odd, even_part, odd_part)


def add_kernel(*refs):
    total = refs[0][...]
    for ref in refs[1:-1]:
        total = total + ref[...]
    refs[-1][...] = total


def small(kernel, outs, *args):
    return pl.pallas_call(
        kernel,
        in_specs=[VMEM] * len(args),
        out_specs=[VMEM] * len(outs),
        out_shape=outs,
        compiler_params=pltpu.CompilerParams(vmem_limit_bytes=2 * MIB),
        cost_estimate=cost(args),
        name=kernel.__name__,
    )(*args)


def blockwise(most, grad_out, routes, slots, gates, capacity, hidden, down_weight):
    peers, ranks = lax.axis_size("expert"), lax.axis_size("dp")
    tokens, top = routes.shape

    def along(rows, pairs):
        return lax.ppermute(rows, "expert", [(2 * a + c, 2 * b + c) for a, b in pairs for c in range(2)])

    def across(rows):
        return lax.ppermute(rows, "expert", [(i, i ^ 1) for i in range(peers)])

    def over(rows, flip):
        return lax.ppermute(rows, "dp", [(i, i ^ flip) for i in range(ranks)])

    block, first_hidden, other_hidden = prepare(most, grad_out, routes, slots, gates, hidden)
    up1 = along(block, [(0, 1), (1, 2), (2, 3)])
    down1 = along(block, [(2, 1), (1, 0)])
    stored = [other_hidden, over(other_hidden, 1), over(other_hidden, 2)]
    *passed, again = take(stored[1], stored[2], block)
    far_stored = [over(passed[0], 2), over(passed[1], 1)]
    weight = load(block, down_weight)

    (first,) = pick(((0, 0, 0, 1),), (block, up1), (weight, down1))
    up2 = along(up1, [(1, 2), (2, 3)])
    down2 = along(again, [(2, 0)])
    pair = (first, across(first))
    sent, kept = [], []
    for local in range(2):
        send, keep, info = partial_share(
            local, most, top, (0,), capacity, weight, pair, after=far_stored if local else ()
        )
        sent.append(send)
        kept.append(keep)

    up3 = along(up2, [(2, 3)])
    (second,) = pick(((2, 0, 0, 1),), (up1, up2, down1), (*sent, *far_stored))
    blocks = [second, across(second)]

    sums, onward = [], []
    for local in range(2):
        send, rest = middle(over(sent[local], 1 + local), kept[local])
        onward.append(send)
        sums += [over(send, 2 - local), rest]
    (third,) = pick(((0, 1, 2, 3),), (down2, down1, up2, up3), ())
    blocks += [third, across(third)]

    halves = []
    before = []
    for local in range(2):
        send, keep, gate, *before = partial_share(
            local, most, top, (1, 2), capacity, weight, blocks, [*stored, far_stored[local]], before,
            (sums[0], sums[2]) if local else onward,
        )
        halves.append((over(send, 1 + local), keep, gate))
    first_grad, mine, theirs = first_finish(most, top, capacity, first_hidden, info, sums, before)

    one = like((top, tokens))
    two = like((2, top, tokens))
    stay, away = small(chips_kernel, [two, two], mine, across(theirs))
    stay, away = small(
        chip_kernel, [one, one], stay, along(away, [(z, z ^ 2) for z in range(peers // 2)])
    )
    (total,) = small(add_kernel, [one], stay, along(away, [(z, z ^ 1) for z in range(peers // 2)]))
    whole = [total] + [over(total, flip) for flip in range(1, ranks)]

    sums = []
    for local, (got, keep, gate) in enumerate(halves):
        send, rest = middle(got, keep, (total,))
        sums += [over(send, 2 - local), rest, gate]
    hidden_grad, gate_grad = finish(most, first_grad, sums, whole)
    return hidden_grad, gate_grad.T


def solution(mesh):
    peers, ranks = mesh.shape["expert"], mesh.shape["dp"]

    def shards(grad_out, routes, slots, gates, capacity, hidden, down_weight):
        tokens, top = routes.shape
        experts = down_weight.shape[0] * peers
        most = top * max(2, (tokens + experts - 1) // experts)
        full = most * experts == tokens * top
        fits = peers == 8 and hidden.shape[1] == 6 * most and 3 * tokens <= grad_out.shape[1]
        square = ranks == 4 and down_weight.shape[0] == 2 and experts <= 256 and most <= 256
        if full and fits and square:
            return blockwise(most, grad_out, routes, slots, gates, capacity, hidden, down_weight)
        return general(grad_out, routes, slots, gates, capacity, hidden, down_weight)

    placed = (
        P("expert", "dp"),
        P("expert", None),
        P("expert", None),
        P("expert", None),
        P("expert"),
        P("expert", None, "dp"),
        P("expert", None, "dp"),
    )
    return jax.shard_map(
        shards,
        mesh=mesh,
        in_specs=placed,
        out_specs=(P("expert", None, "dp"), P("expert", None)),
        check_vma=False,
    )
```

```python
import functools
import math

import jax
import jax.numpy as jnp
from jax import lax
from jax.experimental import pallas as pl
from jax.experimental.pallas import tpu as pltpu
from jax.sharding import PartitionSpec as P

STEPS = 32766.0
TAIL = 16
VMEM = pl.BlockSpec(memory_space=pltpu.VMEM)
ANY = pl.BlockSpec(memory_space=pl.ANY)
SMEM = pl.BlockSpec(memory_space=pltpu.SMEM)


def local_ranks(route_grid, expert_total):
    onehot = (route_grid[..., None] == jnp.arange(expert_total, dtype=jnp.int32)).astype(jnp.int32)
    before = jnp.cumsum(onehot, axis=-2) - onehot
    return jnp.sum(before * onehot, axis=-1)


def capacity_of(local_expert, capacity):
    picks = local_expert[..., None] == jnp.arange(capacity.shape[0], dtype=jnp.int32)
    return jnp.sum(jnp.where(picks, capacity, 0), axis=-1)


def general(grad_out, routes, slots, gates, capacity, hidden, down_weight):
    peer_count = lax.axis_size("expert")
    experts_here = down_weight.shape[0]
    slot_count = hidden.shape[1]
    tok_rows, top_count = routes.shape
    feature_width = grad_out.shape[1]
    expert_total = experts_here * peer_count
    most_rows = top_count * max(2, (tok_rows + expert_total - 1) // expert_total)
    slot_total = experts_here * slot_count
    route_flat = routes.reshape(-1)
    slot_flat = slots.reshape(-1)
    dest_pos = route_flat * most_rows + local_ranks(route_flat, expert_total)
    send_rows = (
        jnp.zeros((expert_total * most_rows, feature_width), jnp.bfloat16)
        .at[dest_pos]
        .set(jnp.repeat(grad_out, top_count, axis=0))
    )
    send_gate = (
        jnp.zeros((expert_total * most_rows,), jnp.bfloat16).at[dest_pos].set(gates.reshape(-1))
    )
    send_slot = (
        jnp.full((expert_total * most_rows,), slot_count, jnp.int32).at[dest_pos].set(slot_flat)
    )
    exchange = functools.partial(
        lax.all_to_all, axis_name="expert", split_axis=0, concat_axis=0, tiled=True
    )
    recv_rows = exchange(send_rows.reshape(peer_count, experts_here * most_rows, feature_width))
    recv_gate = exchange(send_gate.reshape(peer_count, experts_here * most_rows))
    recv_slot = exchange(send_slot.reshape(peer_count, experts_here * most_rows))
    local_expert = jnp.broadcast_to(
        (jnp.arange(experts_here * most_rows, dtype=jnp.int32) // most_rows)[None, :],
        recv_slot.shape,
    )
    usable = recv_slot < capacity_of(local_expert, capacity)
    slot_table = jnp.where(usable, local_expert * slot_count + recv_slot, slot_total).reshape(-1)
    slot_rows = (
        jnp.zeros((slot_total, feature_width), jnp.bfloat16)
        .at[slot_table]
        .set(recv_rows.reshape(-1, feature_width), mode="drop")
    )
    slot_gate = (
        jnp.zeros((slot_total,), jnp.bfloat16)
        .at[slot_table]
        .set(recv_gate.reshape(-1), mode="drop")
    )
    slot_blocks = slot_rows.reshape(experts_here, slot_count, feature_width)
    share_rows = lax.psum_scatter(
        jnp.einsum("efd,ecd->fec", down_weight, slot_blocks, preferred_element_type=jnp.float32),
        "dp",
        scatter_dimension=0,
        tiled=True,
    )
    hidden_share = jnp.transpose(share_rows, (1, 2, 0))
    hidden_grad = (
        slot_gate.reshape(experts_here, slot_count)[..., None].astype(jnp.float32) * hidden_share
    )
    partial_grad = jnp.sum(hidden.astype(jnp.float32) * hidden_share, axis=-1)
    slot_grad = lax.psum(partial_grad, "dp").reshape(-1)
    picked = slot_grad[jnp.minimum(slot_table, slot_total - 1)]
    outgoing = jnp.where(slot_table < slot_total, picked, jnp.float32(0.0)).reshape(
        peer_count, experts_here * most_rows
    )
    incoming = exchange(outgoing).reshape(-1)
    gate_grad = incoming[dest_pos].reshape(tok_rows, top_count)
    return hidden_grad, gate_grad


ORDER = ((0, 1, 2), (1, 0, 2), (2, 1, 0), (2, 1, 0))
MIB = 2**20


def cost(shapes, flops=0):
    size = sum(math.prod(a.shape) * a.dtype.itemsize for a in shapes)
    return pl.CostEstimate(flops=flops, bytes_accessed=size, transcendentals=0)


def hbm(array):
    return pltpu.with_memory_space_constraint(array, pltpu.HBM)


def like(shape, kind=jnp.float32):
    return jax.ShapeDtypeStruct(shape, kind)


def place():
    me, rank = lax.axis_index("expert"), lax.axis_index("dp")
    return me // 2, lax.rem(me, 2), lax.rem(rank, 2), rank // 2


def chip_of(z, step):
    chip = jnp.int32(ORDER[0][step])
    for at_z in range(1, len(ORDER)):
        chip = jnp.where(z == at_z, ORDER[at_z][step], chip)
    return chip


def encode(values):
    peak = jnp.maximum(jnp.max(jnp.abs(values), keepdims=True), 1e-30)
    power = jnp.floor(jnp.log2(peak)) + 1.0
    scaled = values * (jnp.exp2(-power) * (STEPS * STEPS))
    code = jnp.round(scaled * lax.rsqrt(jnp.abs(scaled) + 1e-20))
    return code.astype(jnp.int32).astype(jnp.int16), power


def powers_block(powers, width):
    spans = [jnp.broadcast_to(power, (TAIL, width // len(powers))) for power in powers]
    return jnp.concatenate(spans, axis=1).astype(jnp.int32).astype(jnp.int16)


def decode(coded, part, parts):
    rows = (coded.shape[0] - TAIL) // parts
    lane = part * (coded.shape[1] // parts)
    power = coded[parts * rows :, lane : lane + 128].astype(jnp.int32).astype(jnp.float32)
    code = coded[part * rows : (part + 1) * rows, :].astype(jnp.int32).astype(jnp.float32)
    scale = jnp.exp2(jnp.max(power, keepdims=True)) * (1.0 / (STEPS * STEPS))
    return code * jnp.abs(code) * scale


def prepare_kernel(
    most, rows, routes, slots, gates, hidden, out, first, others, routes_in, slots_in, gates_in, sem
):
    tokens, top = rows.shape[0], routes.shape[0]
    z, core, _, _ = place()
    pairs = [(routes, routes_in), (slots, slots_in), (gates, gates_in), (rows, out.at[:tokens])]
    for step in range(3):
        start = pl.multiple_of(chip_of(z, step) * (2 * most), 2 * most)
        for local in range(2):
            span = others.at[local, 2 * most * (step - 1) : 2 * most * step] if step else first.at[local]
            pairs.append((hidden.at[local, pl.ds(start, 2 * most)], span))
    copies = [pltpu.make_async_copy(a, b, sem.at[i]) for i, (a, b) in enumerate(pairs)]
    for copy in copies:
        copy.start()
    for copy in copies[:3]:
        copy.wait()
    rank = slots_in[...] - (2 * z + core) * most
    parts = [routes_in[...], rank, gates_in[...]]
    packed = jnp.concatenate([part.astype(jnp.float32) for part in parts], axis=1)
    packed = jnp.concatenate([packed, jnp.zeros((TAIL - top, 3 * tokens), jnp.float32)], axis=0)
    out[tokens:, : 3 * tokens] = packed.astype(jnp.bfloat16)
    out[tokens:, 3 * tokens :] = jnp.zeros((TAIL, out.shape[1] - 3 * tokens), jnp.bfloat16)
    for copy in copies[3:]:
        copy.wait()


def prepare(most, grad_out, routes, slots, gates, hidden):
    tokens, feats = grad_out.shape
    top = routes.shape[1]
    experts, _, width = hidden.shape
    return pl.pallas_call(
        functools.partial(prepare_kernel, most),
        in_specs=[ANY] * 5,
        out_specs=[VMEM] * 3,
        out_shape=[
            like((tokens + TAIL, feats), jnp.bfloat16),
            like((experts, 2 * most, width), jnp.bfloat16),
            like((experts, 4 * most, width), jnp.bfloat16),
        ],
        scratch_shapes=[
            pltpu.VMEM((top, tokens), jnp.int32),
            pltpu.VMEM((top, tokens), jnp.int32),
            pltpu.VMEM((top, tokens), jnp.bfloat16),
            pltpu.SemaphoreType.DMA((10,)),
        ],
        compiler_params=pltpu.CompilerParams(vmem_limit_bytes=8 * MIB),
        cost_estimate=cost([grad_out, grad_out, hidden]),
        name="prepare",
    )(*(hbm(a) for a in (grad_out, routes.T, slots.T, gates.T, hidden)))


def load_kernel(after, weight, out, sem):
    copy = pltpu.make_async_copy(weight, out, sem)
    copy.start()
    copy.wait()


def load(after, weight):
    return pl.pallas_call(
        load_kernel,
        in_specs=[ANY, ANY],
        out_specs=VMEM,
        out_shape=like(weight.shape, weight.dtype),
        scratch_shapes=[pltpu.SemaphoreType.DMA],
        cost_estimate=cost([weight, weight]),
        compiler_params=pltpu.CompilerParams(vmem_limit_bytes=16 * MIB),
        name="load_weight",
    )(after, hbm(weight))


def pick_kernel(rules, count, *refs):
    sem = refs[-1]
    outs = refs[-1 - len(rules) : -1]
    z = place()[0]
    for number, rule in enumerate(rules):
        for source in sorted(set(rule)):
            wanted = functools.reduce(
                jnp.logical_or, [z == at_z for at_z in range(len(rule)) if rule[at_z] == source]
            )

            @pl.when(wanted)
            def _(source=source, number=number):
                pltpu.make_async_copy(refs[source], outs[number], sem.at[number]).start()

    for number in range(len(rules)):
        pltpu.make_async_copy(refs[0], outs[number], sem.at[number]).wait()


def pick(rules, blocks, after):
    return pl.pallas_call(
        functools.partial(pick_kernel, rules, len(blocks)),
        in_specs=[VMEM] * len(blocks) + [ANY] * len(after),
        out_specs=[VMEM] * len(rules),
        out_shape=[like(blocks[0].shape, blocks[0].dtype)] * len(rules),
        scratch_shapes=[pltpu.SemaphoreType.DMA((len(rules),))],
        compiler_params=pltpu.CompilerParams(vmem_limit_bytes=8 * MIB),
        cost_estimate=cost(blocks),
        name="pick",
    )(*blocks, *after)


def take_kernel(over_x, over_y, block, one, other, again, sem):
    copies = [
        pltpu.make_async_copy(over_x.at[0], one, sem.at[0]),
        pltpu.make_async_copy(over_y.at[1], other, sem.at[1]),
        pltpu.make_async_copy(block, again, sem.at[2]),
    ]
    for copy in copies:
        copy.start()
    for copy in copies:
        copy.wait()


def take(over_x, over_y, block):
    out = like(over_x.shape[1:], over_x.dtype)
    return pl.pallas_call(
        take_kernel,
        in_specs=[VMEM] * 3,
        out_specs=[VMEM] * 3,
        out_shape=[out, out, like(block.shape, block.dtype)],
        scratch_shapes=[pltpu.SemaphoreType.DMA((3,))],
        compiler_params=pltpu.CompilerParams(vmem_limit_bytes=8 * MIB),
        cost_estimate=cost([out, out]),
        name="take",
    )(over_x, over_y, block)


def expert_view(info, expert, top):
    tokens = info.shape[1] // 3
    at = info[:top, :tokens] == expert.astype(jnp.float32)
    rank = jnp.sum(jnp.where(at, info[:top, tokens : 2 * tokens] + 1.0, 0.0), axis=0, keepdims=True) - 1.0
    gate = jnp.sum(jnp.where(at, info[:top, 2 * tokens :], 0.0), axis=0, keepdims=True)
    return at, rank, gate


def rank_picks(rank, count, first, limit):
    numbers = lax.broadcasted_iota(jnp.int32, (count, rank.shape[1]), 0)
    hit = (numbers.astype(jnp.float32) == rank) & (first + numbers < limit)
    return jnp.where(hit, 1.0, 0.0)


def share_kernel(local, most, top, group, earlier, waits, cap, weight, *refs):
    blocks, refs = refs[: 2 * len(group)], refs[2 * len(group) :]
    if earlier is None:
        send, keep, info, rows = refs[waits:]
    else:
        stored, befores = refs[:4], refs[4 : 4 + earlier]
        send, keep, gates, mine, theirs, rows, info, grads = refs[4 + earlier + waits :]
    z, core, x, y = place()
    tokens = blocks[0].shape[0] - TAIL
    total, width = keep.shape[1], keep.shape[2]
    expert = (2 * z + core) * 2 + local

    def gather(at, block, side):
        table = block[tokens:, : 3 * tokens].astype(jnp.float32)
        info[2 * at + side] = table
        _, rank, gate = expert_view(table, expert, top)
        first = (2 * chip_of(z, group[at]) + side) * most
        picks = rank_picks(rank, most, first, cap[local])
        span = pl.ds(pl.multiple_of((2 * at + side) * most, most), most)
        rows[span, :] = jnp.dot(
            picks.astype(jnp.bfloat16), block[:tokens, :], preferred_element_type=jnp.float32
        ).astype(jnp.bfloat16)
        if earlier is not None:
            weights = jnp.sum(picks * gate, axis=1, keepdims=True)
            gates[span, :] = jnp.broadcast_to(weights, (most, gates.shape[1]))

    for swap in range(2):
        side = lax.rem(core + swap, 2)
        for at in range(len(group)):
            gather(at, blocks[2 * at + swap], side)

    powers = []
    for number, (sent, onward) in enumerate(((1, 1), (1, 0), (0, 1), (0, 0))):
        dx, dy = (sent, onward) if local == 0 else (onward, sent)
        piece = 2 * lax.rem(y + dy, 2) + lax.rem(x + dx, 2)
        part = lax.dot_general(
            rows[...],
            weight[local, pl.ds(pl.multiple_of(piece * width, width), width), :],
            (((1,), (1,)), ((), ())),
            preferred_element_type=jnp.float32,
        )
        if earlier is not None:
            there = stored[3][...] if dx and dy else stored[2 * dy + dx][local]
            grad = there.astype(jnp.float32) * part
            grad = jnp.sum(grad, axis=1, keepdims=True)
            grads[...] = grads[...] + grad if number else grad
        if sent:
            code, power = encode(part)
            send[(1 - onward) * total : (2 - onward) * total, :] = code
            powers.append(power)
        else:
            keep[1 - onward] = part
    send[2 * total :, :] = powers_block(powers, width)

    if earlier is not None:
        for out, befores_of in ((mine, befores[0::2]), (theirs, befores[1::2])):
            out[...] = sum((b[...] for b in befores_of), jnp.zeros(out.shape, jnp.float32))
        for at, step in enumerate(group):
            chip = chip_of(z, step)
            for out, side in ((mine, core), (theirs, 1 - core)):
                named, rank, _ = expert_view(info[2 * at + side], expert, top)
                picks = rank_picks(rank, most, (2 * chip + side) * most, cap[local])
                span = pl.ds(pl.multiple_of((2 * at + side) * most, most), most)
                back = jnp.sum(picks * grads[span, :], axis=0, keepdims=True)
                out[chip] = out[chip] + jnp.where(named, back, 0.0)


def partial_share(local, most, top, group, cap, weight, blocks, stored=None, befores=(), after=()):
    tokens, feats = blocks[0].shape[0] - TAIL, blocks[0].shape[1]
    width = weight.shape[1] // 4
    total = 2 * most * len(group)
    tables = (2 * len(group), TAIL, 3 * tokens)
    outs = [like((2 * total + TAIL, width), jnp.int16), like((2, total, width))]
    scratch = [pltpu.VMEM((total, feats), jnp.bfloat16)]
    args = [cap, weight, *blocks]
    if stored is None:
        outs.append(like(tables))
    else:
        outs += [like((total, 128)), like((3, top, tokens)), like((3, top, tokens))]
        scratch += [pltpu.VMEM(tables, jnp.float32), pltpu.VMEM((total, 1), jnp.float32)]
        args += [*stored, *befores]
    earlier = None if stored is None else len(befores)
    return pl.pallas_call(
        functools.partial(share_kernel, local, most, top, group, earlier, len(after)),
        in_specs=[SMEM] + [VMEM] * (len(args) - 1) + [ANY] * len(after),
        out_specs=[VMEM] * len(outs),
        out_shape=outs,
        scratch_shapes=scratch,
        cost_estimate=cost([weight, *blocks], 8 * total * width * feats),
        compiler_params=pltpu.CompilerParams(vmem_limit_bytes=28 * MIB),
        name=f"share_{local}",
    )(*args, *after)


def middle_kernel(got, keep, *refs):
    send, rest = refs[-2:]
    rows, width = rest.shape
    code, power = encode(keep[0] + decode(got, 0, 2))
    send[:rows, :] = code
    send[rows:, :] = powers_block([power], width)
    rest[...] = keep[1] + decode(got, 1, 2)


def middle(got, keep, after=()):
    _, rows, width = keep.shape
    return pl.pallas_call(
        middle_kernel,
        in_specs=[VMEM, VMEM] + [ANY] * len(after),
        out_specs=[VMEM, VMEM],
        out_shape=[like((rows + TAIL, width), jnp.int16), like((rows, width))],
        cost_estimate=cost([got, keep, keep]),
        compiler_params=pltpu.CompilerParams(vmem_limit_bytes=8 * MIB),
        name="middle",
    )(got, keep, *after)


def first_finish_kernel(
    most, top, cap, hidden, info, got0, rest0, got1, rest1, more_mine, more_theirs, out, mine, theirs
):
    z, core, _, _ = place()
    chip = chip_of(z, 0)
    mine[...] = more_mine[...]
    theirs[...] = more_theirs[...]
    for local, (got, rest) in enumerate(((got0, rest0), (got1, rest1))):
        out[local] = rest[...] + decode(got, 0, 1)
        for parts, side in ((mine, core), (theirs, 1 - core)):
            span = pl.ds(pl.multiple_of(side * most, most), most)
            named, rank, gate = expert_view(info[side], (2 * z + core) * 2 + local, top)
            picks = rank_picks(rank, most, (2 * chip + side) * most, cap[local])
            weight = jnp.sum(picks * gate, axis=1, keepdims=True)
            share = out[local, span, :]
            grad = jnp.sum(hidden[local, span, :].astype(jnp.float32) * share, axis=1, keepdims=True)
            out[local, span, :] = weight * share
            back = jnp.sum(picks * grad, axis=0, keepdims=True)
            parts[chip] = parts[chip] + jnp.where(named, back, 0.0)


def first_finish(most, top, cap, hidden, info, sums, parts):
    tokens = info.shape[2] // 3
    return pl.pallas_call(
        functools.partial(first_finish_kernel, most, top),
        in_specs=[SMEM] + [VMEM] * 8,
        out_specs=[VMEM] * 3,
        out_shape=[like(hidden.shape), like((3, top, tokens)), like((3, top, tokens))],
        compiler_params=pltpu.CompilerParams(vmem_limit_bytes=8 * MIB),
        cost_estimate=cost([*sums, hidden]),
        name="first_finish",
    )(cap, hidden, info, *sums, *parts)


def finish_kernel(most, first, got0, rest0, gates0, got1, rest1, gates1, *refs):
    totals, (out, gate_grad, grads, sem) = refs[:-4], refs[-4:]
    z = place()[0]
    spans = [pl.ds(pl.multiple_of(chip_of(z, s) * (2 * most), 2 * most), 2 * most) for s in range(3)]
    copies = [
        pltpu.make_async_copy(first.at[local], out.at[local, spans[0]], sem.at[local])
        for local in range(2)
    ]
    for copy in copies:
        copy.start()
    for local, (got, rest, gates) in enumerate(((got0, rest0, gates0), (got1, rest1, gates1))):
        grads[local] = gates[:, :1] * (rest[...] + decode(got, 0, 1))
        for step in (1, 2):
            part = grads.at[local, 2 * most * (step - 1) : 2 * most * step]
            copy = pltpu.make_async_copy(part, out.at[local, spans[step]], sem.at[2 * step + local])
            copy.start()
            copies.append(copy)
    gate_grad[...] = sum((total[...] for total in totals[1:]), totals[0][...])
    for copy in copies:
        copy.wait()


def finish(most, first, sums, totals):
    experts, rows, width = first.shape
    return pl.pallas_call(
        functools.partial(finish_kernel, most),
        in_specs=[VMEM] * (7 + len(totals)),
        out_specs=[ANY, VMEM],
        out_shape=[pltpu.HBM((experts, 3 * rows, width), jnp.float32), like(totals[0].shape)],
        scratch_shapes=[
            pltpu.VMEM((experts, 2 * rows, width), jnp.float32),
            pltpu.SemaphoreType.DMA((6,)),
        ],
        compiler_params=pltpu.CompilerParams(vmem_limit_bytes=16 * MIB),
        cost_estimate=cost([*sums, first, first]),
        name="finish",
    )(first, *sums, *totals)


def chips_kernel(mine, got, own, *shifted):
    z = place()[0]
    for shift, out in enumerate((own, *shifted)):
        chip = lax.rem(z + shift, len(ORDER))
        at = jnp.minimum(chip, mine.shape[0] - 1)
        out[...] = jnp.where(chip == at, mine[at] + got[at], 0.0)


def add_kernel(*refs):
    total = refs[0][...]
    for ref in refs[1:-1]:
        total = total + ref[...]
    refs[-1][...] = total


def small(kernel, outs, *args, after=()):
    used = len(args)
    return pl.pallas_call(
        lambda *refs: kernel(*refs[:used], *refs[used + len(after) :]),
        in_specs=[VMEM] * used + [ANY] * len(after),
        out_specs=[VMEM] * len(outs),
        out_shape=outs,
        compiler_params=pltpu.CompilerParams(vmem_limit_bytes=2 * MIB),
        cost_estimate=cost(args),
        name=kernel.__name__,
    )(*args, *after)


def blockwise(most, grad_out, routes, slots, gates, capacity, hidden, down_weight):
    peers, ranks = lax.axis_size("expert"), lax.axis_size("dp")
    tokens, top = routes.shape

    def along(rows, pairs):
        return lax.ppermute(rows, "expert", [(2 * a + c, 2 * b + c) for a, b in pairs for c in range(2)])

    def across(rows):
        return lax.ppermute(rows, "expert", [(i, i ^ 1) for i in range(peers)])

    def over(rows, flip):
        return lax.ppermute(rows, "dp", [(i, i ^ flip) for i in range(ranks)])

    block, first_hidden, other_hidden = prepare(most, grad_out, routes, slots, gates, hidden)
    up1 = along(block, [(0, 1), (1, 2), (2, 3)])
    down1 = along(block, [(2, 1), (1, 0)])
    stored = [other_hidden, over(other_hidden, 1), over(other_hidden, 2)]
    *passed, again = take(stored[1], stored[2], block)
    far_stored = [over(passed[0], 2), over(passed[1], 1)]
    weight = load(block, down_weight)

    (first,) = pick(((0, 0, 0, 1),), (block, up1), (weight, down1))
    up2 = along(up1, [(1, 2), (2, 3)])
    down2 = along(again, [(2, 0)])
    pair = (first, across(first))
    sent, kept = [], []
    for local in range(2):
        send, keep, info = partial_share(
            local, most, top, (0,), capacity, weight, pair, after=far_stored if local else ()
        )
        sent.append(send)
        kept.append(keep)

    up3 = along(up2, [(2, 3)])
    (second,) = pick(((2, 0, 0, 1),), (up1, up2, down1), (*sent, *far_stored))
    blocks = [second, across(second)]

    sums, onward = [], []
    for local in range(2):
        send, rest = middle(over(sent[local], 1 + local), kept[local])
        onward.append(send)
        sums += [over(send, 2 - local), rest]
    (third,) = pick(((0, 1, 2, 3),), (down2, down1, up2, up3), ())
    blocks += [third, across(third)]

    halves = []
    before = []
    for local in range(2):
        send, keep, gate, *before = partial_share(
            local, most, top, (1, 2), capacity, weight, blocks, [*stored, far_stored[local]], before,
            (sums[0], sums[2]) if local else onward,
        )
        halves.append((over(send, 1 + local), keep, gate))
    first_grad, mine, theirs = first_finish(most, top, capacity, first_hidden, info, sums, before)

    one = like((top, tokens))
    chips = small(chips_kernel, [one] * 4, mine, across(theirs))
    chips = [chips[0]] + [
        along(part, [(z, (z + shift) % 4) for z in range(4) if (z + shift) % 4 < 3])
        for shift, part in enumerate(chips[1:], 1)
    ]
    (got0, keep0, gate0), (got1, keep1, gate1) = halves
    send0, rest0 = middle(got0, keep0, chips[1:])
    (total,) = small(add_kernel, [one], *chips, after=(send0,))
    send1, rest1 = middle(got1, keep1, (total,))
    sums = [over(send0, 2), rest0, gate0, over(send1, 1), rest1, gate1]
    whole = [total] + [over(total, flip) for flip in range(1, ranks)]
    hidden_grad, gate_grad = finish(most, first_grad, sums, whole)
    return hidden_grad, gate_grad.T


def solution(mesh):
    peers, ranks = mesh.shape["expert"], mesh.shape["dp"]

    def shards(grad_out, routes, slots, gates, capacity, hidden, down_weight):
        tokens, top = routes.shape
        experts = down_weight.shape[0] * peers
        most = top * max(2, (tokens + experts - 1) // experts)
        full = most * experts == tokens * top
        fits = peers == 8 and hidden.shape[1] == 6 * most and 3 * tokens <= grad_out.shape[1]
        square = ranks == 4 and down_weight.shape[0] == 2 and experts <= 256 and most <= 256
        if full and fits and square:
            return blockwise(most, grad_out, routes, slots, gates, capacity, hidden, down_weight)
        return general(grad_out, routes, slots, gates, capacity, hidden, down_weight)

    placed = (
        P("expert", "dp"),
        P("expert", None),
        P("expert", None),
        P("expert", None),
        P("expert"),
        P("expert", None, "dp"),
        P("expert", None, "dp"),
    )
    return jax.shard_map(
        shards,
        mesh=mesh,
        in_specs=placed,
        out_specs=(P("expert", None, "dp"), P("expert", None)),
        check_vma=False,
    )
```

```python
import functools
import math

import jax
import jax.numpy as jnp
from jax import lax
from jax.experimental import pallas as pl
from jax.experimental.pallas import tpu as pltpu
from jax.sharding import PartitionSpec as P

STEPS = 32766.0
TAIL = 16
VMEM = pl.BlockSpec(memory_space=pltpu.VMEM)
ANY = pl.BlockSpec(memory_space=pl.ANY)
SMEM = pl.BlockSpec(memory_space=pltpu.SMEM)


def local_ranks(route_grid, expert_total):
    onehot = (route_grid[..., None] == jnp.arange(expert_total, dtype=jnp.int32)).astype(jnp.int32)
    before = jnp.cumsum(onehot, axis=-2) - onehot
    return jnp.sum(before * onehot, axis=-1)


def capacity_of(local_expert, capacity):
    picks = local_expert[..., None] == jnp.arange(capacity.shape[0], dtype=jnp.int32)
    return jnp.sum(jnp.where(picks, capacity, 0), axis=-1)


def general(grad_out, routes, slots, gates, capacity, hidden, down_weight):
    peer_count = lax.axis_size("expert")
    experts_here = down_weight.shape[0]
    slot_count = hidden.shape[1]
    tok_rows, top_count = routes.shape
    feature_width = grad_out.shape[1]
    expert_total = experts_here * peer_count
    most_rows = top_count * max(2, (tok_rows + expert_total - 1) // expert_total)
    slot_total = experts_here * slot_count
    route_flat = routes.reshape(-1)
    slot_flat = slots.reshape(-1)
    dest_pos = route_flat * most_rows + local_ranks(route_flat, expert_total)
    send_rows = (
        jnp.zeros((expert_total * most_rows, feature_width), jnp.bfloat16)
        .at[dest_pos]
        .set(jnp.repeat(grad_out, top_count, axis=0))
    )
    send_gate = (
        jnp.zeros((expert_total * most_rows,), jnp.bfloat16).at[dest_pos].set(gates.reshape(-1))
    )
    send_slot = (
        jnp.full((expert_total * most_rows,), slot_count, jnp.int32).at[dest_pos].set(slot_flat)
    )
    exchange = functools.partial(
        lax.all_to_all, axis_name="expert", split_axis=0, concat_axis=0, tiled=True
    )
    recv_rows = exchange(send_rows.reshape(peer_count, experts_here * most_rows, feature_width))
    recv_gate = exchange(send_gate.reshape(peer_count, experts_here * most_rows))
    recv_slot = exchange(send_slot.reshape(peer_count, experts_here * most_rows))
    local_expert = jnp.broadcast_to(
        (jnp.arange(experts_here * most_rows, dtype=jnp.int32) // most_rows)[None, :],
        recv_slot.shape,
    )
    usable = recv_slot < capacity_of(local_expert, capacity)
    slot_table = jnp.where(usable, local_expert * slot_count + recv_slot, slot_total).reshape(-1)
    slot_rows = (
        jnp.zeros((slot_total, feature_width), jnp.bfloat16)
        .at[slot_table]
        .set(recv_rows.reshape(-1, feature_width), mode="drop")
    )
    slot_gate = (
        jnp.zeros((slot_total,), jnp.bfloat16)
        .at[slot_table]
        .set(recv_gate.reshape(-1), mode="drop")
    )
    slot_blocks = slot_rows.reshape(experts_here, slot_count, feature_width)
    share_rows = lax.psum_scatter(
        jnp.einsum("efd,ecd->fec", down_weight, slot_blocks, preferred_element_type=jnp.float32),
        "dp",
        scatter_dimension=0,
        tiled=True,
    )
    hidden_share = jnp.transpose(share_rows, (1, 2, 0))
    hidden_grad = (
        slot_gate.reshape(experts_here, slot_count)[..., None].astype(jnp.float32) * hidden_share
    )
    partial_grad = jnp.sum(hidden.astype(jnp.float32) * hidden_share, axis=-1)
    slot_grad = lax.psum(partial_grad, "dp").reshape(-1)
    picked = slot_grad[jnp.minimum(slot_table, slot_total - 1)]
    outgoing = jnp.where(slot_table < slot_total, picked, jnp.float32(0.0)).reshape(
        peer_count, experts_here * most_rows
    )
    incoming = exchange(outgoing).reshape(-1)
    gate_grad = incoming[dest_pos].reshape(tok_rows, top_count)
    return hidden_grad, gate_grad


ORDER = ((0, 1, 2), (1, 0, 2), (2, 1, 0), (2, 1, 0))
MIB = 2**20


def cost(shapes, flops=0):
    size = sum(math.prod(a.shape) * a.dtype.itemsize for a in shapes)
    return pl.CostEstimate(flops=flops, bytes_accessed=size, transcendentals=0)


def hbm(array):
    return pltpu.with_memory_space_constraint(array, pltpu.HBM)


def like(shape, kind=jnp.float32):
    return jax.ShapeDtypeStruct(shape, kind)


def place():
    me, rank = lax.axis_index("expert"), lax.axis_index("dp")
    return me // 2, lax.rem(me, 2), lax.rem(rank, 2), rank // 2


def chip_of(z, step):
    chip = jnp.int32(ORDER[0][step])
    for at_z in range(1, len(ORDER)):
        chip = jnp.where(z == at_z, ORDER[at_z][step], chip)
    return chip


def encode(values):
    peak = jnp.maximum(jnp.max(jnp.abs(values), keepdims=True), 1e-30)
    power = jnp.floor(jnp.log2(peak)) + 1.0
    scaled = values * (jnp.exp2(-power) * (STEPS * STEPS))
    code = jnp.round(scaled * lax.rsqrt(jnp.abs(scaled) + 1e-20))
    return code.astype(jnp.int32).astype(jnp.int16), power


def powers_block(powers, width):
    spans = [jnp.broadcast_to(power, (TAIL, width // len(powers))) for power in powers]
    return jnp.concatenate(spans, axis=1).astype(jnp.int32).astype(jnp.int16)


def decode(coded, part, parts):
    rows = (coded.shape[0] - TAIL) // parts
    lane = part * (coded.shape[1] // parts)
    power = coded[parts * rows :, lane : lane + 128].astype(jnp.int32).astype(jnp.float32)
    code = coded[part * rows : (part + 1) * rows, :].astype(jnp.int32).astype(jnp.float32)
    scale = jnp.exp2(jnp.max(power, keepdims=True)) * (1.0 / (STEPS * STEPS))
    return code * jnp.abs(code) * scale


def prepare_kernel(
    most, rows, routes, slots, gates, hidden, out, first, others, routes_in, slots_in, gates_in, sem
):
    tokens, top = rows.shape[0], routes.shape[0]
    z, core, _, _ = place()
    pairs = [(routes, routes_in), (slots, slots_in), (gates, gates_in), (rows, out.at[:tokens])]
    for step in range(3):
        start = pl.multiple_of(chip_of(z, step) * (2 * most), 2 * most)
        for local in range(2):
            span = others.at[local, 2 * most * (step - 1) : 2 * most * step] if step else first.at[local]
            pairs.append((hidden.at[local, pl.ds(start, 2 * most)], span))
    copies = [pltpu.make_async_copy(a, b, sem.at[i]) for i, (a, b) in enumerate(pairs)]
    for copy in copies:
        copy.start()
    for copy in copies[:3]:
        copy.wait()
    rank = slots_in[...] - (2 * z + core) * most
    parts = [routes_in[...], rank, gates_in[...]]
    packed = jnp.concatenate([part.astype(jnp.float32) for part in parts], axis=1)
    packed = jnp.concatenate([packed, jnp.zeros((TAIL - top, 3 * tokens), jnp.float32)], axis=0)
    out[tokens:, : 3 * tokens] = packed.astype(jnp.bfloat16)
    out[tokens:, 3 * tokens :] = jnp.zeros((TAIL, out.shape[1] - 3 * tokens), jnp.bfloat16)
    for copy in copies[3:]:
        copy.wait()


def prepare(most, grad_out, routes, slots, gates, hidden):
    tokens, feats = grad_out.shape
    top = routes.shape[1]
    experts, _, width = hidden.shape
    return pl.pallas_call(
        functools.partial(prepare_kernel, most),
        in_specs=[ANY] * 5,
        out_specs=[VMEM] * 3,
        out_shape=[
            like((tokens + TAIL, feats), jnp.bfloat16),
            like((experts, 2 * most, width), jnp.bfloat16),
            like((experts, 4 * most, width), jnp.bfloat16),
        ],
        scratch_shapes=[
            pltpu.VMEM((top, tokens), jnp.int32),
            pltpu.VMEM((top, tokens), jnp.int32),
            pltpu.VMEM((top, tokens), jnp.bfloat16),
            pltpu.SemaphoreType.DMA((10,)),
        ],
        compiler_params=pltpu.CompilerParams(vmem_limit_bytes=8 * MIB),
        cost_estimate=cost([grad_out, grad_out, hidden]),
        name="prepare",
    )(*(hbm(a) for a in (grad_out, routes.T, slots.T, gates.T, hidden)))


def load_kernel(after, weight, out, sem):
    copy = pltpu.make_async_copy(weight, out, sem)
    copy.start()
    copy.wait()


def load(after, weight):
    return pl.pallas_call(
        load_kernel,
        in_specs=[ANY, ANY],
        out_specs=VMEM,
        out_shape=like(weight.shape, weight.dtype),
        scratch_shapes=[pltpu.SemaphoreType.DMA],
        cost_estimate=cost([weight, weight]),
        compiler_params=pltpu.CompilerParams(vmem_limit_bytes=16 * MIB),
        name="load_weight",
    )(after, hbm(weight))


def pick_kernel(rules, count, *refs):
    sem = refs[-1]
    outs = refs[-1 - len(rules) : -1]
    z = place()[0]
    for number, rule in enumerate(rules):
        for source in sorted(set(rule)):
            wanted = functools.reduce(
                jnp.logical_or, [z == at_z for at_z in range(len(rule)) if rule[at_z] == source]
            )

            @pl.when(wanted)
            def _(source=source, number=number):
                pltpu.make_async_copy(refs[source], outs[number], sem.at[number]).start()

    for number in range(len(rules)):
        pltpu.make_async_copy(refs[0], outs[number], sem.at[number]).wait()


def pick(rules, blocks, after):
    return pl.pallas_call(
        functools.partial(pick_kernel, rules, len(blocks)),
        in_specs=[VMEM] * len(blocks) + [ANY] * len(after),
        out_specs=[VMEM] * len(rules),
        out_shape=[like(blocks[0].shape, blocks[0].dtype)] * len(rules),
        scratch_shapes=[pltpu.SemaphoreType.DMA((len(rules),))],
        compiler_params=pltpu.CompilerParams(vmem_limit_bytes=8 * MIB),
        cost_estimate=cost(blocks),
        name="pick",
    )(*blocks, *after)


def take_kernel(over_x, over_y, block, one, other, again, sem):
    copies = [
        pltpu.make_async_copy(over_x.at[0], one, sem.at[0]),
        pltpu.make_async_copy(over_y.at[1], other, sem.at[1]),
        pltpu.make_async_copy(block, again, sem.at[2]),
    ]
    for copy in copies:
        copy.start()
    for copy in copies:
        copy.wait()


def take(over_x, over_y, block):
    out = like(over_x.shape[1:], over_x.dtype)
    return pl.pallas_call(
        take_kernel,
        in_specs=[VMEM] * 3,
        out_specs=[VMEM] * 3,
        out_shape=[out, out, like(block.shape, block.dtype)],
        scratch_shapes=[pltpu.SemaphoreType.DMA((3,))],
        compiler_params=pltpu.CompilerParams(vmem_limit_bytes=8 * MIB),
        cost_estimate=cost([out, out]),
        name="take",
    )(over_x, over_y, block)


def expert_view(info, expert, top):
    tokens = info.shape[1] // 3
    at = info[:top, :tokens] == expert.astype(jnp.float32)
    rank = jnp.sum(jnp.where(at, info[:top, tokens : 2 * tokens] + 1.0, 0.0), axis=0, keepdims=True) - 1.0
    gate = jnp.sum(jnp.where(at, info[:top, 2 * tokens :], 0.0), axis=0, keepdims=True)
    return at, rank, gate


def rank_picks(rank, count, first, limit):
    numbers = lax.broadcasted_iota(jnp.int32, (count, rank.shape[1]), 0)
    hit = (numbers.astype(jnp.float32) == rank) & (first + numbers < limit)
    return jnp.where(hit, 1.0, 0.0)


def share_kernel(local, most, top, group, earlier, waits, cap, weight, *refs):
    blocks, refs = refs[: 2 * len(group)], refs[2 * len(group) :]
    if earlier is None:
        send, keep, info, rows = refs[waits:]
    else:
        stored, befores = refs[:4], refs[4 : 4 + earlier]
        send, keep, gates, mine, theirs, rows, info, grads = refs[4 + earlier + waits :]
    z, core, x, y = place()
    tokens = blocks[0].shape[0] - TAIL
    total, width = keep.shape[1], keep.shape[2]
    expert = (2 * z + core) * 2 + local

    def gather(at, block, side):
        table = block[tokens:, : 3 * tokens].astype(jnp.float32)
        info[2 * at + side] = table
        _, rank, gate = expert_view(table, expert, top)
        first = (2 * chip_of(z, group[at]) + side) * most
        picks = rank_picks(rank, most, first, cap[local])
        span = pl.ds(pl.multiple_of((2 * at + side) * most, most), most)
        rows[span, :] = jnp.dot(
            picks.astype(jnp.bfloat16), block[:tokens, :], preferred_element_type=jnp.float32
        ).astype(jnp.bfloat16)
        if earlier is not None:
            weights = jnp.sum(picks * gate, axis=1, keepdims=True)
            gates[span, :] = jnp.broadcast_to(weights, (most, gates.shape[1]))

    for swap in range(2):
        side = lax.rem(core + swap, 2)
        for at in range(len(group)):
            gather(at, blocks[2 * at + swap], side)

    powers = []
    for number, (sent, onward) in enumerate(((1, 1), (1, 0), (0, 1), (0, 0))):
        dx, dy = (sent, onward) if local == 0 else (onward, sent)
        piece = 2 * lax.rem(y + dy, 2) + lax.rem(x + dx, 2)
        part = lax.dot_general(
            rows[...],
            weight[local, pl.ds(pl.multiple_of(piece * width, width), width), :],
            (((1,), (1,)), ((), ())),
            preferred_element_type=jnp.float32,
        )
        if earlier is not None:
            there = stored[3][...] if dx and dy else stored[2 * dy + dx][local]
            grad = there.astype(jnp.float32) * part
            grad = jnp.sum(grad, axis=1, keepdims=True)
            grads[...] = grads[...] + grad if number else grad
        if sent:
            code, power = encode(part)
            send[(1 - onward) * total : (2 - onward) * total, :] = code
            powers.append(power)
        else:
            keep[1 - onward] = part
    send[2 * total :, :] = powers_block(powers, width)

    if earlier is not None:
        for out, befores_of in ((mine, befores[0::2]), (theirs, befores[1::2])):
            out[...] = sum((b[...] for b in befores_of), jnp.zeros(out.shape, jnp.float32))
        for at, step in enumerate(group):
            chip = chip_of(z, step)
            for out, side in ((mine, core), (theirs, 1 - core)):
                named, rank, _ = expert_view(info[2 * at + side], expert, top)
                picks = rank_picks(rank, most, (2 * chip + side) * most, cap[local])
                span = pl.ds(pl.multiple_of((2 * at + side) * most, most), most)
                back = jnp.sum(picks * grads[span, :], axis=0, keepdims=True)
                out[chip] = out[chip] + jnp.where(named, back, 0.0)


def partial_share(local, most, top, group, cap, weight, blocks, stored=None, befores=(), after=()):
    tokens, feats = blocks[0].shape[0] - TAIL, blocks[0].shape[1]
    width = weight.shape[1] // 4
    total = 2 * most * len(group)
    tables = (2 * len(group), TAIL, 3 * tokens)
    outs = [like((2 * total + TAIL, width), jnp.int16), like((2, total, width))]
    scratch = [pltpu.VMEM((total, feats), jnp.bfloat16)]
    args = [cap, weight, *blocks]
    if stored is None:
        outs.append(like(tables))
    else:
        outs += [like((total, 128)), like((3, top, tokens)), like((3, top, tokens))]
        scratch += [pltpu.VMEM(tables, jnp.float32), pltpu.VMEM((total, 1), jnp.float32)]
        args += [*stored, *befores]
    earlier = None if stored is None else len(befores)
    return pl.pallas_call(
        functools.partial(share_kernel, local, most, top, group, earlier, len(after)),
        in_specs=[SMEM] + [VMEM] * (len(args) - 1) + [ANY] * len(after),
        out_specs=[VMEM] * len(outs),
        out_shape=outs,
        scratch_shapes=scratch,
        cost_estimate=cost([weight, *blocks], 8 * total * width * feats),
        compiler_params=pltpu.CompilerParams(vmem_limit_bytes=28 * MIB),
        name=f"share_{local}",
    )(*args, *after)


def middle_kernel(got, keep, *refs):
    send, rest = refs[-2:]
    rows, width = rest.shape
    code, power = encode(keep[0] + decode(got, 0, 2))
    send[:rows, :] = code
    send[rows:, :] = powers_block([power], width)
    rest[...] = keep[1] + decode(got, 1, 2)


def middle(got, keep, after=()):
    _, rows, width = keep.shape
    return pl.pallas_call(
        middle_kernel,
        in_specs=[VMEM, VMEM] + [ANY] * len(after),
        out_specs=[VMEM, VMEM],
        out_shape=[like((rows + TAIL, width), jnp.int16), like((rows, width))],
        cost_estimate=cost([got, keep, keep]),
        compiler_params=pltpu.CompilerParams(vmem_limit_bytes=8 * MIB),
        name="middle",
    )(got, keep, *after)


def first_finish_kernel(
    most, top, cap, hidden, info, got0, rest0, got1, rest1, more_mine, more_theirs, out, mine, theirs
):
    z, core, _, _ = place()
    chip = chip_of(z, 0)
    mine[...] = more_mine[...]
    theirs[...] = more_theirs[...]
    for local, (got, rest) in enumerate(((got0, rest0), (got1, rest1))):
        out[local] = rest[...] + decode(got, 0, 1)
        for parts, side in ((mine, core), (theirs, 1 - core)):
            span = pl.ds(pl.multiple_of(side * most, most), most)
            named, rank, gate = expert_view(info[side], (2 * z + core) * 2 + local, top)
            picks = rank_picks(rank, most, (2 * chip + side) * most, cap[local])
            weight = jnp.sum(picks * gate, axis=1, keepdims=True)
            share = out[local, span, :]
            grad = jnp.sum(hidden[local, span, :].astype(jnp.float32) * share, axis=1, keepdims=True)
            out[local, span, :] = weight * share
            back = jnp.sum(picks * grad, axis=0, keepdims=True)
            parts[chip] = parts[chip] + jnp.where(named, back, 0.0)


def first_finish(most, top, cap, hidden, info, sums, parts):
    tokens = info.shape[2] // 3
    return pl.pallas_call(
        functools.partial(first_finish_kernel, most, top),
        in_specs=[SMEM] + [VMEM] * 8,
        out_specs=[VMEM] * 3,
        out_shape=[like(hidden.shape), like((3, top, tokens)), like((3, top, tokens))],
        compiler_params=pltpu.CompilerParams(vmem_limit_bytes=8 * MIB),
        cost_estimate=cost([*sums, hidden]),
        name="first_finish",
    )(cap, hidden, info, *sums, *parts)


def finish_kernel(most, first, got0, rest0, gates0, got1, rest1, gates1, *refs):
    totals, (out, gate_grad) = refs[:-2], refs[-2:]
    gate_grad[...] = sum((total[...] for total in totals[1:]), totals[0][...])
    z = place()[0]
    spans = [pl.ds(pl.multiple_of(chip_of(z, s) * (2 * most), 2 * most), 2 * most) for s in range(3)]
    for local, (got, rest, gates) in enumerate(((got0, rest0, gates0), (got1, rest1, gates1))):
        out[local, spans[0], :] = first[local]
        grad = gates[:, :1] * (rest[...] + decode(got, 0, 1))
        out[local, spans[1], :] = grad[: 2 * most]
        out[local, spans[2], :] = grad[2 * most :]


def finish(most, first, sums, totals):
    experts, rows, width = first.shape
    return pl.pallas_call(
        functools.partial(finish_kernel, most),
        in_specs=[VMEM] * (7 + len(totals)),
        out_specs=[VMEM, VMEM],
        out_shape=[like((experts, 3 * rows, width)), like(totals[0].shape)],
        compiler_params=pltpu.CompilerParams(vmem_limit_bytes=16 * MIB),
        cost_estimate=cost([*sums, first, first]),
        name="finish",
    )(first, *sums, *totals)


def chips_kernel(mine, got, stay, away):
    z = place()[0]
    low, mid, high = (mine[i] + got[i] for i in range(3))
    none = jnp.zeros(low.shape, jnp.float32)
    stay[0] = jnp.where(z < 2, low, high)
    stay[1] = jnp.where(z < 2, mid, none)
    away[0] = jnp.where(z < 2, high, low)
    away[1] = jnp.where(z < 2, none, mid)


def chip_kernel(kept, got, stay, away):
    odd = lax.rem(place()[0], 2) == 1
    even_part, odd_part = (kept[i] + got[i] for i in range(2))
    stay[...] = jnp.where(odd, odd_part, even_part)
    away[...] = jnp.where(odd, even_part, odd_part)


def add_kernel(*refs):
    total = refs[0][...]
    for ref in refs[1:-1]:
        total = total + ref[...]
    refs[-1][...] = total


def small(kernel, outs, *args, after=()):
    used = len(args)
    return pl.pallas_call(
        lambda *refs: kernel(*refs[:used], *refs[used + len(after) :]),
        in_specs=[VMEM] * used + [ANY] * len(after),
        out_specs=[VMEM] * len(outs),
        out_shape=outs,
        compiler_params=pltpu.CompilerParams(vmem_limit_bytes=2 * MIB),
        cost_estimate=cost(args),
        name=kernel.__name__,
    )(*args, *after)


def blockwise(most, grad_out, routes, slots, gates, capacity, hidden, down_weight):
    peers, ranks = lax.axis_size("expert"), lax.axis_size("dp")
    tokens, top = routes.shape

    def along(rows, pairs):
        return lax.ppermute(rows, "expert", [(2 * a + c, 2 * b + c) for a, b in pairs for c in range(2)])

    def across(rows):
        return lax.ppermute(rows, "expert", [(i, i ^ 1) for i in range(peers)])

    def over(rows, flip):
        return lax.ppermute(rows, "dp", [(i, i ^ flip) for i in range(ranks)])

    block, first_hidden, other_hidden = prepare(most, grad_out, routes, slots, gates, hidden)
    up1 = along(block, [(0, 1), (1, 2), (2, 3)])
    down1 = along(block, [(2, 1), (1, 0)])
    stored = [other_hidden, over(other_hidden, 1), over(other_hidden, 2)]
    *passed, again = take(stored[1], stored[2], block)
    far_stored = [over(passed[0], 2), over(passed[1], 1)]
    weight = load(block, down_weight)

    (first,) = pick(((0, 0, 0, 1),), (block, up1), (weight, down1))
    up2 = along(up1, [(1, 2), (2, 3)])
    down2 = along(again, [(2, 0)])
    pair = (first, across(first))
    sent, kept = [], []
    for local in range(2):
        send, keep, info = partial_share(
            local, most, top, (0,), capacity, weight, pair, after=far_stored[:1] if local else ()
        )
        sent.append(send)
        kept.append(keep)

    up3 = along(up2, [(2, 3)])
    (second,) = pick(((2, 0, 0, 1),), (up1, up2, down1), (*sent, *far_stored))
    blocks = [second, across(second)]

    sums, onward = [], []
    for local in range(2):
        send, rest = middle(over(sent[local], 1 + local), kept[local])
        onward.append(send)
        sums += [over(send, 2 - local), rest]
    (third,) = pick(((0, 1, 2, 3),), (down2, down1, up2, up3), ())
    blocks += [third, across(third)]

    halves = []
    before = []
    for local in range(2):
        send, keep, gate, *before = partial_share(
            local, most, top, (1, 2), capacity, weight, blocks, [*stored, far_stored[local]], before,
            (sums[0], sums[2]) if local else onward,
        )
        halves.append((over(send, 1 + local), keep, gate))
    first_grad, mine, theirs = first_finish(most, top, capacity, first_hidden, info, sums, before)

    one = like((top, tokens))
    two = like((2, top, tokens))
    (got0, keep0, gate0), (got1, keep1, gate1) = halves
    stay, away = small(chips_kernel, [two, two], mine, across(theirs))
    came = along(away, [(z, z ^ 2) for z in range(peers // 2)])
    stay, away = small(chip_kernel, [one, one], stay, came)
    send0, rest0 = middle(got0, keep0, (away,))
    (total,) = small(
        add_kernel, [one], stay, along(away, [(z, z ^ 1) for z in range(peers // 2)]), after=(send0,)
    )
    whole = [total] + [over(total, flip) for flip in range(1, ranks)]
    send1, rest1 = middle(got1, keep1, (total,))
    sums = [over(send0, 2), rest0, gate0, over(send1, 1), rest1, gate1]
    hidden_grad, gate_grad = finish(most, first_grad, sums, whole)
    return hidden_grad, gate_grad.T


def solution(mesh):
    peers, ranks = mesh.shape["expert"], mesh.shape["dp"]

    def shards(grad_out, routes, slots, gates, capacity, hidden, down_weight):
        tokens, top = routes.shape
        experts = down_weight.shape[0] * peers
        most = top * max(2, (tokens + experts - 1) // experts)
        full = most * experts == tokens * top
        fits = peers == 8 and hidden.shape[1] == 6 * most and 3 * tokens <= grad_out.shape[1]
        square = ranks == 4 and down_weight.shape[0] == 2 and experts <= 256 and most <= 256
        if full and fits and square:
            return blockwise(most, grad_out, routes, slots, gates, capacity, hidden, down_weight)
        return general(grad_out, routes, slots, gates, capacity, hidden, down_weight)

    placed = (
        P("expert", "dp"),
        P("expert", None),
        P("expert", None),
        P("expert", None),
        P("expert"),
        P("expert", None, "dp"),
        P("expert", None, "dp"),
    )
    return jax.shard_map(
        shards,
        mesh=mesh,
        in_specs=placed,
        out_specs=(P("expert", None, "dp"), P("expert", None)),
        check_vma=False,
    )
```

```python
import functools
import math

import jax
import jax.numpy as jnp
from jax import lax
from jax.experimental import pallas as pl
from jax.experimental.pallas import tpu as pltpu
from jax.sharding import PartitionSpec as P

STEPS = 32766.0
TAIL = 16
VMEM = pl.BlockSpec(memory_space=pltpu.VMEM)
ANY = pl.BlockSpec(memory_space=pl.ANY)
SMEM = pl.BlockSpec(memory_space=pltpu.SMEM)


def local_ranks(route_grid, expert_total):
    onehot = (route_grid[..., None] == jnp.arange(expert_total, dtype=jnp.int32)).astype(jnp.int32)
    before = jnp.cumsum(onehot, axis=-2) - onehot
    return jnp.sum(before * onehot, axis=-1)


def capacity_of(local_expert, capacity):
    picks = local_expert[..., None] == jnp.arange(capacity.shape[0], dtype=jnp.int32)
    return jnp.sum(jnp.where(picks, capacity, 0), axis=-1)


def general(grad_out, routes, slots, gates, capacity, hidden, down_weight):
    peer_count = lax.axis_size("expert")
    experts_here = down_weight.shape[0]
    slot_count = hidden.shape[1]
    tok_rows, top_count = routes.shape
    feature_width = grad_out.shape[1]
    expert_total = experts_here * peer_count
    most_rows = top_count * max(2, (tok_rows + expert_total - 1) // expert_total)
    slot_total = experts_here * slot_count
    route_flat = routes.reshape(-1)
    slot_flat = slots.reshape(-1)
    dest_pos = route_flat * most_rows + local_ranks(route_flat, expert_total)
    send_rows = (
        jnp.zeros((expert_total * most_rows, feature_width), jnp.bfloat16)
        .at[dest_pos]
        .set(jnp.repeat(grad_out, top_count, axis=0))
    )
    send_gate = (
        jnp.zeros((expert_total * most_rows,), jnp.bfloat16).at[dest_pos].set(gates.reshape(-1))
    )
    send_slot = (
        jnp.full((expert_total * most_rows,), slot_count, jnp.int32).at[dest_pos].set(slot_flat)
    )
    exchange = functools.partial(
        lax.all_to_all, axis_name="expert", split_axis=0, concat_axis=0, tiled=True
    )
    recv_rows = exchange(send_rows.reshape(peer_count, experts_here * most_rows, feature_width))
    recv_gate = exchange(send_gate.reshape(peer_count, experts_here * most_rows))
    recv_slot = exchange(send_slot.reshape(peer_count, experts_here * most_rows))
    local_expert = jnp.broadcast_to(
        (jnp.arange(experts_here * most_rows, dtype=jnp.int32) // most_rows)[None, :],
        recv_slot.shape,
    )
    usable = recv_slot < capacity_of(local_expert, capacity)
    slot_table = jnp.where(usable, local_expert * slot_count + recv_slot, slot_total).reshape(-1)
    slot_rows = (
        jnp.zeros((slot_total, feature_width), jnp.bfloat16)
        .at[slot_table]
        .set(recv_rows.reshape(-1, feature_width), mode="drop")
    )
    slot_gate = (
        jnp.zeros((slot_total,), jnp.bfloat16)
        .at[slot_table]
        .set(recv_gate.reshape(-1), mode="drop")
    )
    slot_blocks = slot_rows.reshape(experts_here, slot_count, feature_width)
    share_rows = lax.psum_scatter(
        jnp.einsum("efd,ecd->fec", down_weight, slot_blocks, preferred_element_type=jnp.float32),
        "dp",
        scatter_dimension=0,
        tiled=True,
    )
    hidden_share = jnp.transpose(share_rows, (1, 2, 0))
    hidden_grad = (
        slot_gate.reshape(experts_here, slot_count)[..., None].astype(jnp.float32) * hidden_share
    )
    partial_grad = jnp.sum(hidden.astype(jnp.float32) * hidden_share, axis=-1)
    slot_grad = lax.psum(partial_grad, "dp").reshape(-1)
    picked = slot_grad[jnp.minimum(slot_table, slot_total - 1)]
    outgoing = jnp.where(slot_table < slot_total, picked, jnp.float32(0.0)).reshape(
        peer_count, experts_here * most_rows
    )
    incoming = exchange(outgoing).reshape(-1)
    gate_grad = incoming[dest_pos].reshape(tok_rows, top_count)
    return hidden_grad, gate_grad


ORDER = ((0, 1, 2), (1, 0, 2), (2, 1, 0), (2, 1, 0))
MIB = 2**20


def cost(shapes, flops=0):
    size = sum(math.prod(a.shape) * a.dtype.itemsize for a in shapes)
    return pl.CostEstimate(flops=flops, bytes_accessed=size, transcendentals=0)


def hbm(array):
    return pltpu.with_memory_space_constraint(array, pltpu.HBM)


def like(shape, kind=jnp.float32):
    return jax.ShapeDtypeStruct(shape, kind)


def place():
    me, rank = lax.axis_index("expert"), lax.axis_index("dp")
    return me // 2, lax.rem(me, 2), lax.rem(rank, 2), rank // 2


def chip_of(z, step):
    chip = jnp.int32(ORDER[0][step])
    for at_z in range(1, len(ORDER)):
        chip = jnp.where(z == at_z, ORDER[at_z][step], chip)
    return chip


def encode(values):
    peak = jnp.maximum(jnp.max(jnp.abs(values), keepdims=True), 1e-30)
    power = jnp.floor(jnp.log2(peak)) + 1.0
    scaled = values * (jnp.exp2(-power) * (STEPS * STEPS))
    code = jnp.round(scaled * lax.rsqrt(jnp.abs(scaled) + 1e-20))
    return code.astype(jnp.int32).astype(jnp.int16), power


def powers_block(powers, width):
    spans = [jnp.broadcast_to(power, (TAIL, width // len(powers))) for power in powers]
    return jnp.concatenate(spans, axis=1).astype(jnp.int32).astype(jnp.int16)


def decode(coded, part, parts):
    rows = (coded.shape[0] - TAIL) // parts
    lane = part * (coded.shape[1] // parts)
    power = coded[parts * rows :, lane : lane + 128].astype(jnp.int32).astype(jnp.float32)
    code = coded[part * rows : (part + 1) * rows, :].astype(jnp.int32).astype(jnp.float32)
    scale = jnp.exp2(jnp.max(power, keepdims=True)) * (1.0 / (STEPS * STEPS))
    return code * jnp.abs(code) * scale


def prepare_kernel(
    most, rows, routes, slots, gates, hidden, out, first, others, routes_in, slots_in, gates_in, sem
):
    tokens, top = rows.shape[0], routes.shape[0]
    z, core, _, _ = place()
    pairs = [(routes, routes_in), (slots, slots_in), (gates, gates_in), (rows, out.at[:tokens])]
    for step in range(3):
        start = pl.multiple_of(chip_of(z, step) * (2 * most), 2 * most)
        for local in range(2):
            span = others.at[local, 2 * most * (step - 1) : 2 * most * step] if step else first.at[local]
            pairs.append((hidden.at[local, pl.ds(start, 2 * most)], span))
    copies = [pltpu.make_async_copy(a, b, sem.at[i]) for i, (a, b) in enumerate(pairs)]
    for copy in copies:
        copy.start()
    for copy in copies[:3]:
        copy.wait()
    rank = slots_in[...] - (2 * z + core) * most
    parts = [routes_in[...], rank, gates_in[...]]
    packed = jnp.concatenate([part.astype(jnp.float32) for part in parts], axis=1)
    packed = jnp.concatenate([packed, jnp.zeros((TAIL - top, 3 * tokens), jnp.float32)], axis=0)
    out[tokens:, : 3 * tokens] = packed.astype(jnp.bfloat16)
    out[tokens:, 3 * tokens :] = jnp.zeros((TAIL, out.shape[1] - 3 * tokens), jnp.bfloat16)
    for copy in copies[3:]:
        copy.wait()


def prepare(most, grad_out, routes, slots, gates, hidden):
    tokens, feats = grad_out.shape
    top = routes.shape[1]
    experts, _, width = hidden.shape
    return pl.pallas_call(
        functools.partial(prepare_kernel, most),
        in_specs=[ANY] * 5,
        out_specs=[VMEM] * 3,
        out_shape=[
            like((tokens + TAIL, feats), jnp.bfloat16),
            like((experts, 2 * most, width), jnp.bfloat16),
            like((experts, 4 * most, width), jnp.bfloat16),
        ],
        scratch_shapes=[
            pltpu.VMEM((top, tokens), jnp.int32),
            pltpu.VMEM((top, tokens), jnp.int32),
            pltpu.VMEM((top, tokens), jnp.bfloat16),
            pltpu.SemaphoreType.DMA((10,)),
        ],
        compiler_params=pltpu.CompilerParams(vmem_limit_bytes=8 * MIB),
        cost_estimate=cost([grad_out, grad_out, hidden]),
        name="prepare",
    )(*(hbm(a) for a in (grad_out, routes.T, slots.T, gates.T, hidden)))


def load_kernel(after, weight, out, sem):
    copy = pltpu.make_async_copy(weight, out, sem)
    copy.start()
    copy.wait()


def load(after, weight):
    return pl.pallas_call(
        load_kernel,
        in_specs=[ANY, ANY],
        out_specs=VMEM,
        out_shape=like(weight.shape, weight.dtype),
        scratch_shapes=[pltpu.SemaphoreType.DMA],
        cost_estimate=cost([weight, weight]),
        compiler_params=pltpu.CompilerParams(vmem_limit_bytes=16 * MIB),
        name="load_weight",
    )(after, hbm(weight))


def pick_kernel(rules, count, *refs):
    sem = refs[-1]
    outs = refs[-1 - len(rules) : -1]
    z = place()[0]
    for number, rule in enumerate(rules):
        for source in sorted(set(rule)):
            wanted = functools.reduce(
                jnp.logical_or, [z == at_z for at_z in range(len(rule)) if rule[at_z] == source]
            )

            @pl.when(wanted)
            def _(source=source, number=number):
                pltpu.make_async_copy(refs[source], outs[number], sem.at[number]).start()

    for number in range(len(rules)):
        pltpu.make_async_copy(refs[0], outs[number], sem.at[number]).wait()


def pick(rules, blocks, after):
    return pl.pallas_call(
        functools.partial(pick_kernel, rules, len(blocks)),
        in_specs=[VMEM] * len(blocks) + [ANY] * len(after),
        out_specs=[VMEM] * len(rules),
        out_shape=[like(blocks[0].shape, blocks[0].dtype)] * len(rules),
        scratch_shapes=[pltpu.SemaphoreType.DMA((len(rules),))],
        compiler_params=pltpu.CompilerParams(vmem_limit_bytes=8 * MIB),
        cost_estimate=cost(blocks),
        name="pick",
    )(*blocks, *after)


def take_kernel(over_x, over_y, block, one, other, again, sem):
    copies = [
        pltpu.make_async_copy(over_x.at[0], one, sem.at[0]),
        pltpu.make_async_copy(over_y.at[1], other, sem.at[1]),
        pltpu.make_async_copy(block, again, sem.at[2]),
    ]
    for copy in copies:
        copy.start()
    for copy in copies:
        copy.wait()


def take(over_x, over_y, block):
    out = like(over_x.shape[1:], over_x.dtype)
    return pl.pallas_call(
        take_kernel,
        in_specs=[VMEM] * 3,
        out_specs=[VMEM] * 3,
        out_shape=[out, out, like(block.shape, block.dtype)],
        scratch_shapes=[pltpu.SemaphoreType.DMA((3,))],
        compiler_params=pltpu.CompilerParams(vmem_limit_bytes=8 * MIB),
        cost_estimate=cost([out, out]),
        name="take",
    )(over_x, over_y, block)


def expert_view(info, expert, top):
    tokens = info.shape[1] // 3
    at = info[:top, :tokens] == expert.astype(jnp.float32)
    rank = jnp.sum(jnp.where(at, info[:top, tokens : 2 * tokens] + 1.0, 0.0), axis=0, keepdims=True) - 1.0
    gate = jnp.sum(jnp.where(at, info[:top, 2 * tokens :], 0.0), axis=0, keepdims=True)
    return at, rank, gate


def rank_picks(rank, count, first, limit):
    numbers = lax.broadcasted_iota(jnp.int32, (count, rank.shape[1]), 0)
    hit = (numbers.astype(jnp.float32) == rank) & (first + numbers < limit)
    return jnp.where(hit, 1.0, 0.0)


def share_kernel(local, most, top, group, earlier, waits, cap, weight, *refs):
    blocks, refs = refs[: 2 * len(group)], refs[2 * len(group) :]
    if earlier is None:
        send, keep, info, rows = refs[waits:]
    else:
        stored, befores = refs[:4], refs[4 : 4 + earlier]
        send, keep, gates, mine, theirs, rows, info, grads = refs[4 + earlier + waits :]
    z, core, x, y = place()
    tokens = blocks[0].shape[0] - TAIL
    total, width = keep.shape[1], keep.shape[2]
    expert = (2 * z + core) * 2 + local

    def gather(at, block, side):
        table = block[tokens:, : 3 * tokens].astype(jnp.float32)
        info[2 * at + side] = table
        _, rank, gate = expert_view(table, expert, top)
        first = (2 * chip_of(z, group[at]) + side) * most
        picks = rank_picks(rank, most, first, cap[local])
        span = pl.ds(pl.multiple_of((2 * at + side) * most, most), most)
        rows[span, :] = jnp.dot(
            picks.astype(jnp.bfloat16), block[:tokens, :], preferred_element_type=jnp.float32
        ).astype(jnp.bfloat16)
        if earlier is not None:
            weights = jnp.sum(picks * gate, axis=1, keepdims=True)
            gates[span, :] = jnp.broadcast_to(weights, (most, gates.shape[1]))

    for swap in range(2):
        side = lax.rem(core + swap, 2)
        for at in range(len(group)):
            gather(at, blocks[2 * at + swap], side)

    powers = []
    for number, (sent, onward) in enumerate(((1, 1), (1, 0), (0, 1), (0, 0))):
        dx, dy = (sent, onward) if local == 0 else (onward, sent)
        piece = 2 * lax.rem(y + dy, 2) + lax.rem(x + dx, 2)
        part = lax.dot_general(
            rows[...],
            weight[local, pl.ds(pl.multiple_of(piece * width, width), width), :],
            (((1,), (1,)), ((), ())),
            preferred_element_type=jnp.float32,
        )
        if earlier is not None:
            there = stored[3][...] if dx and dy else stored[2 * dy + dx][local]
            grad = there.astype(jnp.float32) * part
            grad = jnp.sum(grad, axis=1, keepdims=True)
            grads[...] = grads[...] + grad if number else grad
        if sent:
            code, power = encode(part)
            send[(1 - onward) * total : (2 - onward) * total, :] = code
            powers.append(power)
        else:
            keep[1 - onward] = part
    send[2 * total :, :] = powers_block(powers, width)

    if earlier is not None:
        for out, befores_of in ((mine, befores[0::2]), (theirs, befores[1::2])):
            out[...] = sum((b[...] for b in befores_of), jnp.zeros(out.shape, jnp.float32))
        for at, step in enumerate(group):
            chip = chip_of(z, step)
            for out, side in ((mine, core), (theirs, 1 - core)):
                named, rank, _ = expert_view(info[2 * at + side], expert, top)
                picks = rank_picks(rank, most, (2 * chip + side) * most, cap[local])
                span = pl.ds(pl.multiple_of((2 * at + side) * most, most), most)
                back = jnp.sum(picks * grads[span, :], axis=0, keepdims=True)
                out[chip] = out[chip] + jnp.where(named, back, 0.0)


def partial_share(local, most, top, group, cap, weight, blocks, stored=None, befores=(), after=()):
    tokens, feats = blocks[0].shape[0] - TAIL, blocks[0].shape[1]
    width = weight.shape[1] // 4
    total = 2 * most * len(group)
    tables = (2 * len(group), TAIL, 3 * tokens)
    outs = [like((2 * total + TAIL, width), jnp.int16), like((2, total, width))]
    scratch = [pltpu.VMEM((total, feats), jnp.bfloat16)]
    args = [cap, weight, *blocks]
    if stored is None:
        outs.append(like(tables))
    else:
        outs += [like((total, 128)), like((3, top, tokens)), like((3, top, tokens))]
        scratch += [pltpu.VMEM(tables, jnp.float32), pltpu.VMEM((total, 1), jnp.float32)]
        args += [*stored, *befores]
    earlier = None if stored is None else len(befores)
    return pl.pallas_call(
        functools.partial(share_kernel, local, most, top, group, earlier, len(after)),
        in_specs=[SMEM] + [VMEM] * (len(args) - 1) + [ANY] * len(after),
        out_specs=[VMEM] * len(outs),
        out_shape=outs,
        scratch_shapes=scratch,
        cost_estimate=cost([weight, *blocks], 8 * total * width * feats),
        compiler_params=pltpu.CompilerParams(vmem_limit_bytes=28 * MIB),
        name=f"share_{local}",
    )(*args, *after)


def middle_kernel(got, keep, *refs):
    send, rest = refs[-2:]
    rows, width = rest.shape
    code, power = encode(keep[0] + decode(got, 0, 2))
    send[:rows, :] = code
    send[rows:, :] = powers_block([power], width)
    rest[...] = keep[1] + decode(got, 1, 2)


def middle(got, keep, after=()):
    _, rows, width = keep.shape
    return pl.pallas_call(
        middle_kernel,
        in_specs=[VMEM, VMEM] + [ANY] * len(after),
        out_specs=[VMEM, VMEM],
        out_shape=[like((rows + TAIL, width), jnp.int16), like((rows, width))],
        cost_estimate=cost([got, keep, keep]),
        compiler_params=pltpu.CompilerParams(vmem_limit_bytes=8 * MIB),
        name="middle",
    )(got, keep, *after)


def first_finish_kernel(
    most, top, cap, hidden, info, got0, rest0, got1, rest1, more_mine, more_theirs, out, mine, theirs
):
    z, core, _, _ = place()
    chip = chip_of(z, 0)
    mine[...] = more_mine[...]
    theirs[...] = more_theirs[...]
    for local, (got, rest) in enumerate(((got0, rest0), (got1, rest1))):
        out[local] = rest[...] + decode(got, 0, 1)
        for parts, side in ((mine, core), (theirs, 1 - core)):
            span = pl.ds(pl.multiple_of(side * most, most), most)
            named, rank, gate = expert_view(info[side], (2 * z + core) * 2 + local, top)
            picks = rank_picks(rank, most, (2 * chip + side) * most, cap[local])
            weight = jnp.sum(picks * gate, axis=1, keepdims=True)
            share = out[local, span, :]
            grad = jnp.sum(hidden[local, span, :].astype(jnp.float32) * share, axis=1, keepdims=True)
            out[local, span, :] = weight * share
            back = jnp.sum(picks * grad, axis=0, keepdims=True)
            parts[chip] = parts[chip] + jnp.where(named, back, 0.0)


def first_finish(most, top, cap, hidden, info, sums, parts):
    tokens = info.shape[2] // 3
    return pl.pallas_call(
        functools.partial(first_finish_kernel, most, top),
        in_specs=[SMEM] + [VMEM] * 8,
        out_specs=[VMEM] * 3,
        out_shape=[like(hidden.shape), like((3, top, tokens)), like((3, top, tokens))],
        compiler_params=pltpu.CompilerParams(vmem_limit_bytes=8 * MIB),
        cost_estimate=cost([*sums, hidden]),
        name="first_finish",
    )(cap, hidden, info, *sums, *parts)


def finish_kernel(most, first, got0, rest0, gates0, got1, rest1, gates1, *refs):
    totals, (out, gate_grad) = refs[:-2], refs[-2:]
    gate_grad[...] = sum((total[...] for total in totals[1:]), totals[0][...])
    z = place()[0]
    spans = [pl.ds(pl.multiple_of(chip_of(z, s) * (2 * most), 2 * most), 2 * most) for s in range(3)]
    for local, (got, rest, gates) in enumerate(((got0, rest0, gates0), (got1, rest1, gates1))):
        out[local, spans[0], :] = first[local]
        grad = gates[:, :1] * (rest[...] + decode(got, 0, 1))
        out[local, spans[1], :] = grad[: 2 * most]
        out[local, spans[2], :] = grad[2 * most :]


def finish(most, first, sums, totals):
    experts, rows, width = first.shape
    return pl.pallas_call(
        functools.partial(finish_kernel, most),
        in_specs=[VMEM] * (7 + len(totals)),
        out_specs=[VMEM, VMEM],
        out_shape=[like((experts, 3 * rows, width)), like(totals[0].shape)],
        compiler_params=pltpu.CompilerParams(vmem_limit_bytes=16 * MIB),
        cost_estimate=cost([*sums, first, first]),
        name="finish",
    )(first, *sums, *totals)


def chips_kernel(mine, got, stay, away):
    z = place()[0]
    low, mid, high = (mine[i] + got[i] for i in range(3))
    none = jnp.zeros(low.shape, jnp.float32)
    stay[0] = jnp.where(z < 2, low, high)
    stay[1] = jnp.where(z < 2, mid, none)
    away[0] = jnp.where(z < 2, high, low)
    away[1] = jnp.where(z < 2, none, mid)


def chip_kernel(kept, got, stay, away):
    odd = lax.rem(place()[0], 2) == 1
    even_part, odd_part = (kept[i] + got[i] for i in range(2))
    stay[...] = jnp.where(odd, odd_part, even_part)
    away[...] = jnp.where(odd, even_part, odd_part)


def add_kernel(*refs):
    total = refs[0][...]
    for ref in refs[1:-1]:
        total = total + ref[...]
    refs[-1][...] = total


def small(kernel, outs, *args, after=()):
    used = len(args)
    return pl.pallas_call(
        lambda *refs: kernel(*refs[:used], *refs[used + len(after) :]),
        in_specs=[VMEM] * used + [ANY] * len(after),
        out_specs=[VMEM] * len(outs),
        out_shape=outs,
        compiler_params=pltpu.CompilerParams(vmem_limit_bytes=2 * MIB),
        cost_estimate=cost(args),
        name=kernel.__name__,
    )(*args, *after)


def blockwise(most, grad_out, routes, slots, gates, capacity, hidden, down_weight):
    peers, ranks = lax.axis_size("expert"), lax.axis_size("dp")
    tokens, top = routes.shape

    def along(rows, pairs):
        return lax.ppermute(rows, "expert", [(2 * a + c, 2 * b + c) for a, b in pairs for c in range(2)])

    def across(rows):
        return lax.ppermute(rows, "expert", [(i, i ^ 1) for i in range(peers)])

    def over(rows, flip):
        return lax.ppermute(rows, "dp", [(i, i ^ flip) for i in range(ranks)])

    block, first_hidden, other_hidden = prepare(most, grad_out, routes, slots, gates, hidden)
    up1 = along(block, [(0, 1), (1, 2), (2, 3)])
    down1 = along(block, [(2, 1), (1, 0)])
    stored = [other_hidden, over(other_hidden, 1), over(other_hidden, 2)]
    *passed, again = take(stored[1], stored[2], block)
    far_stored = [over(passed[0], 2), over(passed[1], 1)]
    weight = load(block, down_weight)

    (first,) = pick(((0, 0, 0, 1),), (block, up1), (weight, down1))
    up2 = along(up1, [(1, 2), (2, 3)])
    down2 = along(again, [(2, 0)])
    pair = (first, across(first))
    sent, kept = [], []
    for local in range(2):
        send, keep, info = partial_share(
            local, most, top, (0,), capacity, weight, pair, after=far_stored[:1] if local else ()
        )
        sent.append(send)
        kept.append(keep)

    up3 = along(up2, [(2, 3)])
    (second,) = pick(((2, 0, 0, 1),), (up1, up2, down1), (*sent, *far_stored))
    blocks = [second, across(second)]

    sums, onward = [], []
    for local in range(2):
        send, rest = middle(over(sent[local], 1 + local), kept[local])
        onward.append(send)
        sums += [over(send, 2 - local), rest]
    (third,) = pick(((0, 1, 2, 3),), (down2, down1, up2, up3), ())
    blocks += [third, across(third)]

    halves = [None, None]
    before = []
    for local in (1, 0):
        send, keep, gate, *before = partial_share(
            local, most, top, (1, 2), capacity, weight, blocks, [*stored, far_stored[local]], before,
            onward if local else (sums[0], sums[2]),
        )
        halves[local] = (over(send, 1 + local), keep, gate)
    first_grad, mine, theirs = first_finish(most, top, capacity, first_hidden, info, sums, before)

    one = like((top, tokens))
    two = like((2, top, tokens))
    (got0, keep0, gate0), (got1, keep1, gate1) = halves
    stay, away = small(chips_kernel, [two, two], mine, across(theirs))
    came = along(away, [(z, z ^ 2) for z in range(peers // 2)])
    stay, away = small(chip_kernel, [one, one], stay, came)
    send1, rest1 = middle(got1, keep1, (away,))
    (total,) = small(
        add_kernel, [one], stay, along(away, [(z, z ^ 1) for z in range(peers // 2)]), after=(send1,)
    )
    whole = [total] + [over(total, flip) for flip in range(1, ranks)]
    send0, rest0 = middle(got0, keep0, (total,))
    sums = [over(send0, 2), rest0, gate0, over(send1, 1), rest1, gate1]
    hidden_grad, gate_grad = finish(most, first_grad, sums, whole)
    return hidden_grad, gate_grad.T


def solution(mesh):
    peers, ranks = mesh.shape["expert"], mesh.shape["dp"]

    def shards(grad_out, routes, slots, gates, capacity, hidden, down_weight):
        tokens, top = routes.shape
        experts = down_weight.shape[0] * peers
        most = top * max(2, (tokens + experts - 1) // experts)
        full = most * experts == tokens * top
        fits = peers == 8 and hidden.shape[1] == 6 * most and 3 * tokens <= grad_out.shape[1]
        square = ranks == 4 and down_weight.shape[0] == 2 and experts <= 256 and most <= 256
        if full and fits and square:
            return blockwise(most, grad_out, routes, slots, gates, capacity, hidden, down_weight)
        return general(grad_out, routes, slots, gates, capacity, hidden, down_weight)

    placed = (
        P("expert", "dp"),
        P("expert", None),
        P("expert", None),
        P("expert", None),
        P("expert"),
        P("expert", None, "dp"),
        P("expert", None, "dp"),
    )
    return jax.shard_map(
        shards,
        mesh=mesh,
        in_specs=placed,
        out_specs=(P("expert", None, "dp"), P("expert", None)),
        check_vma=False,
    )
```

```python
import functools
import math

import jax
import jax.numpy as jnp
from jax import lax
from jax.experimental import pallas as pl
from jax.experimental.pallas import tpu as pltpu
from jax.sharding import PartitionSpec as P

STEPS = 32766.0
TAIL = 16
VMEM = pl.BlockSpec(memory_space=pltpu.VMEM)
ANY = pl.BlockSpec(memory_space=pl.ANY)
SMEM = pl.BlockSpec(memory_space=pltpu.SMEM)


def local_ranks(route_grid, expert_total):
    onehot = (route_grid[..., None] == jnp.arange(expert_total, dtype=jnp.int32)).astype(jnp.int32)
    before = jnp.cumsum(onehot, axis=-2) - onehot
    return jnp.sum(before * onehot, axis=-1)


def capacity_of(local_expert, capacity):
    picks = local_expert[..., None] == jnp.arange(capacity.shape[0], dtype=jnp.int32)
    return jnp.sum(jnp.where(picks, capacity, 0), axis=-1)


def general(grad_out, routes, slots, gates, capacity, hidden, down_weight):
    peer_count = lax.axis_size("expert")
    experts_here = down_weight.shape[0]
    slot_count = hidden.shape[1]
    tok_rows, top_count = routes.shape
    feature_width = grad_out.shape[1]
    expert_total = experts_here * peer_count
    most_rows = top_count * max(2, (tok_rows + expert_total - 1) // expert_total)
    slot_total = experts_here * slot_count
    route_flat = routes.reshape(-1)
    slot_flat = slots.reshape(-1)
    dest_pos = route_flat * most_rows + local_ranks(route_flat, expert_total)
    send_rows = (
        jnp.zeros((expert_total * most_rows, feature_width), jnp.bfloat16)
        .at[dest_pos]
        .set(jnp.repeat(grad_out, top_count, axis=0))
    )
    send_gate = (
        jnp.zeros((expert_total * most_rows,), jnp.bfloat16).at[dest_pos].set(gates.reshape(-1))
    )
    send_slot = (
        jnp.full((expert_total * most_rows,), slot_count, jnp.int32).at[dest_pos].set(slot_flat)
    )
    exchange = functools.partial(
        lax.all_to_all, axis_name="expert", split_axis=0, concat_axis=0, tiled=True
    )
    recv_rows = exchange(send_rows.reshape(peer_count, experts_here * most_rows, feature_width))
    recv_gate = exchange(send_gate.reshape(peer_count, experts_here * most_rows))
    recv_slot = exchange(send_slot.reshape(peer_count, experts_here * most_rows))
    local_expert = jnp.broadcast_to(
        (jnp.arange(experts_here * most_rows, dtype=jnp.int32) // most_rows)[None, :],
        recv_slot.shape,
    )
    usable = recv_slot < capacity_of(local_expert, capacity)
    slot_table = jnp.where(usable, local_expert * slot_count + recv_slot, slot_total).reshape(-1)
    slot_rows = (
        jnp.zeros((slot_total, feature_width), jnp.bfloat16)
        .at[slot_table]
        .set(recv_rows.reshape(-1, feature_width), mode="drop")
    )
    slot_gate = (
        jnp.zeros((slot_total,), jnp.bfloat16)
        .at[slot_table]
        .set(recv_gate.reshape(-1), mode="drop")
    )
    slot_blocks = slot_rows.reshape(experts_here, slot_count, feature_width)
    share_rows = lax.psum_scatter(
        jnp.einsum("efd,ecd->fec", down_weight, slot_blocks, preferred_element_type=jnp.float32),
        "dp",
        scatter_dimension=0,
        tiled=True,
    )
    hidden_share = jnp.transpose(share_rows, (1, 2, 0))
    hidden_grad = (
        slot_gate.reshape(experts_here, slot_count)[..., None].astype(jnp.float32) * hidden_share
    )
    partial_grad = jnp.sum(hidden.astype(jnp.float32) * hidden_share, axis=-1)
    slot_grad = lax.psum(partial_grad, "dp").reshape(-1)
    picked = slot_grad[jnp.minimum(slot_table, slot_total - 1)]
    outgoing = jnp.where(slot_table < slot_total, picked, jnp.float32(0.0)).reshape(
        peer_count, experts_here * most_rows
    )
    incoming = exchange(outgoing).reshape(-1)
    gate_grad = incoming[dest_pos].reshape(tok_rows, top_count)
    return hidden_grad, gate_grad


ORDER = ((0, 1, 2), (1, 0, 2), (2, 1, 0), (2, 1, 0))
MIB = 2**20


def cost(shapes, flops=0):
    size = sum(math.prod(a.shape) * a.dtype.itemsize for a in shapes)
    return pl.CostEstimate(flops=flops, bytes_accessed=size, transcendentals=0)


def hbm(array):
    return pltpu.with_memory_space_constraint(array, pltpu.HBM)


def like(shape, kind=jnp.float32):
    return jax.ShapeDtypeStruct(shape, kind)


def place():
    me, rank = lax.axis_index("expert"), lax.axis_index("dp")
    return me // 2, lax.rem(me, 2), lax.rem(rank, 2), rank // 2


def chip_of(z, step):
    chip = jnp.int32(ORDER[0][step])
    for at_z in range(1, len(ORDER)):
        chip = jnp.where(z == at_z, ORDER[at_z][step], chip)
    return chip


def encode(values):
    peak = jnp.maximum(jnp.max(jnp.abs(values), keepdims=True), 1e-30)
    power = jnp.floor(jnp.log2(peak)) + 1.0
    scaled = (values * jnp.exp2(-power)) * (STEPS * STEPS)
    code = jnp.round(scaled * lax.rsqrt(jnp.abs(scaled) + 1e-20))
    return code.astype(jnp.int32).astype(jnp.int16), power


def powers_block(powers, width):
    spans = [jnp.broadcast_to(power, (TAIL, width // len(powers))) for power in powers]
    return jnp.concatenate(spans, axis=1).astype(jnp.int32).astype(jnp.int16)


def decode(coded, part, parts):
    rows = (coded.shape[0] - TAIL) // parts
    lane = part * (coded.shape[1] // parts)
    power = coded[parts * rows :, lane : lane + 128].astype(jnp.int32).astype(jnp.float32)
    code = coded[part * rows : (part + 1) * rows, :].astype(jnp.int32).astype(jnp.float32)
    scale = jnp.exp2(jnp.max(power, keepdims=True))
    return (code * jnp.abs(code) * (1.0 / (STEPS * STEPS))) * scale


def prepare_kernel(
    most, rows, routes, slots, gates, hidden, out, first, others, routes_in, slots_in, gates_in, sem
):
    tokens, top = rows.shape[0], routes.shape[0]
    z, core, _, _ = place()
    pairs = [(routes, routes_in), (slots, slots_in), (gates, gates_in), (rows, out.at[:tokens])]
    for step in range(3):
        start = pl.multiple_of(chip_of(z, step) * (2 * most), 2 * most)
        for local in range(2):
            span = others.at[local, 2 * most * (step - 1) : 2 * most * step] if step else first.at[local]
            pairs.append((hidden.at[local, pl.ds(start, 2 * most)], span))
    copies = [pltpu.make_async_copy(a, b, sem.at[i]) for i, (a, b) in enumerate(pairs)]
    for copy in copies:
        copy.start()
    for copy in copies[:3]:
        copy.wait()
    rank = slots_in[...] - (2 * z + core) * most
    parts = [routes_in[...], rank, gates_in[...]]
    packed = jnp.concatenate([part.astype(jnp.float32) for part in parts], axis=1)
    packed = jnp.concatenate([packed, jnp.zeros((TAIL - top, 3 * tokens), jnp.float32)], axis=0)
    out[tokens:, : 3 * tokens] = packed.astype(jnp.bfloat16)
    out[tokens:, 3 * tokens :] = jnp.zeros((TAIL, out.shape[1] - 3 * tokens), jnp.bfloat16)
    for copy in copies[3:]:
        copy.wait()


def prepare(most, grad_out, routes, slots, gates, hidden):
    tokens, feats = grad_out.shape
    top = routes.shape[1]
    experts, _, width = hidden.shape
    return pl.pallas_call(
        functools.partial(prepare_kernel, most),
        in_specs=[ANY] * 5,
        out_specs=[VMEM] * 3,
        out_shape=[
            like((tokens + TAIL, feats), jnp.bfloat16),
            like((experts, 2 * most, width), jnp.bfloat16),
            like((experts, 4 * most, width), jnp.bfloat16),
        ],
        scratch_shapes=[
            pltpu.VMEM((top, tokens), jnp.int32),
            pltpu.VMEM((top, tokens), jnp.int32),
            pltpu.VMEM((top, tokens), jnp.bfloat16),
            pltpu.SemaphoreType.DMA((10,)),
        ],
        compiler_params=pltpu.CompilerParams(vmem_limit_bytes=8 * MIB),
        cost_estimate=cost([grad_out, grad_out, hidden]),
        name="prepare",
    )(*(hbm(a) for a in (grad_out, routes.T, slots.T, gates.T, hidden)))


def load_kernel(after, weight, out, sem):
    copy = pltpu.make_async_copy(weight, out, sem)
    copy.start()
    copy.wait()


def load(after, weight):
    return pl.pallas_call(
        load_kernel,
        in_specs=[ANY, ANY],
        out_specs=VMEM,
        out_shape=like(weight.shape, weight.dtype),
        scratch_shapes=[pltpu.SemaphoreType.DMA],
        cost_estimate=cost([weight, weight]),
        compiler_params=pltpu.CompilerParams(vmem_limit_bytes=16 * MIB),
        name="load_weight",
    )(after, hbm(weight))


def pick_kernel(rules, count, *refs):
    sem = refs[-1]
    outs = refs[-1 - len(rules) : -1]
    z = place()[0]
    for number, rule in enumerate(rules):
        for source in sorted(set(rule)):
            wanted = functools.reduce(
                jnp.logical_or, [z == at_z for at_z in range(len(rule)) if rule[at_z] == source]
            )

            @pl.when(wanted)
            def _(source=source, number=number):
                pltpu.make_async_copy(refs[source], outs[number], sem.at[number]).start()

    for number in range(len(rules)):
        pltpu.make_async_copy(refs[0], outs[number], sem.at[number]).wait()


def pick(rules, blocks, after):
    return pl.pallas_call(
        functools.partial(pick_kernel, rules, len(blocks)),
        in_specs=[VMEM] * len(blocks) + [ANY] * len(after),
        out_specs=[VMEM] * len(rules),
        out_shape=[like(blocks[0].shape, blocks[0].dtype)] * len(rules),
        scratch_shapes=[pltpu.SemaphoreType.DMA((len(rules),))],
        compiler_params=pltpu.CompilerParams(vmem_limit_bytes=8 * MIB),
        cost_estimate=cost(blocks),
        name="pick",
    )(*blocks, *after)


def take_kernel(over_x, over_y, block, one, other, again, sem):
    copies = [
        pltpu.make_async_copy(over_x.at[0], one, sem.at[0]),
        pltpu.make_async_copy(over_y.at[1], other, sem.at[1]),
        pltpu.make_async_copy(block, again, sem.at[2]),
    ]
    for copy in copies:
        copy.start()
    for copy in copies:
        copy.wait()


def take(over_x, over_y, block):
    out = like(over_x.shape[1:], over_x.dtype)
    return pl.pallas_call(
        take_kernel,
        in_specs=[VMEM] * 3,
        out_specs=[VMEM] * 3,
        out_shape=[out, out, like(block.shape, block.dtype)],
        scratch_shapes=[pltpu.SemaphoreType.DMA((3,))],
        compiler_params=pltpu.CompilerParams(vmem_limit_bytes=8 * MIB),
        cost_estimate=cost([out, out]),
        name="take",
    )(over_x, over_y, block)


def expert_view(info, expert, top):
    tokens = info.shape[1] // 3
    at = info[:top, :tokens] == expert.astype(jnp.float32)
    rank = jnp.sum(jnp.where(at, info[:top, tokens : 2 * tokens] + 1.0, 0.0), axis=0, keepdims=True) - 1.0
    gate = jnp.sum(jnp.where(at, info[:top, 2 * tokens :], 0.0), axis=0, keepdims=True)
    return at, rank, gate


def rank_picks(rank, count, first, limit):
    numbers = lax.broadcasted_iota(jnp.int32, (count, rank.shape[1]), 0)
    hit = (numbers.astype(jnp.float32) == rank) & (first + numbers < limit)
    return jnp.where(hit, 1.0, 0.0)


def share_kernel(local, most, top, group, earlier, waits, cap, weight, *refs):
    blocks, refs = refs[: 2 * len(group)], refs[2 * len(group) :]
    if earlier is None:
        send, keep, info, rows = refs[waits:]
    else:
        stored, befores = refs[:4], refs[4 : 4 + earlier]
        send, keep, gates, mine, theirs, rows, info, grads = refs[4 + earlier + waits :]
    z, core, x, y = place()
    tokens = blocks[0].shape[0] - TAIL
    total, width = keep.shape[1], keep.shape[2]
    expert = (2 * z + core) * 2 + local

    def gather(at, block, side):
        table = block[tokens:, : 3 * tokens].astype(jnp.float32)
        info[2 * at + side] = table
        _, rank, gate = expert_view(table, expert, top)
        first = (2 * chip_of(z, group[at]) + side) * most
        picks = rank_picks(rank, most, first, cap[local])
        span = pl.ds(pl.multiple_of((2 * at + side) * most, most), most)
        rows[span, :] = jnp.dot(
            picks.astype(jnp.bfloat16), block[:tokens, :], preferred_element_type=jnp.float32
        ).astype(jnp.bfloat16)
        if earlier is not None:
            weights = jnp.sum(picks * gate, axis=1, keepdims=True)
            gates[span, :] = jnp.broadcast_to(weights, (most, gates.shape[1]))

    for swap in range(2):
        side = lax.rem(core + swap, 2)
        for at in range(len(group)):
            gather(at, blocks[2 * at + swap], side)

    powers = []
    for number, (sent, onward) in enumerate(((1, 1), (1, 0), (0, 1), (0, 0))):
        dx, dy = (sent, onward) if local == 0 else (onward, sent)
        piece = 2 * lax.rem(y + dy, 2) + lax.rem(x + dx, 2)
        part = lax.dot_general(
            rows[...],
            weight[local, pl.ds(pl.multiple_of(piece * width, width), width), :],
            (((1,), (1,)), ((), ())),
            preferred_element_type=jnp.float32,
        )
        if earlier is not None:
            there = stored[3][...] if dx and dy else stored[2 * dy + dx][local]
            grad = there.astype(jnp.float32) * part
            grad = jnp.sum(grad, axis=1, keepdims=True)
            grads[...] = grads[...] + grad if number else grad
        if sent:
            code, power = encode(part)
            send[(1 - onward) * total : (2 - onward) * total, :] = code
            powers.append(power)
        else:
            keep[1 - onward] = part
    send[2 * total :, :] = powers_block(powers, width)

    if earlier is not None:
        for out, befores_of in ((mine, befores[0::2]), (theirs, befores[1::2])):
            out[...] = sum((b[...] for b in befores_of), jnp.zeros(out.shape, jnp.float32))
        for at, step in enumerate(group):
            chip = chip_of(z, step)
            for out, side in ((mine, core), (theirs, 1 - core)):
                named, rank, _ = expert_view(info[2 * at + side], expert, top)
                picks = rank_picks(rank, most, (2 * chip + side) * most, cap[local])
                span = pl.ds(pl.multiple_of((2 * at + side) * most, most), most)
                back = jnp.sum(picks * grads[span, :], axis=0, keepdims=True)
                out[chip] = out[chip] + jnp.where(named, back, 0.0)


def partial_share(local, most, top, group, cap, weight, blocks, stored=None, befores=(), after=()):
    tokens, feats = blocks[0].shape[0] - TAIL, blocks[0].shape[1]
    width = weight.shape[1] // 4
    total = 2 * most * len(group)
    tables = (2 * len(group), TAIL, 3 * tokens)
    outs = [like((2 * total + TAIL, width), jnp.int16), like((2, total, width))]
    scratch = [pltpu.VMEM((total, feats), jnp.bfloat16)]
    args = [cap, weight, *blocks]
    if stored is None:
        outs.append(like(tables))
    else:
        outs += [like((total, 128)), like((3, top, tokens)), like((3, top, tokens))]
        scratch += [pltpu.VMEM(tables, jnp.float32), pltpu.VMEM((total, 1), jnp.float32)]
        args += [*stored, *befores]
    earlier = None if stored is None else len(befores)
    return pl.pallas_call(
        functools.partial(share_kernel, local, most, top, group, earlier, len(after)),
        in_specs=[SMEM] + [VMEM] * (len(args) - 1) + [ANY] * len(after),
        out_specs=[VMEM] * len(outs),
        out_shape=outs,
        scratch_shapes=scratch,
        cost_estimate=cost([weight, *blocks], 8 * total * width * feats),
        compiler_params=pltpu.CompilerParams(vmem_limit_bytes=28 * MIB),
        name=f"share_{local}",
    )(*args, *after)


def middle_kernel(got, keep, *refs):
    send, rest = refs[-2:]
    rows, width = rest.shape
    code, power = encode(keep[0] + decode(got, 0, 2))
    send[:rows, :] = code
    send[rows:, :] = powers_block([power], width)
    rest[...] = keep[1] + decode(got, 1, 2)


def middle(got, keep, after=()):
    _, rows, width = keep.shape
    return pl.pallas_call(
        middle_kernel,
        in_specs=[VMEM, VMEM] + [ANY] * len(after),
        out_specs=[VMEM, VMEM],
        out_shape=[like((rows + TAIL, width), jnp.int16), like((rows, width))],
        cost_estimate=cost([got, keep, keep]),
        compiler_params=pltpu.CompilerParams(vmem_limit_bytes=8 * MIB),
        name="middle",
    )(got, keep, *after)


def first_finish_kernel(
    most, top, cap, hidden, info, got0, rest0, got1, rest1, more_mine, more_theirs, out, mine, theirs
):
    z, core, _, _ = place()
    chip = chip_of(z, 0)
    mine[...] = more_mine[...]
    theirs[...] = more_theirs[...]
    for local, (got, rest) in enumerate(((got0, rest0), (got1, rest1))):
        out[local] = rest[...] + decode(got, 0, 1)
        for parts, side in ((mine, core), (theirs, 1 - core)):
            span = pl.ds(pl.multiple_of(side * most, most), most)
            named, rank, gate = expert_view(info[side], (2 * z + core) * 2 + local, top)
            picks = rank_picks(rank, most, (2 * chip + side) * most, cap[local])
            weight = jnp.sum(picks * gate, axis=1, keepdims=True)
            share = out[local, span, :]
            grad = jnp.sum(hidden[local, span, :].astype(jnp.float32) * share, axis=1, keepdims=True)
            out[local, span, :] = weight * share
            back = jnp.sum(picks * grad, axis=0, keepdims=True)
            parts[chip] = parts[chip] + jnp.where(named, back, 0.0)


def first_finish(most, top, cap, hidden, info, sums, parts):
    tokens = info.shape[2] // 3
    return pl.pallas_call(
        functools.partial(first_finish_kernel, most, top),
        in_specs=[SMEM] + [VMEM] * 8,
        out_specs=[VMEM] * 3,
        out_shape=[like(hidden.shape), like((3, top, tokens)), like((3, top, tokens))],
        compiler_params=pltpu.CompilerParams(vmem_limit_bytes=8 * MIB),
        cost_estimate=cost([*sums, hidden]),
        name="first_finish",
    )(cap, hidden, info, *sums, *parts)


def finish_kernel(most, first, got0, rest0, gates0, got1, rest1, gates1, *refs):
    totals, (out, gate_grad) = refs[:-2], refs[-2:]
    gate_grad[...] = sum((total[...] for total in totals[1:]), totals[0][...])
    z = place()[0]
    spans = [pl.ds(pl.multiple_of(chip_of(z, s) * (2 * most), 2 * most), 2 * most) for s in range(3)]
    for local, (got, rest, gates) in enumerate(((got0, rest0, gates0), (got1, rest1, gates1))):
        out[local, spans[0], :] = first[local]
        grad = gates[:, :1] * (rest[...] + decode(got, 0, 1))
        out[local, spans[1], :] = grad[: 2 * most]
        out[local, spans[2], :] = grad[2 * most :]


def finish(most, first, sums, totals):
    experts, rows, width = first.shape
    return pl.pallas_call(
        functools.partial(finish_kernel, most),
        in_specs=[VMEM] * (7 + len(totals)),
        out_specs=[VMEM, VMEM],
        out_shape=[like((experts, 3 * rows, width)), like(totals[0].shape)],
        compiler_params=pltpu.CompilerParams(vmem_limit_bytes=16 * MIB),
        cost_estimate=cost([*sums, first, first]),
        name="finish",
    )(first, *sums, *totals)


def chips_kernel(mine, got, stay, away):
    z = place()[0]
    low, mid, high = (mine[i] + got[i] for i in range(3))
    none = jnp.zeros(low.shape, jnp.float32)
    stay[0] = jnp.where(z < 2, low, high)
    stay[1] = jnp.where(z < 2, mid, none)
    away[0] = jnp.where(z < 2, high, low)
    away[1] = jnp.where(z < 2, none, mid)


def chip_kernel(kept, got, stay, away):
    odd = lax.rem(place()[0], 2) == 1
    even_part, odd_part = (kept[i] + got[i] for i in range(2))
    stay[...] = jnp.where(odd, odd_part, even_part)
    away[...] = jnp.where(odd, even_part, odd_part)


def add_kernel(*refs):
    total = refs[0][...]
    for ref in refs[1:-1]:
        total = total + ref[...]
    refs[-1][...] = total


def small(kernel, outs, *args, after=()):
    used = len(args)
    return pl.pallas_call(
        lambda *refs: kernel(*refs[:used], *refs[used + len(after) :]),
        in_specs=[VMEM] * used + [ANY] * len(after),
        out_specs=[VMEM] * len(outs),
        out_shape=outs,
        compiler_params=pltpu.CompilerParams(vmem_limit_bytes=2 * MIB),
        cost_estimate=cost(args),
        name=kernel.__name__,
    )(*args, *after)


def blockwise(most, grad_out, routes, slots, gates, capacity, hidden, down_weight):
    peers, ranks = lax.axis_size("expert"), lax.axis_size("dp")
    tokens, top = routes.shape

    def along(rows, pairs):
        return lax.ppermute(rows, "expert", [(2 * a + c, 2 * b + c) for a, b in pairs for c in range(2)])

    def across(rows):
        return lax.ppermute(rows, "expert", [(i, i ^ 1) for i in range(peers)])

    def over(rows, flip):
        return lax.ppermute(rows, "dp", [(i, i ^ flip) for i in range(ranks)])

    block, first_hidden, other_hidden = prepare(most, grad_out, routes, slots, gates, hidden)
    up1 = along(block, [(0, 1), (1, 2), (2, 3)])
    down1 = along(block, [(2, 1), (1, 0)])
    stored = [other_hidden, over(other_hidden, 1), over(other_hidden, 2)]
    *passed, again = take(stored[1], stored[2], block)
    far_stored = [over(passed[0], 2), over(passed[1], 1)]
    weight = load(block, down_weight)

    (first,) = pick(((0, 0, 0, 1),), (block, up1), (weight, down1))
    up2 = along(up1, [(1, 2), (2, 3)])
    down2 = along(again, [(2, 0)])
    pair = (first, across(first))
    sent, kept = [], []
    for local in range(2):
        send, keep, info = partial_share(
            local, most, top, (0,), capacity, weight, pair, after=far_stored[:1] if local else ()
        )
        sent.append(send)
        kept.append(keep)

    up3 = along(up2, [(2, 3)])
    (second,) = pick(((2, 0, 0, 1),), (up1, up2, down1), (*sent, *far_stored))
    blocks = [second, across(second)]

    sums, onward = [], []
    for local in range(2):
        send, rest = middle(over(sent[local], 1 + local), kept[local])
        onward.append(send)
        sums += [over(send, 2 - local), rest]
    (third,) = pick(((0, 1, 2, 3),), (down2, down1, up2, up3), ())
    blocks += [third, across(third)]

    halves = [None, None]
    before = []
    for local in (1, 0):
        send, keep, gate, *before = partial_share(
            local, most, top, (1, 2), capacity, weight, blocks, [*stored, far_stored[local]], before,
            onward if local else (sums[0], sums[2]),
        )
        halves[local] = (over(send, 1 + local), keep, gate)
    first_grad, mine, theirs = first_finish(most, top, capacity, first_hidden, info, sums, before)

    one = like((top, tokens))
    two = like((2, top, tokens))
    (got0, keep0, gate0), (got1, keep1, gate1) = halves
    stay, away = small(chips_kernel, [two, two], mine, across(theirs))
    came = along(away, [(z, z ^ 2) for z in range(peers // 2)])
    stay, away = small(chip_kernel, [one, one], stay, came)
    send1, rest1 = middle(got1, keep1, (away,))
    (total,) = small(
        add_kernel, [one], stay, along(away, [(z, z ^ 1) for z in range(peers // 2)]), after=(send1,)
    )
    whole = [total] + [over(total, flip) for flip in range(1, ranks)]
    send0, rest0 = middle(got0, keep0, (total,))
    sums = [over(send0, 2), rest0, gate0, over(send1, 1), rest1, gate1]
    hidden_grad, gate_grad = finish(most, first_grad, sums, whole)
    return hidden_grad, gate_grad.T


def solution(mesh):
    peers, ranks = mesh.shape["expert"], mesh.shape["dp"]

    def shards(grad_out, routes, slots, gates, capacity, hidden, down_weight):
        tokens, top = routes.shape
        experts = down_weight.shape[0] * peers
        most = top * max(2, (tokens + experts - 1) // experts)
        full = most * experts == tokens * top
        fits = peers == 8 and hidden.shape[1] == 6 * most and 3 * tokens <= grad_out.shape[1]
        square = ranks == 4 and down_weight.shape[0] == 2 and experts <= 256 and most <= 256
        if full and fits and square:
            return blockwise(most, grad_out, routes, slots, gates, capacity, hidden, down_weight)
        return general(grad_out, routes, slots, gates, capacity, hidden, down_weight)

    placed = (
        P("expert", "dp"),
        P("expert", None),
        P("expert", None),
        P("expert", None),
        P("expert"),
        P("expert", None, "dp"),
        P("expert", None, "dp"),
    )
    return jax.shard_map(
        shards,
        mesh=mesh,
        in_specs=placed,
        out_specs=(P("expert", None, "dp"), P("expert", None)),
        check_vma=False,
    )
```

```python
import functools
import math

import jax
import jax.numpy as jnp
from jax import lax
from jax.experimental import pallas as pl
from jax.experimental.pallas import tpu as pltpu
from jax.sharding import PartitionSpec as P

STEPS = 32766.0
TAIL = 16
VMEM = pl.BlockSpec(memory_space=pltpu.VMEM)
ANY = pl.BlockSpec(memory_space=pl.ANY)
SMEM = pl.BlockSpec(memory_space=pltpu.SMEM)


def local_ranks(route_grid, expert_total):
    onehot = (route_grid[..., None] == jnp.arange(expert_total, dtype=jnp.int32)).astype(jnp.int32)
    before = jnp.cumsum(onehot, axis=-2) - onehot
    return jnp.sum(before * onehot, axis=-1)


def capacity_of(local_expert, capacity):
    picks = local_expert[..., None] == jnp.arange(capacity.shape[0], dtype=jnp.int32)
    return jnp.sum(jnp.where(picks, capacity, 0), axis=-1)


def general(grad_out, routes, slots, gates, capacity, hidden, down_weight):
    peer_count = lax.axis_size("expert")
    experts_here = down_weight.shape[0]
    slot_count = hidden.shape[1]
    tok_rows, top_count = routes.shape
    feature_width = grad_out.shape[1]
    expert_total = experts_here * peer_count
    most_rows = top_count * max(2, (tok_rows + expert_total - 1) // expert_total)
    slot_total = experts_here * slot_count
    route_flat = routes.reshape(-1)
    slot_flat = slots.reshape(-1)
    dest_pos = route_flat * most_rows + local_ranks(route_flat, expert_total)
    send_rows = (
        jnp.zeros((expert_total * most_rows, feature_width), jnp.bfloat16)
        .at[dest_pos]
        .set(jnp.repeat(grad_out, top_count, axis=0))
    )
    send_gate = (
        jnp.zeros((expert_total * most_rows,), jnp.bfloat16).at[dest_pos].set(gates.reshape(-1))
    )
    send_slot = (
        jnp.full((expert_total * most_rows,), slot_count, jnp.int32).at[dest_pos].set(slot_flat)
    )
    exchange = functools.partial(
        lax.all_to_all, axis_name="expert", split_axis=0, concat_axis=0, tiled=True
    )
    recv_rows = exchange(send_rows.reshape(peer_count, experts_here * most_rows, feature_width))
    recv_gate = exchange(send_gate.reshape(peer_count, experts_here * most_rows))
    recv_slot = exchange(send_slot.reshape(peer_count, experts_here * most_rows))
    local_expert = jnp.broadcast_to(
        (jnp.arange(experts_here * most_rows, dtype=jnp.int32) // most_rows)[None, :],
        recv_slot.shape,
    )
    usable = recv_slot < capacity_of(local_expert, capacity)
    slot_table = jnp.where(usable, local_expert * slot_count + recv_slot, slot_total).reshape(-1)
    slot_rows = (
        jnp.zeros((slot_total, feature_width), jnp.bfloat16)
        .at[slot_table]
        .set(recv_rows.reshape(-1, feature_width), mode="drop")
    )
    slot_gate = (
        jnp.zeros((slot_total,), jnp.bfloat16)
        .at[slot_table]
        .set(recv_gate.reshape(-1), mode="drop")
    )
    slot_blocks = slot_rows.reshape(experts_here, slot_count, feature_width)
    share_rows = lax.psum_scatter(
        jnp.einsum("efd,ecd->fec", down_weight, slot_blocks, preferred_element_type=jnp.float32),
        "dp",
        scatter_dimension=0,
        tiled=True,
    )
    hidden_share = jnp.transpose(share_rows, (1, 2, 0))
    hidden_grad = (
        slot_gate.reshape(experts_here, slot_count)[..., None].astype(jnp.float32) * hidden_share
    )
    partial_grad = jnp.sum(hidden.astype(jnp.float32) * hidden_share, axis=-1)
    slot_grad = lax.psum(partial_grad, "dp").reshape(-1)
    picked = slot_grad[jnp.minimum(slot_table, slot_total - 1)]
    outgoing = jnp.where(slot_table < slot_total, picked, jnp.float32(0.0)).reshape(
        peer_count, experts_here * most_rows
    )
    incoming = exchange(outgoing).reshape(-1)
    gate_grad = incoming[dest_pos].reshape(tok_rows, top_count)
    return hidden_grad, gate_grad


ORDER = ((0, 1, 2), (1, 0, 2), (2, 1, 0), (2, 1, 0))
MIB = 2**20


def cost(shapes, flops=0):
    size = sum(math.prod(a.shape) * a.dtype.itemsize for a in shapes)
    return pl.CostEstimate(flops=flops, bytes_accessed=size, transcendentals=0)


def hbm(array):
    return pltpu.with_memory_space_constraint(array, pltpu.HBM)


def like(shape, kind=jnp.float32):
    return jax.ShapeDtypeStruct(shape, kind)


def place():
    me, rank = lax.axis_index("expert"), lax.axis_index("dp")
    return me // 2, lax.rem(me, 2), lax.rem(rank, 2), rank // 2


def chip_of(z, step):
    chip = jnp.int32(ORDER[0][step])
    for at_z in range(1, len(ORDER)):
        chip = jnp.where(z == at_z, ORDER[at_z][step], chip)
    return chip


def encode(values):
    peak = jnp.maximum(jnp.max(jnp.abs(values), keepdims=True), 1e-30)
    power = jnp.floor(jnp.log2(peak)) + 1.0
    scaled = (values * jnp.exp2(-power)) * (STEPS * STEPS)
    code = jnp.round(scaled * lax.rsqrt(jnp.abs(scaled) + 1e-20))
    return code.astype(jnp.int32).astype(jnp.int16), power


def powers_block(powers, width):
    spans = [jnp.broadcast_to(power, (TAIL, width // len(powers))) for power in powers]
    return jnp.concatenate(spans, axis=1).astype(jnp.int32).astype(jnp.int16)


def decode(coded, part, parts):
    rows = (coded.shape[0] - TAIL) // parts
    lane = part * (coded.shape[1] // parts)
    power = coded[parts * rows :, lane : lane + 128].astype(jnp.int32).astype(jnp.float32)
    code = coded[part * rows : (part + 1) * rows, :].astype(jnp.int32).astype(jnp.float32)
    scale = jnp.exp2(jnp.max(power, keepdims=True))
    return (code * jnp.abs(code) * (1.0 / (STEPS * STEPS))) * scale


def prepare_kernel(
    most, rows, routes, slots, gates, hidden, out, first, others, routes_in, slots_in, gates_in, sem
):
    tokens, top = rows.shape[0], routes.shape[0]
    z, core, _, _ = place()
    pairs = [(routes, routes_in), (slots, slots_in), (gates, gates_in), (rows, out.at[:tokens])]
    for step in range(3):
        start = pl.multiple_of(chip_of(z, step) * (2 * most), 2 * most)
        for local in range(2):
            span = others.at[local, 2 * most * (step - 1) : 2 * most * step] if step else first.at[local]
            pairs.append((hidden.at[local, pl.ds(start, 2 * most)], span))
    copies = [pltpu.make_async_copy(a, b, sem.at[i]) for i, (a, b) in enumerate(pairs)]
    for copy in copies:
        copy.start()
    for copy in copies[:3]:
        copy.wait()
    rank = slots_in[...] - (2 * z + core) * most
    parts = [routes_in[...], rank, gates_in[...]]
    packed = jnp.concatenate([part.astype(jnp.float32) for part in parts], axis=1)
    packed = jnp.concatenate([packed, jnp.zeros((TAIL - top, 3 * tokens), jnp.float32)], axis=0)
    out[tokens:, : 3 * tokens] = packed.astype(jnp.bfloat16)
    out[tokens:, 3 * tokens :] = jnp.zeros((TAIL, out.shape[1] - 3 * tokens), jnp.bfloat16)
    for copy in copies[3:]:
        copy.wait()


def prepare(most, grad_out, routes, slots, gates, hidden):
    tokens, feats = grad_out.shape
    top = routes.shape[1]
    experts, _, width = hidden.shape
    return pl.pallas_call(
        functools.partial(prepare_kernel, most),
        in_specs=[ANY] * 5,
        out_specs=[VMEM] * 3,
        out_shape=[
            like((tokens + TAIL, feats), jnp.bfloat16),
            like((experts, 2 * most, width), jnp.bfloat16),
            like((experts, 4 * most, width), jnp.bfloat16),
        ],
        scratch_shapes=[
            pltpu.VMEM((top, tokens), jnp.int32),
            pltpu.VMEM((top, tokens), jnp.int32),
            pltpu.VMEM((top, tokens), jnp.bfloat16),
            pltpu.SemaphoreType.DMA((10,)),
        ],
        compiler_params=pltpu.CompilerParams(vmem_limit_bytes=8 * MIB),
        cost_estimate=cost([grad_out, grad_out, hidden]),
        name="prepare",
    )(*(hbm(a) for a in (grad_out, routes.T, slots.T, gates.T, hidden)))


def load_kernel(after, weight, out, sem):
    copy = pltpu.make_async_copy(weight, out, sem)
    copy.start()
    copy.wait()


def load(after, weight):
    return pl.pallas_call(
        load_kernel,
        in_specs=[ANY, ANY],
        out_specs=VMEM,
        out_shape=like(weight.shape, weight.dtype),
        scratch_shapes=[pltpu.SemaphoreType.DMA],
        cost_estimate=cost([weight, weight]),
        compiler_params=pltpu.CompilerParams(vmem_limit_bytes=16 * MIB),
        name="load_weight",
    )(after, hbm(weight))


def pick_kernel(rules, count, *refs):
    sem = refs[-1]
    outs = refs[-1 - len(rules) : -1]
    z = place()[0]
    for number, rule in enumerate(rules):
        for source in sorted(set(rule)):
            wanted = functools.reduce(
                jnp.logical_or, [z == at_z for at_z in range(len(rule)) if rule[at_z] == source]
            )

            @pl.when(wanted)
            def _(source=source, number=number):
                pltpu.make_async_copy(refs[source], outs[number], sem.at[number]).start()

    for number in range(len(rules)):
        pltpu.make_async_copy(refs[0], outs[number], sem.at[number]).wait()


def pick(rules, blocks, after):
    return pl.pallas_call(
        functools.partial(pick_kernel, rules, len(blocks)),
        in_specs=[VMEM] * len(blocks) + [ANY] * len(after),
        out_specs=[VMEM] * len(rules),
        out_shape=[like(blocks[0].shape, blocks[0].dtype)] * len(rules),
        scratch_shapes=[pltpu.SemaphoreType.DMA((len(rules),))],
        compiler_params=pltpu.CompilerParams(vmem_limit_bytes=8 * MIB),
        cost_estimate=cost(blocks),
        name="pick",
    )(*blocks, *after)


def take_kernel(over_x, over_y, block, one, other, again, sem):
    copies = [
        pltpu.make_async_copy(over_x.at[0], one, sem.at[0]),
        pltpu.make_async_copy(over_y.at[1], other, sem.at[1]),
        pltpu.make_async_copy(block, again, sem.at[2]),
    ]
    for copy in copies:
        copy.start()
    for copy in copies:
        copy.wait()


def take(over_x, over_y, block):
    out = like(over_x.shape[1:], over_x.dtype)
    return pl.pallas_call(
        take_kernel,
        in_specs=[VMEM] * 3,
        out_specs=[VMEM] * 3,
        out_shape=[out, out, like(block.shape, block.dtype)],
        scratch_shapes=[pltpu.SemaphoreType.DMA((3,))],
        compiler_params=pltpu.CompilerParams(vmem_limit_bytes=8 * MIB),
        cost_estimate=cost([out, out]),
        name="take",
    )(over_x, over_y, block)


def expert_view(info, expert, top):
    tokens = info.shape[1] // 3
    at = info[:top, :tokens] == expert.astype(jnp.float32)
    rank = jnp.sum(jnp.where(at, info[:top, tokens : 2 * tokens] + 1.0, 0.0), axis=0, keepdims=True) - 1.0
    gate = jnp.sum(jnp.where(at, info[:top, 2 * tokens :], 0.0), axis=0, keepdims=True)
    return at, rank, gate


def rank_picks(rank, count, first, limit):
    numbers = lax.broadcasted_iota(jnp.int32, (count, rank.shape[1]), 0)
    hit = (numbers.astype(jnp.float32) == rank) & (first + numbers < limit)
    return jnp.where(hit, 1.0, 0.0)


def share_kernel(local, most, top, group, earlier, waits, cap, weight, *refs):
    blocks, refs = refs[: 2 * len(group)], refs[2 * len(group) :]
    if earlier is None:
        send, keep, info, rows = refs[waits:]
    else:
        stored, befores = refs[:4], refs[4 : 4 + earlier]
        send, keep, gates, mine, theirs, rows, info, grads = refs[4 + earlier + waits :]
    z, core, x, y = place()
    tokens = blocks[0].shape[0] - TAIL
    total, width = keep.shape[1], keep.shape[2]
    expert = (2 * z + core) * 2 + local

    def gather(at, block, side):
        table = block[tokens:, : 3 * tokens].astype(jnp.float32)
        info[2 * at + side] = table
        _, rank, gate = expert_view(table, expert, top)
        first = (2 * chip_of(z, group[at]) + side) * most
        picks = rank_picks(rank, most, first, cap[local])
        span = pl.ds(pl.multiple_of((2 * at + side) * most, most), most)
        rows[span, :] = jnp.dot(
            picks.astype(jnp.bfloat16), block[:tokens, :], preferred_element_type=jnp.float32
        ).astype(jnp.bfloat16)
        if earlier is not None:
            weights = jnp.sum(picks * gate, axis=1, keepdims=True)
            gates[span, :] = jnp.broadcast_to(weights, (most, gates.shape[1]))

    for swap in range(2):
        side = lax.rem(core + swap, 2)
        for at in range(len(group)):
            gather(at, blocks[2 * at + swap], side)

    powers = []
    for number, (sent, onward) in enumerate(((1, 1), (1, 0), (0, 1), (0, 0))):
        dx, dy = (sent, onward) if local == 0 else (onward, sent)
        piece = 2 * lax.rem(y + dy, 2) + lax.rem(x + dx, 2)
        part = lax.dot_general(
            rows[...],
            weight[local, pl.ds(pl.multiple_of(piece * width, width), width), :],
            (((1,), (1,)), ((), ())),
            preferred_element_type=jnp.float32,
        )
        if earlier is not None:
            there = stored[3][...] if dx and dy else stored[2 * dy + dx][local]
            grad = there.astype(jnp.float32) * part
            grad = jnp.sum(grad, axis=1, keepdims=True)
            grads[...] = grads[...] + grad if number else grad
        if sent:
            code, power = encode(part)
            send[(1 - onward) * total : (2 - onward) * total, :] = code
            powers.append(power)
        else:
            keep[1 - onward] = part
    send[2 * total :, :] = powers_block(powers, width)

    if earlier is not None:
        for out, befores_of in ((mine, befores[0::2]), (theirs, befores[1::2])):
            out[...] = sum((b[...] for b in befores_of), jnp.zeros(out.shape, jnp.float32))
        for at, step in enumerate(group):
            chip = chip_of(z, step)
            for out, side in ((mine, core), (theirs, 1 - core)):
                named, rank, _ = expert_view(info[2 * at + side], expert, top)
                picks = rank_picks(rank, most, (2 * chip + side) * most, cap[local])
                span = pl.ds(pl.multiple_of((2 * at + side) * most, most), most)
                back = jnp.sum(picks * grads[span, :], axis=0, keepdims=True)
                out[chip] = out[chip] + jnp.where(named, back, 0.0)


def partial_share(local, most, top, group, cap, weight, blocks, stored=None, befores=(), after=()):
    tokens, feats = blocks[0].shape[0] - TAIL, blocks[0].shape[1]
    width = weight.shape[1] // 4
    total = 2 * most * len(group)
    tables = (2 * len(group), TAIL, 3 * tokens)
    outs = [like((2 * total + TAIL, width), jnp.int16), like((2, total, width))]
    scratch = [pltpu.VMEM((total, feats), jnp.bfloat16)]
    args = [cap, weight, *blocks]
    if stored is None:
        outs.append(like(tables))
    else:
        outs += [like((total, 128)), like((3, top, tokens)), like((3, top, tokens))]
        scratch += [pltpu.VMEM(tables, jnp.float32), pltpu.VMEM((total, 1), jnp.float32)]
        args += [*stored, *befores]
    earlier = None if stored is None else len(befores)
    return pl.pallas_call(
        functools.partial(share_kernel, local, most, top, group, earlier, len(after)),
        in_specs=[SMEM] + [VMEM] * (len(args) - 1) + [ANY] * len(after),
        out_specs=[VMEM] * len(outs),
        out_shape=outs,
        scratch_shapes=scratch,
        cost_estimate=cost([weight, *blocks], 8 * total * width * feats),
        compiler_params=pltpu.CompilerParams(vmem_limit_bytes=28 * MIB),
        name=f"share_{local}",
    )(*args, *after)


def middle_kernel(got, keep, *refs):
    send, rest = refs[-2:]
    rows, width = rest.shape
    code, power = encode(keep[0] + decode(got, 0, 2))
    send[:rows, :] = code
    send[rows:, :] = powers_block([power], width)
    rest[...] = keep[1] + decode(got, 1, 2)


def middle(got, keep, after=()):
    _, rows, width = keep.shape
    return pl.pallas_call(
        middle_kernel,
        in_specs=[VMEM, VMEM] + [ANY] * len(after),
        out_specs=[VMEM, VMEM],
        out_shape=[like((rows + TAIL, width), jnp.int16), like((rows, width))],
        cost_estimate=cost([got, keep, keep]),
        compiler_params=pltpu.CompilerParams(vmem_limit_bytes=8 * MIB),
        name="middle",
    )(got, keep, *after)


def first_finish_kernel(
    most, top, cap, hidden, info, got0, rest0, got1, rest1, more_mine, more_theirs, out, mine, theirs
):
    z, core, _, _ = place()
    chip = chip_of(z, 0)
    mine[...] = more_mine[...]
    theirs[...] = more_theirs[...]
    for local, (got, rest) in enumerate(((got0, rest0), (got1, rest1))):
        out[local] = rest[...] + decode(got, 0, 1)
        for parts, side in ((mine, core), (theirs, 1 - core)):
            span = pl.ds(pl.multiple_of(side * most, most), most)
            named, rank, gate = expert_view(info[side], (2 * z + core) * 2 + local, top)
            picks = rank_picks(rank, most, (2 * chip + side) * most, cap[local])
            weight = jnp.sum(picks * gate, axis=1, keepdims=True)
            share = out[local, span, :]
            grad = jnp.sum(hidden[local, span, :].astype(jnp.float32) * share, axis=1, keepdims=True)
            out[local, span, :] = weight * share
            back = jnp.sum(picks * grad, axis=0, keepdims=True)
            parts[chip] = parts[chip] + jnp.where(named, back, 0.0)


def first_finish(most, top, cap, hidden, info, sums, parts):
    tokens = info.shape[2] // 3
    return pl.pallas_call(
        functools.partial(first_finish_kernel, most, top),
        in_specs=[SMEM] + [VMEM] * 8,
        out_specs=[VMEM] * 3,
        out_shape=[like(hidden.shape), like((3, top, tokens)), like((3, top, tokens))],
        compiler_params=pltpu.CompilerParams(vmem_limit_bytes=8 * MIB),
        cost_estimate=cost([*sums, hidden]),
        name="first_finish",
    )(cap, hidden, info, *sums, *parts)


def finish_kernel(most, first, got0, rest0, gates0, got1, rest1, gates1, *refs):
    totals, (out, gate_grad) = refs[:-2], refs[-2:]
    gate_grad[...] = sum((total[...] for total in totals[1:]), totals[0][...])
    z = place()[0]
    spans = [pl.ds(pl.multiple_of(chip_of(z, s) * (2 * most), 2 * most), 2 * most) for s in range(3)]
    for local, (got, rest, gates) in enumerate(((got0, rest0, gates0), (got1, rest1, gates1))):
        out[local, spans[0], :] = first[local]
        grad = gates[:, :1] * (rest[...] + decode(got, 0, 1))
        out[local, spans[1], :] = grad[: 2 * most]
        out[local, spans[2], :] = grad[2 * most :]


def finish(most, first, sums, totals):
    experts, rows, width = first.shape
    return pl.pallas_call(
        functools.partial(finish_kernel, most),
        in_specs=[VMEM] * (7 + len(totals)),
        out_specs=[VMEM, VMEM],
        out_shape=[like((experts, 3 * rows, width)), like(totals[0].shape)],
        compiler_params=pltpu.CompilerParams(vmem_limit_bytes=16 * MIB),
        cost_estimate=cost([*sums, first, first]),
        name="finish",
    )(first, *sums, *totals)


def chips_kernel(mine, got, stay, away):
    z = place()[0]
    low, mid, high = (mine[i] + got[i] for i in range(3))
    none = jnp.zeros(low.shape, jnp.float32)
    stay[0] = jnp.where(z < 2, low, high)
    stay[1] = jnp.where(z < 2, mid, none)
    away[0] = jnp.where(z < 2, high, low)
    away[1] = jnp.where(z < 2, none, mid)


def chip_kernel(kept, got, stay, away):
    odd = lax.rem(place()[0], 2) == 1
    even_part, odd_part = (kept[i] + got[i] for i in range(2))
    stay[...] = jnp.where(odd, odd_part, even_part)
    away[...] = jnp.where(odd, even_part, odd_part)


def add_kernel(*refs):
    total = refs[0][...]
    for ref in refs[1:-1]:
        total = total + ref[...]
    refs[-1][...] = total


def small(kernel, outs, *args, after=()):
    used = len(args)
    return pl.pallas_call(
        lambda *refs: kernel(*refs[:used], *refs[used + len(after) :]),
        in_specs=[VMEM] * used + [ANY] * len(after),
        out_specs=[VMEM] * len(outs),
        out_shape=outs,
        compiler_params=pltpu.CompilerParams(vmem_limit_bytes=2 * MIB),
        cost_estimate=cost(args),
        name=kernel.__name__,
    )(*args, *after)


def blockwise(most, grad_out, routes, slots, gates, capacity, hidden, down_weight):
    peers, ranks = lax.axis_size("expert"), lax.axis_size("dp")
    tokens, top = routes.shape

    def along(rows, pairs):
        return lax.ppermute(rows, "expert", [(2 * a + c, 2 * b + c) for a, b in pairs for c in range(2)])

    def across(rows):
        return lax.ppermute(rows, "expert", [(i, i ^ 1) for i in range(peers)])

    def over(rows, flip):
        return lax.ppermute(rows, "dp", [(i, i ^ flip) for i in range(ranks)])

    block, first_hidden, other_hidden = prepare(most, grad_out, routes, slots, gates, hidden)
    up1 = along(block, [(0, 1), (1, 2), (2, 3)])
    down1 = along(block, [(2, 1), (1, 0)])
    stored = [other_hidden, over(other_hidden, 1), over(other_hidden, 2)]
    *passed, again = take(stored[1], stored[2], block)
    far_stored = [over(passed[0], 2), over(passed[1], 1)]
    weight = load(block, down_weight)

    (first,) = pick(((0, 0, 0, 1),), (block, up1), (weight, down1))
    up2 = along(up1, [(1, 2), (2, 3)])
    down2 = along(again, [(2, 0)])
    pair = (first, across(first))
    sent, kept = [], []
    for local in range(2):
        send, keep, info = partial_share(
            local, most, top, (0,), capacity, weight, pair, after=far_stored[:1] if local else ()
        )
        sent.append(send)
        kept.append(keep)

    up3 = along(up2, [(2, 3)])
    (second,) = pick(((2, 0, 0, 1),), (up1, up2, down1), (*sent, *far_stored))
    blocks = [second, across(second)]

    sums, onward = [], []
    for local in range(2):
        send, rest = middle(over(sent[local], 1 + local), kept[local])
        onward.append(send)
        sums += [over(send, 2 - local), rest]
    (third,) = pick(((0, 1, 2, 3),), (down2, down1, up2, up3), ())
    blocks += [third, across(third)]

    halves = [None, None]
    before = []
    for local in (1, 0):
        send, keep, gate, *before = partial_share(
            local, most, top, (1, 2), capacity, weight, blocks, [*stored, far_stored[local]], before,
            () if local else (sums[0], sums[2]),
        )
        halves[local] = (over(send, 1 + local), keep, gate)
    first_grad, mine, theirs = first_finish(most, top, capacity, first_hidden, info, sums, before)

    one = like((top, tokens))
    two = like((2, top, tokens))
    (got0, keep0, gate0), (got1, keep1, gate1) = halves
    stay, away = small(chips_kernel, [two, two], mine, across(theirs))
    came = along(away, [(z, z ^ 2) for z in range(peers // 2)])
    stay, away = small(chip_kernel, [one, one], stay, came)
    send1, rest1 = middle(got1, keep1, (away,))
    (total,) = small(
        add_kernel, [one], stay, along(away, [(z, z ^ 1) for z in range(peers // 2)]), after=(send1,)
    )
    whole = [total] + [over(total, flip) for flip in range(1, ranks)]
    send0, rest0 = middle(got0, keep0, (total,))
    sums = [over(send0, 2), rest0, gate0, over(send1, 1), rest1, gate1]
    hidden_grad, gate_grad = finish(most, first_grad, sums, whole)
    return hidden_grad, gate_grad.T


def solution(mesh):
    peers, ranks = mesh.shape["expert"], mesh.shape["dp"]

    def shards(grad_out, routes, slots, gates, capacity, hidden, down_weight):
        tokens, top = routes.shape
        experts = down_weight.shape[0] * peers
        most = top * max(2, (tokens + experts - 1) // experts)
        full = most * experts == tokens * top
        fits = peers == 8 and hidden.shape[1] == 6 * most and 3 * tokens <= grad_out.shape[1]
        square = ranks == 4 and down_weight.shape[0] == 2 and experts <= 256 and most <= 256
        if full and fits and square:
            return blockwise(most, grad_out, routes, slots, gates, capacity, hidden, down_weight)
        return general(grad_out, routes, slots, gates, capacity, hidden, down_weight)

    placed = (
        P("expert", "dp"),
        P("expert", None),
        P("expert", None),
        P("expert", None),
        P("expert"),
        P("expert", None, "dp"),
        P("expert", None, "dp"),
    )
    return jax.shard_map(
        shards,
        mesh=mesh,
        in_specs=placed,
        out_specs=(P("expert", None, "dp"), P("expert", None)),
        check_vma=False,
    )
```
